256 devices in a mesh: ctx: 8 (over x, y_hi), fsdp: 32 (over z, y_lo, core).
Axes of the slice: x: 4, y: 4 (y_hi: 2, y_lo: 2; y = y_hi * 2 + y_lo), z: 8, core: 2. Of those that a mesh axis runs over, the one named last changes fastest.
Arguments:
- queries: bfloat16 [768, 4, 8192], P('fsdp'), may hold values from -14 to 14
- key_pages: bfloat16 [192, 64, 1024], P('ctx'), may hold values from -7 to 7
- value_pages: bfloat16 [192, 64, 1024], P('ctx'), may hold values from -6 to 6
- new_keys: bfloat16 [768, 4, 8, 128], P('fsdp', None, 'ctx'), may hold values from -7 to 7
- new_values: bfloat16 [768, 4, 8, 128], P('fsdp', None, 'ctx'), may hold values from -6 to 6
- page_table: int32 [768, 16], P('fsdp'), may hold values from 0 to 191, as said below
- lengths: int32 [768], P('fsdp'), may hold values from 1 to 1024
- parents: int32 [768, 4], P('fsdp'), may hold values from -1 to 2, as said below
- o_weight: bfloat16 [8192, 8192], P('ctx', 'fsdp'), may hold values from -0.0625 to 0.0625
Outputs:
- mixed: bfloat16 [768, 4, 8192], P('fsdp', None, 'ctx')
The draws below stay inside these ranges and needn't reach their ends.
Inputs may be any that keep to these rules, and one draw needn't show every extreme that they name: `page_table`: each row holds 16 distinct page ids; aligned groups of 8 consecutive trajectories share their first 8 entries, which lie below 96; the other entries are drawn for each trajectory from the common pool of pages at or above 96, so many trajectories reuse them. parents[t, i] lies below i; parents[t, 0] is -1.
All inputs are finite; a program needn't handle non-finite values.
Results may differ from the reference program's by a relative error of at most 0.0053.
Values may be sent and summed in bfloat16 or wider, within the bound.
A program may use at most 128 MiB of HBM per device.

```python
import jax
import jax.numpy as jnp
from jax import lax

D = 8192
HEADS = 64
KV = 8
HD = 128
NEW = 4
PAGE = 64
MAXP = 16
SHARE = 8
TRAJ = 768
PAGES = 192


def draw_queries(key, part):
    key = jax.random.fold_in(key, 2)
    values = jnp.clip(jax.random.normal(key, (TRAJ, NEW, HEADS, HD), jnp.float32), -4.5, 4.5)
    return values.reshape(TRAJ, NEW, HEADS * HD).astype(jnp.bfloat16)


def draw_key_pages(key, part):
    key = jax.random.fold_in(key, 3)
    values = jnp.clip(jax.random.normal(key, (PAGES, PAGE, KV * HD), jnp.float32), -4.5, 4.5)
    return values.astype(jnp.bfloat16)


def draw_new_keys(key, part):
    key = jax.random.fold_in(key, 4)
    values = jnp.clip(jax.random.normal(key, (TRAJ, NEW, KV, HD), jnp.float32), -4.5, 4.5)
    return values.astype(jnp.bfloat16)


def draw_page_table(key, part):
    key = jax.random.fold_in(key, 11)
    group_keys = jax.random.split(jax.random.fold_in(key, 1), TRAJ // SHARE)
    prefix = jax.vmap(lambda single: jax.random.permutation(single, PAGES // 2)[:MAXP // 2])(group_keys)
    prefix = jnp.repeat(prefix, SHARE, axis=0)
    own_keys = jax.random.split(jax.random.fold_in(key, 2), TRAJ)
    tails = jax.vmap(lambda single: jax.random.permutation(single, PAGES // 2)[:MAXP - MAXP // 2])(own_keys)
    tails = tails + PAGES // 2
    return jnp.concatenate([prefix, tails], axis=1).astype(jnp.int32)


def draw_lengths(key, part):
    key = jax.random.fold_in(key, 12)
    ceiling = jax.random.randint(jax.random.fold_in(key, 1), (TRAJ,), 2, MAXP * PAGE + 1)
    counts = jax.random.randint(jax.random.fold_in(key, 2), (TRAJ,), 1, ceiling)
    return counts.at[0].set(MAXP * PAGE).astype(jnp.int32)


def draw_parents(key, part):
    key = jax.random.fold_in(key, 13)
    ceiling = jnp.arange(NEW, dtype=jnp.int32)[None, :]
    chosen = jax.random.randint(key, (TRAJ, NEW), -1, ceiling)
    return chosen.at[0, NEW - 1].set(NEW - 2).astype(jnp.int32)


def block_scale(rng, shape, cuts, least, top_value):
    def one(axis_at, parts):
        steps = jax.random.uniform(jax.random.fold_in(jax.random.fold_in(rng, 6), axis_at), (parts,), jnp.float32, least / len(cuts), top_value / len(cuts))
        return jnp.repeat(jnp.exp(steps), shape[axis_at] // parts).reshape((-1,) + (1,) * (len(shape) - axis_at - 1))

    loudness = one(*cuts[0])
    for cut in cuts[1:]:
        loudness = loudness * one(*cut)
    return loudness


def noise(rng, dims, scale, bound, cuts=(), held_as=jnp.bfloat16):
    array = jax.random.normal(rng, dims, jnp.float32) * scale
    if len(cuts) > 0:
        array = block_scale(rng, dims, cuts, -0.22, 0.18) * array
    return jnp.clip(array, min=-bound, max=bound).astype(held_as)


def setup_inputs(seed: int = 0) -> dict:
    seeds = jax.random.split(jax.random.key(seed), 10)
    return {
        "queries": draw_queries(jax.random.fold_in(seeds[9], 71), 0),
        "key_pages": draw_key_pages(jax.random.fold_in(seeds[9], 71), 0),
        "value_pages": noise(seeds[2], (PAGES, PAGE, KV * HD), 1.0, 6.0, ((0, 8),)),
        "new_keys": draw_new_keys(jax.random.fold_in(seeds[9], 71), 0),
        "new_values": noise(seeds[4], (TRAJ, NEW, KV, HD), 1.0, 6.0, ((0, 32), (2, 8))),
        "page_table": draw_page_table(jax.random.fold_in(seeds[9], 71), 0),
        "lengths": draw_lengths(jax.random.fold_in(seeds[9], 71), 0),
        "parents": draw_parents(jax.random.fold_in(seeds[9], 71), 0),
        "o_weight": noise(seeds[8], (HEADS * HD, D), (HEADS * HD) ** -0.5, 0.0625, ((0, 8), (1, 32))),
    }


def ancestry(parents, count):
    index = jnp.arange(count, dtype=jnp.int32)
    reach = (parents[:, :, None] * 0 + index[None, None, :]) == index[None, :, None]
    current = parents
    for level in range(count):
        reach = reach | (current[:, :, None] == index[None, None, :])
        hitting = (current[:, :, None] == index[None, None, :]).astype(jnp.int32)
        upward = jnp.sum(hitting * parents[:, None, :], axis=-1)
        current = jnp.where(current >= 0, upward, -1).astype(jnp.int32)
    return reach


def attend_block(queries, new_keys, new_values, table, counts, parents, key_pages, value_pages):
    group = HEADS // KV
    scale = 1.0 / (HD ** 0.5)
    batch = queries.shape[0]
    query_f = queries.astype(jnp.float32).reshape(batch, NEW, KV, group, HD)
    keys_f = key_pages[table].astype(jnp.float32).reshape(batch, MAXP, PAGE, KV, HD)
    values_f = value_pages[table].astype(jnp.float32).reshape(batch, MAXP, PAGE, KV, HD)
    scores = jnp.einsum("bnkgd,bjokd->bnkgjo", query_f, keys_f) * scale
    position = jnp.arange(MAXP, dtype=jnp.int32)[:, None] * PAGE + jnp.arange(PAGE, dtype=jnp.int32)[None, :]
    live = position[None] < counts[:, None, None]
    live = live[:, None, None, None]
    block_max = jnp.max(jnp.where(live, scores, -1e30), axis=-1)
    expo = jnp.where(live, jnp.exp(scores - block_max[..., None]), 0.0)
    block_sum = jnp.sum(expo, axis=-1)
    weights = expo.astype(jnp.bfloat16)
    block_out = jnp.einsum("bnkgjo,bjokd->bnkgjd", weights.astype(jnp.float32), values_f)
    new_scores = jnp.einsum("bnkgd,bmkd->bnkgm", query_f, new_keys.astype(jnp.float32)) * scale
    seen = ancestry(parents, NEW)[:, :, None, None, :]
    new_max = jnp.max(jnp.where(seen, new_scores, -1e30), axis=-1)
    new_expo = jnp.where(seen, jnp.exp(new_scores - new_max[..., None]), 0.0)
    new_sum = jnp.sum(new_expo, axis=-1)
    new_weights = new_expo.astype(jnp.bfloat16)
    new_out = jnp.einsum("bnkgm,bmkd->bnkgd", new_weights.astype(jnp.float32), new_values.astype(jnp.float32))
    overall = jnp.maximum(jnp.max(block_max, axis=-1), new_max)
    factor = jnp.exp(block_max - overall[..., None])
    new_factor = jnp.exp(new_max - overall)
    numer = jnp.sum(block_out * factor[..., None], axis=-2) + new_out * new_factor[..., None]
    denom = jnp.sum(block_sum * factor, axis=-1) + new_sum * new_factor
    attended = numer / denom[..., None]
    return attended.reshape(batch, NEW, HEADS * HD).astype(jnp.bfloat16)


def reference(queries, key_pages, value_pages, new_keys, new_values, page_table, lengths, parents, o_weight):
    blocks = TRAJ // SHARE

    def one_block(pieces):
        return attend_block(pieces[0], pieces[1], pieces[2], pieces[3], pieces[4], pieces[5], key_pages, value_pages)

    grouped = (
        queries.reshape(blocks, SHARE, NEW, HEADS * HD),
        new_keys.reshape(blocks, SHARE, NEW, KV, HD),
        new_values.reshape(blocks, SHARE, NEW, KV, HD),
        page_table.reshape(blocks, SHARE, MAXP),
        lengths.reshape(blocks, SHARE),
        parents.reshape(blocks, SHARE, NEW),
    )
    attended = lax.map(one_block, grouped)
    flat = attended.reshape(TRAJ * NEW, HEADS * HD)
    mixed = jnp.dot(flat, o_weight, preferred_element_type=jnp.float32)
    return mixed.astype(jnp.bfloat16).reshape(TRAJ, NEW, D)
```

```python
import functools

import jax
import jax.numpy as jnp
from jax import lax
from jax.experimental import pallas as pl
from jax.experimental.pallas import tpu as pltpu
from jax.sharding import PartitionSpec as P

SHARE = 8
DEAD = -1e30
LOG2E = 1.4426950408889634


def attention_kernel(
    shared_entries,
    table_ref,
    lengths_ref,
    parents_ref,
    query_hbm,
    keys_hbm,
    values_hbm,
    new_keys_hbm,
    new_values_hbm,
    out_hbm,
    lse_ref,
    query_ref,
    group_ref,
    new_keys_ref,
    new_values_ref,
    acc_ref,
    max_ref,
    sum_ref,
    out_ref,
    keys_ref,
    values_ref,
    unit_ref,
    query_sem,
    new_sem,
    out_sem,
    key_sem,
    value_sem,
):
    table_len, traj = table_ref.shape
    new = parents_ref.shape[0]
    pages_local, page_len, width = keys_hbm.shape
    kv_count, head_size, lanes = acc_ref.shape
    rows = SHARE * new
    groups = traj // SHARE
    heads = lanes // rows
    slots = keys_ref.shape[0]
    ctx_index = lax.axis_index("ctx")
    first_page = ctx_index * pages_local
    scale = LOG2E / head_size**0.5

    query_copies = [
        pltpu.make_async_copy(
            query_hbm.at[pl.ds(group * SHARE, SHARE)],
            query_ref.at[pl.ds(group * SHARE, SHARE)],
            query_sem.at[group],
        )
        for group in range(groups)
    ]
    new_copies = [
        pltpu.make_async_copy(new_keys_hbm, new_keys_ref, new_sem.at[0]),
        pltpu.make_async_copy(new_values_hbm, new_values_ref, new_sem.at[1]),
    ]
    query_copies[0].start()
    for copy in new_copies + query_copies[1:]:
        copy.start()

    def entry_live(member, entry, count, owner, reach):
        page = table_ref[entry, owner] - first_page
        live = (page >= 0) & (page < pages_local) & (reach > entry * page_len)

        @pl.when(live)
        def _():
            unit_ref[0, count] = member
            unit_ref[1, count] = page
            unit_ref[2, count] = entry * page_len

        return count + live.astype(jnp.int32)

    def own_units(owner, count):
        reach = lengths_ref[owner]
        last = jnp.minimum((reach + page_len - 1) // page_len, table_len)
        return lax.fori_loop(
            shared_entries,
            last,
            lambda entry, count: entry_live(owner % SHARE, entry, count, owner, reach),
            count,
        )

    count = 0
    bounds = [0]
    for group in range(groups):
        reach = lengths_ref[group * SHARE]
        for member in range(1, SHARE):
            reach = jnp.maximum(reach, lengths_ref[group * SHARE + member])
        count = lax.fori_loop(
            0,
            jnp.minimum((reach + page_len - 1) // page_len, shared_entries),
            lambda entry, count: entry_live(-1, entry, count, group * SHARE, reach),
            count,
        )
        count = lax.fori_loop(group * SHARE, (group + 1) * SHARE, own_units, count)
        bounds.append(count)

    def fetch(unit):
        slot = unit % slots
        page = unit_ref[1, unit]
        return (
            pltpu.make_async_copy(keys_hbm.at[page], keys_ref.at[slot], key_sem.at[slot]),
            pltpu.make_async_copy(values_hbm.at[page], values_ref.at[slot], value_sem.at[slot]),
        )

    def start_fetch(unit):
        @pl.when(unit < count)
        def _():
            for copy in fetch(unit):
                copy.start()

    for ahead in range(slots - 1):
        start_fetch(ahead)

    lane = lax.broadcasted_iota(jnp.int32, (1, lanes), 1)
    lane_token = lane % rows
    lane_traj = lane_token // new
    sub = lax.broadcasted_iota(jnp.int32, (rows, lanes), 0)
    own_row = lax.broadcasted_iota(jnp.int32, (kv_count, lanes), 0) == ctx_index
    position = lax.broadcasted_iota(jnp.int32, (page_len, lanes), 0)

    def gather_queries(group, kv):
        parts = []
        for head in range(heads):
            column = (kv * heads + head) * head_size
            if not isinstance(column, int):
                column = pl.multiple_of(column, head_size)
            value = query_ref[group * SHARE : (group + 1) * SHARE, :, pl.ds(column, head_size)]
            parts.append(value.reshape(rows, head_size))
        return jnp.concatenate(parts, axis=0)

    def block(keys, values, query, live):
        scores = (
            lax.dot_general(
                keys, query, (((1,), (1,)), ((), ())), preferred_element_type=jnp.float32
            )
            * scale
        )
        scores = jnp.where(live, scores, DEAD)
        block_max = jnp.max(scores, axis=0, keepdims=True)
        expo = jnp.exp2(scores - jnp.maximum(block_max, 0.1 * DEAD))
        block_sum = jnp.sum(expo, axis=0, keepdims=True)
        block_out = lax.dot_general(
            values,
            expo.astype(jnp.bfloat16),
            (((0,), (0,)), ((), ())),
            preferred_element_type=jnp.float32,
        )
        return block_max, block_sum, block_out

    def new_block(group):
        bits = jnp.zeros((1, lanes), jnp.int32)
        for member in range(SHARE):
            seen = []
            for token in range(new):
                parent = parents_ref[token, group * SHARE + member]
                mask = jnp.int32(1 << token)
                for earlier in range(token):
                    mask = mask | jnp.where(parent == earlier, seen[earlier], 0)
                seen.append(mask)
                bits = jnp.where(lane_token == member * new + token, mask, bits)
        live = (sub // new == lane_traj) & (((bits >> (sub % new)) & 1) == 1)
        span = slice(group * SHARE, (group + 1) * SHARE)
        return block(
            new_keys_ref[span].reshape(rows, head_size),
            new_values_ref[span].reshape(rows, head_size),
            gather_queries(group, ctx_index),
            live,
        )

    def unit_step(group, unit):
        start_fetch(unit + slots - 1)
        slot = unit % slots
        member = unit_ref[0, unit]
        offset = unit_ref[2, unit]
        limit = jnp.zeros((1, lanes), jnp.int32)
        for each in range(SHARE):
            reach = jnp.where(
                (member < 0) | (member == each), lengths_ref[group * SHARE + each] - offset, 0
            )
            limit = jnp.where(lane_traj == each, reach, limit)
        live = position < limit
        for copy in fetch(unit):
            copy.wait()
        run_max = max_ref[...]
        run_sum = sum_ref[...]
        next_max = []
        next_sum = []
        for kv in range(kv_count):
            columns = slice(kv * head_size, (kv + 1) * head_size)
            block_max, block_sum, block_out = block(
                keys_ref[slot, :, columns],
                values_ref[slot, :, columns],
                group_ref[kv],
                live,
            )
            old_max = run_max[kv : kv + 1]
            new_max = jnp.maximum(old_max, block_max)
            keep = jnp.exp2(old_max - new_max)
            factor = jnp.exp2(block_max - new_max)
            next_max.append(new_max)
            next_sum.append(run_sum[kv : kv + 1] * keep + block_sum * factor)
            acc_ref[kv] = acc_ref[kv] * keep + block_out * factor
        max_ref[...] = jnp.concatenate(next_max, axis=0)
        sum_ref[...] = jnp.concatenate(next_sum, axis=0)

    def finish(group):
        total = sum_ref[...]
        some = total > 0.0
        safe = jnp.where(some, total, 1.0)
        inverse = jnp.where(some, 1.0 / safe, 0.0)
        lse = jnp.where(some, max_ref[...] + jnp.log2(safe), DEAD)
        for kv in range(kv_count):
            lse_ref[kv, group : group + 1] = lse[kv : kv + 1]
        return inverse

    out_copies = []
    for group in range(groups):
        query_copies[group].wait()
        if group == 0:
            for copy in new_copies:
                copy.wait()
        block_max, block_sum, block_out = new_block(group)
        max_ref[...] = jnp.where(own_row, block_max, DEAD)
        sum_ref[...] = jnp.where(own_row, block_sum, 0.0)
        busy = bounds[group + 1] > bounds[group]

        @pl.when(busy)
        def _():
            for kv in range(kv_count):
                group_ref[kv] = gather_queries(group, kv)
                acc_ref[kv] = jnp.zeros((head_size, lanes), jnp.float32)
            acc_ref[ctx_index] = block_out

            def step(unit, _):
                unit_step(group, unit)
                return 0

            lax.fori_loop(bounds[group], bounds[group + 1], step, 0)
            inverse = finish(group)
            for kv in range(kv_count):
                out_ref[group, kv] = (acc_ref[kv] * inverse[kv : kv + 1]).astype(jnp.bfloat16)

        @pl.when(jnp.logical_not(busy))
        def _():
            inverse = finish(group)
            own = jnp.sum(jnp.where(own_row, inverse, 0.0), axis=0, keepdims=True)
            for kv in range(kv_count):
                out_ref[group, kv] = jnp.zeros((head_size, lanes), jnp.bfloat16)
            out_ref[group, ctx_index] = (block_out * own).astype(jnp.bfloat16)

        copy = pltpu.make_async_copy(out_ref.at[group], out_hbm.at[:, group], out_sem.at[group])
        copy.start()
        out_copies.append(copy)
    for copy in out_copies:
        copy.wait()


def page_attention(table, lengths, parents, query, keys, values, new_keys, new_values):
    table_len, traj = table.shape
    new = parents.shape[0]
    head_size = new_keys.shape[-1]
    rows = SHARE * new
    groups = traj // SHARE
    pages, page_len, width = keys.shape
    kv_count = width // head_size
    heads = query.shape[2] // width
    lanes = rows * heads
    slots = 4
    units = traj * table_len
    smem = pl.BlockSpec(memory_space=pltpu.SMEM)
    vmem = pl.BlockSpec(memory_space=pltpu.VMEM)
    anywhere = pl.BlockSpec(memory_space=pl.ANY)
    bf16, f32, dma = jnp.bfloat16, jnp.float32, pltpu.SemaphoreType.DMA
    return pl.pallas_call(
        functools.partial(attention_kernel, table_len // 2),
        out_shape=(
            jax.ShapeDtypeStruct((kv_count, groups, head_size, lanes), bf16),
            jax.ShapeDtypeStruct((kv_count, 8, lanes), f32),
        ),
        in_specs=[smem, smem, smem] + [anywhere] * 5,
        out_specs=(anywhere, vmem),
        scratch_shapes=[
            pltpu.VMEM(query.shape, bf16),
            pltpu.VMEM((kv_count, lanes, head_size), bf16),
            pltpu.VMEM(new_keys.shape, bf16),
            pltpu.VMEM(new_values.shape, bf16),
            pltpu.VMEM((kv_count, head_size, lanes), f32),
            pltpu.VMEM((kv_count, lanes), f32),
            pltpu.VMEM((kv_count, lanes), f32),
            pltpu.VMEM((groups, kv_count, head_size, lanes), bf16),
            pltpu.VMEM((slots, page_len, width), bf16),
            pltpu.VMEM((slots, page_len, width), bf16),
            pltpu.SMEM((3, units), jnp.int32),
            dma((groups,)),
            dma((2,)),
            dma((groups,)),
            dma((slots,)),
            dma((slots,)),
        ],
        cost_estimate=pl.CostEstimate(
            flops=10**10, bytes_accessed=10**7, transcendentals=10**7
        ),
        compiler_params=pltpu.CompilerParams(vmem_limit_bytes=56 * 1024 * 1024),
    )(table, lengths, parents, query, keys, values, new_keys, new_values)


def attend(queries, keys, values, new_keys, new_values, table, lengths, parents):
    traj, new, _, head_size = new_keys.shape
    return page_attention(
        table.T,
        lengths,
        parents.T,
        queries,
        keys,
        values,
        new_keys.reshape(traj, new, head_size),
        new_values.reshape(traj, new, head_size),
    )


CTX_STEPS = ((2, 1), (2, 0), (1, 1), (3, 1), (0, 1), (1, 0), (3, 0))
MESH = pl.DeviceIdType.MESH


def project_kernel(
    near,
    part_hbm,
    lse_ref,
    weight_hbm,
    other_weight,
    out_ref,
    weights,
    part_own,
    part_in,
    lse_in,
    total,
    own_rows,
    pair_rows,
    far_rows,
    product,
    shard_in,
    summed,
    returned,
    final,
    own_sem,
    weight_sem,
    weight_sems,
    part_sems,
    lse_sems,
    ring_sems,
    shard_sems,
    return_sems,
    final_send,
    final_recv,
):
    count = lax.axis_size("ctx")
    c = lax.axis_index("ctx")
    f = lax.axis_index("fsdp")
    z, r = f // near, f % near
    groups, head_size, lanes = part_own.shape
    rows = own_rows.shape[0]
    half = rows // 2
    token_rows = rows // groups
    heads = lanes // token_rows
    shard = product.shape[2]
    steps = len(CTX_STEPS)

    def ctx_step(index, sign):
        dx, dy = CTX_STEPS[index]
        return ((c // 2 + count + sign * dx) % (count // 2)) * 2 + (c % 2 + dy) % 2

    def at_ctx(other):
        return (other, f)

    def at_z(step):
        return (c, ((z + count + step) % count) * near + r)

    barrier = pltpu.get_barrier_semaphore()
    for index in range(steps):
        pl.semaphore_signal(barrier, inc=1, device_id=at_ctx(ctx_step(index, 1)), device_id_type=MESH)
    for step in range(1, count):
        pl.semaphore_signal(barrier, inc=1, device_id=at_z(step), device_id_type=MESH)
    other_core = (c, z * near + r // 2 * 2 + (r + 1) % 2)
    pl.semaphore_signal(barrier, inc=1, device_id=other_core, device_id_type=MESH)
    pl.semaphore_wait(barrier, steps + count)

    sent = []

    def send(source, target, sems, index, device):
        copy = pltpu.make_async_remote_copy(
            src_ref=source,
            dst_ref=target,
            send_sem=sems.at[(0,) + index],
            recv_sem=sems.at[(1,) + index],
            device_id=device,
            device_id_type=MESH,
        )
        copy.start()
        sent.append(copy)
        return copy

    lse_copies = []
    part_copies = []
    for index in range(steps):
        other = ctx_step(index, 1)
        lse_copies.append(
            send(lse_ref.at[other], lse_in.at[index], lse_sems, (index,), at_ctx(other))
        )
    for index in range(steps):
        other = ctx_step(index, 1)
        part_copies.append(
            send(part_hbm.at[other], part_in.at[index], part_sems, (index,), at_ctx(other))
        )
    own_copy = pltpu.make_async_copy(part_hbm.at[c], part_own, own_sem)
    own_copy.start()
    weight_copy = pltpu.make_async_copy(weight_hbm, weights.at[0], weight_sem)
    weight_copy.start()
    other_copies = [
        send(weight_hbm, weights.at[1], weight_sems, (0,), other_core),
        send(other_weight, weights.at[2], weight_sems, (1,), other_core),
    ]
    for copy in lse_copies:
        copy.wait_recv()
    each_lse = [lse_ref[c]] + [lse_in[index] for index in range(steps)]
    top = functools.reduce(jnp.maximum, each_lse)
    weighing = [jnp.exp2(lse - top) for lse in each_lse]
    inverse = 1.0 / functools.reduce(jnp.add, weighing)
    weighing = [weight * inverse for weight in weighing]
    own_copy.wait()
    for group in range(groups):
        total[group] = part_own[group].astype(jnp.float32) * weighing[0][group : group + 1]
    for index in range(steps):
        part_copies[index].wait_recv()
        for group in range(groups):
            total[group] += (
                part_in[index, group].astype(jnp.float32) * weighing[index + 1][group : group + 1]
            )
    for group in range(groups):
        turned = total[group].T.astype(jnp.bfloat16)
        for head in range(heads):
            own_rows[
                group * token_rows : (group + 1) * token_rows,
                head * head_size : (head + 1) * head_size,
            ] = turned[head * token_rows : (head + 1) * token_rows]

    ring = {}

    def forward(way, distance, part):
        base = 0 if way == 0 else rows
        span = pl.ds(part * half, half)
        far_span = pl.ds(base + part * half, half)
        source = own_rows.at[span] if distance == 1 else pair_rows.at[distance - 2, far_span]
        target = far_rows.at[span] if distance == 4 else pair_rows.at[distance - 1, far_span]
        ring[way, distance, part] = send(
            source, target, ring_sems, (way, distance - 1, part), at_z(1 if way == 0 else -1)
        )

    for part in range(2):
        for way in range(2):
            forward(way, 1, part)

    weight_copy.wait()
    for copy in other_copies:
        copy.wait_recv()
    shard_copies = {}

    def project(stage, value, base):
        size = value.shape[0]
        for index, weight in enumerate(
            (weights.at[0], weights.at[1], other_weight, weights.at[2])
        ):
            block = (r // 2 + index // 2) % 2 * 2 + (r % 2 + index % 2) % 2
            result = jnp.dot(value, weight[...], preferred_element_type=jnp.float32)
            result = result.astype(jnp.bfloat16)
            product[block * 2, base : base + size] = result[:, :shard]
            product[block * 2 + 1, base : base + size] = result[:, shard:]
        span = pl.ds(base, size)
        for index in range(steps):
            other = ctx_step(index, 1)
            shard_copies[stage, index] = send(
                product.at[other, span],
                shard_in.at[index, span],
                shard_sems,
                (stage, index),
                at_ctx(other),
            )

    return_copies = {}
    final_copies = []

    def reduce_stage(stage, base, size):
        for index in range(steps):
            shard_copies[stage, index].wait_recv()
        value = product[c, base : base + size].astype(jnp.float32)
        for index in range(steps):
            value = value + shard_in[index, base : base + size].astype(jnp.float32)
        summed[base : base + size] = value.astype(jnp.bfloat16)

    def send_back(slot, step, base):
        return_copies[slot] = send(
            summed.at[pl.ds(base, rows)], returned.at[slot], return_sems, (slot,), at_z(step)
        )

    def place(slot, source, column):
        copy = pltpu.make_async_remote_copy(
            src_ref=source,
            dst_ref=final.at[c],
            send_sem=final_send.at[slot],
            recv_sem=final_recv.at[c],
            device_id=at_ctx(column),
            device_id_type=MESH,
        )
        final_copies.append((copy, column))

        @pl.when(column != c)
        def _():
            copy.start()

        @pl.when(column == c)
        def _():
            final[c] = source[...]

    def arrive(slot, column):
        return_copies[slot].wait_recv()
        place(slot, returned.at[slot], column)

    def finish(stage):
        if stage == 0:
            reduce_stage(0, 0, rows)
            place(0, summed.at[pl.ds(0, rows)], z)
        elif stage < 4:
            base = rows * (2 * stage - 1)
            reduce_stage(stage, base, 2 * rows)
            send_back(2 * stage - 1, -stage, base)
            send_back(2 * stage, stage, base + rows)
        else:
            reduce_stage(4, 7 * rows, rows)
            send_back(7, 4, 7 * rows)

    def settle(stage):
        if 0 < stage < 4:
            arrive(2 * stage - 1, (z + stage) % count)
            arrive(2 * stage, (z + count - stage) % count)
        elif stage == 4:
            arrive(7, (z + 4) % count)

    project(0, own_rows[...], 0)
    for distance in range(1, 4):
        for part in range(2):
            for way in range(2):
                ring[way, distance, part].wait_recv()
                if distance < 3 or part == way:
                    forward(way, distance + 1, part)
        project(distance, pair_rows[distance - 1], rows * (2 * distance - 1))
        finish(distance - 1)
        settle(distance - 2)
    for way in range(2):
        ring[way, 4, way].wait_recv()
    project(4, far_rows[...], 7 * rows)
    finish(3)
    settle(2)
    finish(4)
    settle(3)
    settle(4)

    for copy, column in final_copies:

        @pl.when(column != c)
        def _():
            copy.wait_send()

    for source in range(count):

        @pl.when(c != source)
        def _():
            pltpu.make_async_remote_copy(
                src_ref=final.at[source],
                dst_ref=final.at[source],
                send_sem=final_send.at[0],
                recv_sem=final_recv.at[source],
                device_id=at_ctx((c + 1) % count),
                device_id_type=MESH,
            ).wait_recv()

        out_ref[:, source * shard : (source + 1) * shard] = final[source]
    for copy in sent:
        copy.wait_send()


def project(part, lse, weight, other_weight, near):
    count, groups, head_size, lanes = part.shape
    width = weight.shape[0]
    rows = groups * lanes * head_size // width
    columns = near * weight.shape[1]
    shard = columns // count
    steps = len(CTX_STEPS)
    vmem = pl.BlockSpec(memory_space=pltpu.VMEM)
    anywhere = pl.BlockSpec(memory_space=pl.ANY)
    bf16, f32, dma = jnp.bfloat16, jnp.float32, pltpu.SemaphoreType.DMA
    return pl.pallas_call(
        functools.partial(project_kernel, near),
        out_shape=jax.ShapeDtypeStruct((rows, columns), bf16),
        in_specs=[anywhere, vmem, anywhere, vmem],
        out_specs=vmem,
        scratch_shapes=[
            pltpu.VMEM((near - 1,) + weight.shape, bf16),
            pltpu.VMEM((groups, head_size, lanes), bf16),
            pltpu.VMEM((steps, groups, head_size, lanes), bf16),
            pltpu.VMEM((steps, lse.shape[1], lanes), f32),
            pltpu.VMEM((groups, head_size, lanes), f32),
            pltpu.VMEM((rows, width), bf16),
            pltpu.VMEM((3, 2 * rows, width), bf16),
            pltpu.VMEM((rows, width), bf16),
            pltpu.VMEM((count, 8 * rows, shard), bf16),
            pltpu.VMEM((steps, 8 * rows, shard), bf16),
            pltpu.VMEM((8 * rows, shard), bf16),
            pltpu.VMEM((8, rows, shard), bf16),
            pltpu.VMEM((count, rows, shard), bf16),
            dma,
            dma,
            dma((2, 2)),
            dma((2, steps)),
            dma((2, steps)),
            dma((2, 2, 4, 2)),
            dma((2, 5, steps)),
            dma((2, 8)),
            dma((8,)),
            dma((count,)),
        ],
        compiler_params=pltpu.CompilerParams(
            collective_id=0, has_side_effects=True, vmem_limit_bytes=52 * 1024 * 1024
        ),
    )(part, lse, weight, other_weight)


def shards(
    queries, key_pages, value_pages, new_keys, new_values, page_table, lengths, parents, o_weight
):
    ctx_count = lax.axis_size("ctx")
    fsdp_count = lax.axis_size("fsdp")
    traj, new, _ = queries.shape
    near = fsdp_count // ctx_count
    other_weight = lax.ppermute(o_weight, "fsdp", [(at, at ^ 2) for at in range(fsdp_count)])
    part, lse = attend(
        queries, key_pages, value_pages, new_keys, new_values, page_table, lengths, parents
    )
    mixed = project(part, lse, o_weight, other_weight, near)
    return mixed.reshape(traj, new, -1)


def solution(mesh):
    placed = (
        P("fsdp", None, None),
        P("ctx", None, None),
        P("ctx", None, None),
        P("fsdp", None, "ctx", None),
        P("fsdp", None, "ctx", None),
        P("fsdp", None),
        P("fsdp"),
        P("fsdp", None),
        P("ctx", "fsdp"),
    )
    return jax.shard_map(
        shards, mesh=mesh, in_specs=placed, out_specs=P("fsdp", None, "ctx"), check_vma=False
    )
```

```python
import functools

import jax
import jax.numpy as jnp
from jax import lax
from jax.experimental import pallas as pl
from jax.experimental.pallas import tpu as pltpu
from jax.sharding import PartitionSpec as P

SHARE = 8
DEAD = -1e30
LOG2E = 1.4426950408889634


def attention_kernel(
    shared_entries,
    table_ref,
    lengths_ref,
    parents_ref,
    query_hbm,
    keys_hbm,
    values_hbm,
    new_keys_hbm,
    new_values_hbm,
    out_hbm,
    lse_ref,
    query_ref,
    group_ref,
    new_keys_ref,
    new_values_ref,
    acc_ref,
    max_ref,
    sum_ref,
    out_ref,
    keys_ref,
    values_ref,
    unit_ref,
    query_sem,
    new_sem,
    out_sem,
    key_sem,
    value_sem,
):
    table_len, traj = table_ref.shape
    new = parents_ref.shape[0]
    pages_local, page_len, width = keys_hbm.shape
    kv_count, head_size, lanes = acc_ref.shape
    rows = SHARE * new
    groups = traj // SHARE
    heads = lanes // rows
    slots = keys_ref.shape[0]
    ctx_index = lax.axis_index("ctx")
    first_page = ctx_index * pages_local
    scale = LOG2E / head_size**0.5

    query_copies = [
        pltpu.make_async_copy(
            query_hbm.at[pl.ds(group * SHARE, SHARE)],
            query_ref.at[pl.ds(group * SHARE, SHARE)],
            query_sem.at[group],
        )
        for group in range(groups)
    ]
    new_copies = [
        pltpu.make_async_copy(new_keys_hbm, new_keys_ref, new_sem.at[0]),
        pltpu.make_async_copy(new_values_hbm, new_values_ref, new_sem.at[1]),
    ]
    query_copies[0].start()
    for copy in new_copies + query_copies[1:]:
        copy.start()

    def entry_live(member, entry, count, owner, reach):
        page = table_ref[entry, owner] - first_page
        live = (page >= 0) & (page < pages_local) & (reach > entry * page_len)

        @pl.when(live)
        def _():
            unit_ref[0, count] = member
            unit_ref[1, count] = page
            unit_ref[2, count] = entry * page_len

        return count + live.astype(jnp.int32)

    def own_units(owner, count):
        reach = lengths_ref[owner]
        last = jnp.minimum((reach + page_len - 1) // page_len, table_len)
        return lax.fori_loop(
            shared_entries,
            last,
            lambda entry, count: entry_live(owner % SHARE, entry, count, owner, reach),
            count,
        )

    count = 0
    bounds = [0]
    for group in range(groups):
        reach = lengths_ref[group * SHARE]
        for member in range(1, SHARE):
            reach = jnp.maximum(reach, lengths_ref[group * SHARE + member])
        count = lax.fori_loop(
            0,
            jnp.minimum((reach + page_len - 1) // page_len, shared_entries),
            lambda entry, count: entry_live(-1, entry, count, group * SHARE, reach),
            count,
        )
        count = lax.fori_loop(group * SHARE, (group + 1) * SHARE, own_units, count)
        bounds.append(count)

    def fetch(unit):
        slot = unit % slots
        page = unit_ref[1, unit]
        return (
            pltpu.make_async_copy(keys_hbm.at[page], keys_ref.at[slot], key_sem.at[slot]),
            pltpu.make_async_copy(values_hbm.at[page], values_ref.at[slot], value_sem.at[slot]),
        )

    def start_fetch(unit):
        @pl.when(unit < count)
        def _():
            for copy in fetch(unit):
                copy.start()

    for ahead in range(slots - 1):
        start_fetch(ahead)

    lane = lax.broadcasted_iota(jnp.int32, (1, lanes), 1)
    lane_token = lane // (lanes // 2) * (rows // 2) + lane % (rows // 2)
    lane_traj = lane_token // new
    sub = lax.broadcasted_iota(jnp.int32, (rows, lanes), 0)
    own_row = lax.broadcasted_iota(jnp.int32, (kv_count, lanes), 0) == ctx_index
    position = lax.broadcasted_iota(jnp.int32, (page_len, lanes), 0)

    def gather_queries(group, kv):
        parts = []
        for head in range(heads):
            column = (kv * heads + head) * head_size
            if not isinstance(column, int):
                column = pl.multiple_of(column, head_size)
            value = query_ref[group * SHARE : (group + 1) * SHARE, :, pl.ds(column, head_size)]
            parts.append(value.reshape(rows, head_size))
        return jnp.concatenate(
            [part[: rows // 2] for part in parts] + [part[rows // 2 :] for part in parts], axis=0
        )

    def block(keys, values, query, live):
        scores = (
            lax.dot_general(
                keys, query, (((1,), (1,)), ((), ())), preferred_element_type=jnp.float32
            )
            * scale
        )
        scores = jnp.where(live, scores, DEAD)
        block_max = jnp.max(scores, axis=0, keepdims=True)
        expo = jnp.exp2(scores - jnp.maximum(block_max, 0.1 * DEAD))
        block_sum = jnp.sum(expo, axis=0, keepdims=True)
        block_out = lax.dot_general(
            values,
            expo.astype(jnp.bfloat16),
            (((0,), (0,)), ((), ())),
            preferred_element_type=jnp.float32,
        )
        return block_max, block_sum, block_out

    def new_block(group):
        bits = jnp.zeros((1, lanes), jnp.int32)
        for member in range(SHARE):
            seen = []
            for token in range(new):
                parent = parents_ref[token, group * SHARE + member]
                mask = jnp.int32(1 << token)
                for earlier in range(token):
                    mask = mask | jnp.where(parent == earlier, seen[earlier], 0)
                seen.append(mask)
                bits = jnp.where(lane_token == member * new + token, mask, bits)
        live = (sub // new == lane_traj) & (((bits >> (sub % new)) & 1) == 1)
        span = slice(group * SHARE, (group + 1) * SHARE)
        return block(
            new_keys_ref[span].reshape(rows, head_size),
            new_values_ref[span].reshape(rows, head_size),
            gather_queries(group, ctx_index),
            live,
        )

    def unit_step(group, unit):
        start_fetch(unit + slots - 1)
        slot = unit % slots
        member = unit_ref[0, unit]
        offset = unit_ref[2, unit]
        limit = jnp.zeros((1, lanes), jnp.int32)
        for each in range(SHARE):
            reach = jnp.where(
                (member < 0) | (member == each), lengths_ref[group * SHARE + each] - offset, 0
            )
            limit = jnp.where(lane_traj == each, reach, limit)
        live = position < limit
        for copy in fetch(unit):
            copy.wait()
        run_max = max_ref[...]
        run_sum = sum_ref[...]
        next_max = []
        next_sum = []
        for kv in range(kv_count):
            columns = slice(kv * head_size, (kv + 1) * head_size)
            block_max, block_sum, block_out = block(
                keys_ref[slot, :, columns],
                values_ref[slot, :, columns],
                group_ref[kv],
                live,
            )
            old_max = run_max[kv : kv + 1]
            new_max = jnp.maximum(old_max, block_max)
            keep = jnp.exp2(old_max - new_max)
            factor = jnp.exp2(block_max - new_max)
            next_max.append(new_max)
            next_sum.append(run_sum[kv : kv + 1] * keep + block_sum * factor)
            acc_ref[kv] = acc_ref[kv] * keep + block_out * factor
        max_ref[...] = jnp.concatenate(next_max, axis=0)
        sum_ref[...] = jnp.concatenate(next_sum, axis=0)

    def finish(group):
        total = sum_ref[...]
        some = total > 0.0
        safe = jnp.where(some, total, 1.0)
        inverse = jnp.where(some, 1.0 / safe, 0.0)
        lse = jnp.where(some, max_ref[...] + jnp.log2(safe), DEAD)
        for kv in range(kv_count):
            for half in range(2):
                row = half * groups + group
                lse_ref[kv, row : row + 1] = lse[
                    kv : kv + 1, half * (lanes // 2) : (half + 1) * (lanes // 2)
                ]
        return inverse

    def store(group, kv, value):
        for half in range(2):
            out_ref[group, kv, half] = value[
                :, half * (lanes // 2) : (half + 1) * (lanes // 2)
            ]

    out_copies = []
    for group in range(groups):
        query_copies[group].wait()
        if group == 0:
            for copy in new_copies:
                copy.wait()
        block_max, block_sum, block_out = new_block(group)
        max_ref[...] = jnp.where(own_row, block_max, DEAD)
        sum_ref[...] = jnp.where(own_row, block_sum, 0.0)
        busy = bounds[group + 1] > bounds[group]

        @pl.when(busy)
        def _():
            for kv in range(kv_count):
                group_ref[kv] = gather_queries(group, kv)
                acc_ref[kv] = jnp.zeros((head_size, lanes), jnp.float32)
            acc_ref[ctx_index] = block_out

            def step(unit, _):
                unit_step(group, unit)
                return 0

            lax.fori_loop(bounds[group], bounds[group + 1], step, 0)
            inverse = finish(group)
            for kv in range(kv_count):
                store(group, kv, (acc_ref[kv] * inverse[kv : kv + 1]).astype(jnp.bfloat16))

        @pl.when(jnp.logical_not(busy))
        def _():
            inverse = finish(group)
            own = jnp.sum(jnp.where(own_row, inverse, 0.0), axis=0, keepdims=True)
            for kv in range(kv_count):
                store(group, kv, jnp.zeros((head_size, lanes), jnp.bfloat16))
            store(group, ctx_index, (block_out * own).astype(jnp.bfloat16))

        copy = pltpu.make_async_copy(out_ref.at[group], out_hbm.at[:, :, group], out_sem.at[group])
        copy.start()
        out_copies.append(copy)
    for copy in out_copies:
        copy.wait()


def page_attention(table, lengths, parents, query, keys, values, new_keys, new_values):
    table_len, traj = table.shape
    new = parents.shape[0]
    head_size = new_keys.shape[-1]
    rows = SHARE * new
    groups = traj // SHARE
    pages, page_len, width = keys.shape
    kv_count = width // head_size
    heads = query.shape[2] // width
    lanes = rows * heads
    slots = 4
    units = traj * table_len
    smem = pl.BlockSpec(memory_space=pltpu.SMEM)
    vmem = pl.BlockSpec(memory_space=pltpu.VMEM)
    anywhere = pl.BlockSpec(memory_space=pl.ANY)
    bf16, f32, dma = jnp.bfloat16, jnp.float32, pltpu.SemaphoreType.DMA
    return pl.pallas_call(
        functools.partial(attention_kernel, table_len // 2),
        out_shape=(
            jax.ShapeDtypeStruct((kv_count, 2, groups, head_size, lanes // 2), bf16),
            jax.ShapeDtypeStruct((kv_count, 8, lanes // 2), f32),
        ),
        in_specs=[smem, smem, smem] + [anywhere] * 5,
        out_specs=(anywhere, vmem),
        scratch_shapes=[
            pltpu.VMEM(query.shape, bf16),
            pltpu.VMEM((kv_count, lanes, head_size), bf16),
            pltpu.VMEM(new_keys.shape, bf16),
            pltpu.VMEM(new_values.shape, bf16),
            pltpu.VMEM((kv_count, head_size, lanes), f32),
            pltpu.VMEM((kv_count, lanes), f32),
            pltpu.VMEM((kv_count, lanes), f32),
            pltpu.VMEM((groups, kv_count, 2, head_size, lanes // 2), bf16),
            pltpu.VMEM((slots, page_len, width), bf16),
            pltpu.VMEM((slots, page_len, width), bf16),
            pltpu.SMEM((3, units), jnp.int32),
            dma((groups,)),
            dma((2,)),
            dma((groups,)),
            dma((slots,)),
            dma((slots,)),
        ],
        cost_estimate=pl.CostEstimate(
            flops=10**10, bytes_accessed=10**7, transcendentals=10**7
        ),
        compiler_params=pltpu.CompilerParams(vmem_limit_bytes=56 * 1024 * 1024),
    )(table, lengths, parents, query, keys, values, new_keys, new_values)


def attend(queries, keys, values, new_keys, new_values, table, lengths, parents):
    traj, new, _, head_size = new_keys.shape
    return page_attention(
        table.T,
        lengths,
        parents.T,
        queries,
        keys,
        values,
        new_keys.reshape(traj, new, head_size),
        new_values.reshape(traj, new, head_size),
    )


CTX_STEPS = ((2, 1), (2, 0), (1, 1), (3, 1), (0, 1), (1, 0), (3, 0))
MESH = pl.DeviceIdType.MESH


def project_kernel(
    near,
    part_hbm,
    lse_hbm,
    weight_hbm,
    weight_below,
    weight_above,
    out_ref,
    weights,
    part_own,
    part_in,
    lse_own,
    lse_in,
    total,
    gathered,
    product,
    shard_in,
    summed,
    final,
    own_sems,
    part_sems,
    lse_sems,
    ring_sems,
    gather_sems,
    shard_sems,
    final_sems,
):
    count = lax.axis_size("ctx")
    c = lax.axis_index("ctx")
    f = lax.axis_index("fsdp")
    z, r = f // near, f % near
    halves, groups, head_size, lanes = part_own.shape
    rows = gathered.shape[2]
    token_rows = rows // groups
    heads = lanes // token_rows
    shard = product.shape[2]
    piece_rows = weights.shape[1] // 2
    steps = len(CTX_STEPS)

    def ctx_step(dx, dy):
        return ((c // 2 + dx) % (count // 2)) * 2 + (c % 2 + dy) % 2

    others = [ctx_step(*step) for step in CTX_STEPS]
    locals_ = [
        (r // 2 + dy) % 2 * 2 + (r % 2 + dcore) % 2 for dy, dcore in ((0, 1), (1, 0), (1, 1))
    ]

    def at_ctx(other):
        return (other, f)

    def at_local(other):
        return (c, z * near + other)

    def at_z(step):
        return (c, ((z + count + step) % count) * near + r)

    barrier = pltpu.get_barrier_semaphore()
    peers = [at_ctx(other) for other in others]
    peers += [at_z(1), at_z(-1)] + [at_local(other) for other in locals_]
    for peer in peers:
        pl.semaphore_signal(barrier, inc=1, device_id=peer, device_id_type=MESH)
    below, above = (z + count - 1) % count, (z + 1) % count
    own_copies = [
        pltpu.make_async_copy(source, target, own_sems.at[index])
        for index, (source, target) in enumerate(
            (
                (lse_hbm.at[c], lse_own),
                (part_hbm.at[c], part_own),
                (weight_hbm, weights.at[z]),
                (weight_below, weights.at[below]),
                (weight_above, weights.at[above]),
            )
        )
    ]
    for copy in own_copies:
        copy.start()
    pl.semaphore_wait(barrier, len(peers))

    def send(source, target, sems, index, device):
        copy = pltpu.make_async_remote_copy(
            src_ref=source,
            dst_ref=target,
            send_sem=sems.at[(0,) + index],
            recv_sem=sems.at[(1,) + index],
            device_id=device,
            device_id_type=MESH,
        )
        copy.start()
        return copy

    lse_copies = [
        send(lse_hbm.at[other], lse_in.at[index], lse_sems, (index,), at_ctx(other))
        for index, other in enumerate(others)
    ]

    def send_part(half, index):
        return send(
            part_hbm.at[others[index], half],
            part_in.at[index, half],
            part_sems,
            (index, half),
            at_ctx(others[index]),
        )

    ring = {}

    def forward(distance, part):
        for way in range(2):
            if distance == 4 and way != part:
                continue
            origin = (z + count + (1 - distance if way == 0 else distance - 1)) % count
            span = pl.ds(part * piece_rows, piece_rows)
            target = weights.at[origin, span]
            if distance == 2:
                source = (weight_below, weight_above)[way].at[span]
            else:
                source = target
            ring[distance, part, way] = send(
                source, target, ring_sems, (distance - 2, part, way), at_z(1 if way == 0 else -1)
            )

    def receive(distance, part):
        for way in range(2):
            if distance == 4 and way != part:
                continue
            ring[distance, part, way].wait_recv()
        if distance < 4:
            forward(distance + 1, part)

    part_copies = [[send_part(0, index) for index in range(steps)], []]
    forward(2, 0)
    forward(2, 1)
    for index in range(steps):
        part_copies[0][index].wait_send()
        part_copies[1].append(send_part(1, index))

    own_copies[0].wait()
    for copy in lse_copies:
        copy.wait_recv()
    each_lse = [lse_own[...]] + [lse_in[index] for index in range(steps)]
    top = functools.reduce(jnp.maximum, each_lse)
    weighing = [jnp.exp2(lse - top) for lse in each_lse]
    inverse = 1.0 / functools.reduce(jnp.add, weighing)
    weighing = [weight * inverse for weight in weighing]
    own_copies[1].wait()
    gathers = {}

    def combine(half):
        for group in range(groups):
            row = half * groups + group
            total[group] = part_own[half, group].astype(jnp.float32) * weighing[0][row : row + 1]
        for index in range(steps):
            part_copies[half][index].wait_recv()
            for group in range(groups):
                row = half * groups + group
                total[group] += (
                    part_in[index, half, group].astype(jnp.float32)
                    * weighing[index + 1][row : row + 1]
                )
        for group in range(groups):
            turned = total[group].T.astype(jnp.bfloat16)
            for head in range(heads):
                gathered[
                    half,
                    r,
                    group * token_rows : (group + 1) * token_rows,
                    head * head_size : (head + 1) * head_size,
                ] = turned[head * token_rows : (head + 1) * token_rows]
        for index in range(2):
            block = gathered.at[half, r]
            gathers[half, index] = send(
                block, block, gather_sems, (half, index), at_local(locals_[index])
            )

    def relay(half):
        gathers[half, 1].wait_recv()
        block = gathered.at[half, locals_[1]]
        gathers[half, 2] = send(block, block, gather_sems, (half, 2), at_local(locals_[0]))

    receive(2, 0)
    combine(0)
    receive(2, 1)
    relay(0)
    receive(3, 0)
    combine(1)
    relay(1)
    receive(3, 1)
    for half in range(halves):
        for index in (0, 2):
            gathers[half, index].wait_recv()
    for copy in own_copies[2:]:
        copy.wait()
    receive(4, 0)
    receive(4, 1)

    shard_copies = []

    def project(column):
        for half in range(halves):
            value = gathered[half].reshape(near * rows, weights.shape[1])
            result = jnp.dot(value, weights[column], preferred_element_type=jnp.float32)
            product[column, half * near * rows : (half + 1) * near * rows] = result.astype(
                jnp.bfloat16
            )

    for index, other in enumerate(others):
        project(other)
        shard_copies.append(
            send(product.at[other], shard_in.at[index], shard_sems, (index,), at_ctx(other))
        )
    project(c)
    for copy in shard_copies:
        copy.wait_recv()
    final_copies = []
    for index, owner in enumerate([*locals_[::-1], r]):
        for half in range(halves):
            base = pl.multiple_of((half * near + owner) * rows, rows)
            span = pl.ds(base, rows)
            value = product[c, span].astype(jnp.float32)
            for step in range(steps):
                value = value + shard_in[step, span].astype(jnp.float32)
            summed[owner, half] = value.astype(jnp.bfloat16)
        if index < near - 1:
            final_copies.append(
                send(summed.at[owner], final.at[r], final_sems, (index,), at_local(owner))
            )
    final[r] = summed[r]
    for copy in final_copies:
        copy.wait_recv()
    for source in range(near):
        for half in range(halves):
            for group in range(groups):
                start = (group * halves + half) * token_rows
                out_ref[start : start + token_rows, source * shard : (source + 1) * shard] = final[
                    source, half, group * token_rows : (group + 1) * token_rows
                ]
    started = lse_copies + part_copies[1] + shard_copies + final_copies
    for copies in (ring, gathers):
        started += copies.values()
    for copy in started:
        copy.wait_send()


def project(part, lse, weight, weight_below, weight_above, near):
    count, halves, groups, head_size, lanes = part.shape
    width, shard = weight.shape
    rows = groups * lanes * head_size // width
    steps = len(CTX_STEPS)
    vmem = pl.BlockSpec(memory_space=pltpu.VMEM)
    anywhere = pl.BlockSpec(memory_space=pl.ANY)
    bf16, f32, dma = jnp.bfloat16, jnp.float32, pltpu.SemaphoreType.DMA
    return pl.pallas_call(
        functools.partial(project_kernel, near),
        out_shape=jax.ShapeDtypeStruct((halves * rows, near * shard), bf16),
        in_specs=[anywhere, anywhere, anywhere, vmem, vmem],
        out_specs=vmem,
        scratch_shapes=[
            pltpu.VMEM((count,) + weight.shape, bf16),
            pltpu.VMEM((halves, groups, head_size, lanes), bf16),
            pltpu.VMEM((steps, halves, groups, head_size, lanes), bf16),
            pltpu.VMEM(lse.shape[1:], f32),
            pltpu.VMEM((steps,) + lse.shape[1:], f32),
            pltpu.VMEM((groups, head_size, lanes), f32),
            pltpu.VMEM((halves, near, rows, width), bf16),
            pltpu.VMEM((count, near * halves * rows, shard), bf16),
            pltpu.VMEM((steps, near * halves * rows, shard), bf16),
            pltpu.VMEM((near, halves, rows, shard), bf16),
            pltpu.VMEM((near, halves, rows, shard), bf16),
            dma((5,)),
            dma((2, steps, halves)),
            dma((2, steps)),
            dma((2, 3, 2, 2)),
            dma((2, halves, 3)),
            dma((2, steps)),
            dma((2, 3)),
        ],
        compiler_params=pltpu.CompilerParams(
            collective_id=0, has_side_effects=True, vmem_limit_bytes=51 * 1024 * 1024
        ),
    )(part, lse, weight, weight_below, weight_above)


def shards(
    queries, key_pages, value_pages, new_keys, new_values, page_table, lengths, parents, o_weight
):
    ctx_count = lax.axis_size("ctx")
    fsdp_count = lax.axis_size("fsdp")
    traj, new, _ = queries.shape
    near = fsdp_count // ctx_count

    def moved(step):
        pairs = [(at, (at + step * near) % fsdp_count) for at in range(fsdp_count)]
        return lax.ppermute(o_weight, "fsdp", pairs)

    weight_below, weight_above = moved(1), moved(-1)
    part, lse = attend(
        queries, key_pages, value_pages, new_keys, new_values, page_table, lengths, parents
    )
    mixed = project(part, lse, o_weight, weight_below, weight_above, near)
    return mixed.reshape(traj, new, -1)


def solution(mesh):
    placed = (
        P("fsdp", None, None),
        P("ctx", None, None),
        P("ctx", None, None),
        P("fsdp", None, "ctx", None),
        P("fsdp", None, "ctx", None),
        P("fsdp", None),
        P("fsdp"),
        P("fsdp", None),
        P("ctx", "fsdp"),
    )
    return jax.shard_map(
        shards, mesh=mesh, in_specs=placed, out_specs=P("fsdp", None, "ctx"), check_vma=False
    )
```

```python
import functools

import jax
import jax.numpy as jnp
from jax import lax
from jax.experimental import pallas as pl
from jax.experimental.pallas import tpu as pltpu
from jax.sharding import PartitionSpec as P

SHARE = 8
DEAD = -1e30
LOG2E = 1.4426950408889634


def attention_kernel(
    shared_entries,
    table_ref,
    lengths_ref,
    parents_ref,
    query_hbm,
    keys_hbm,
    values_hbm,
    new_keys_hbm,
    new_values_hbm,
    out_hbm,
    lse_ref,
    query_ref,
    group_ref,
    new_keys_ref,
    new_values_ref,
    acc_ref,
    max_ref,
    sum_ref,
    out_ref,
    keys_ref,
    values_ref,
    unit_ref,
    query_sem,
    new_sem,
    out_sem,
    key_sem,
    value_sem,
):
    table_len, traj = table_ref.shape
    new = parents_ref.shape[0]
    pages_local, page_len, width = keys_hbm.shape
    kv_count, head_size, lanes = acc_ref.shape
    rows = SHARE * new
    groups = traj // SHARE
    heads = lanes // rows
    slots = keys_ref.shape[0]
    ctx_index = lax.axis_index("ctx")
    first_page = ctx_index * pages_local
    scale = LOG2E / head_size**0.5

    query_copies = [
        pltpu.make_async_copy(
            query_hbm.at[pl.ds(group * SHARE, SHARE)],
            query_ref.at[pl.ds(group * SHARE, SHARE)],
            query_sem.at[group],
        )
        for group in range(groups)
    ]
    new_copies = [
        pltpu.make_async_copy(new_keys_hbm, new_keys_ref, new_sem.at[0]),
        pltpu.make_async_copy(new_values_hbm, new_values_ref, new_sem.at[1]),
    ]
    query_copies[0].start()
    for copy in new_copies + query_copies[1:]:
        copy.start()

    def entry_live(member, entry, count, owner, reach):
        page = table_ref[entry, owner] - first_page
        live = (page >= 0) & (page < pages_local) & (reach > entry * page_len)

        @pl.when(live)
        def _():
            unit_ref[0, count] = member
            unit_ref[1, count] = page
            unit_ref[2, count] = entry * page_len

        return count + live.astype(jnp.int32)

    def own_units(owner, count):
        reach = lengths_ref[owner]
        last = jnp.minimum((reach + page_len - 1) // page_len, table_len)
        return lax.fori_loop(
            shared_entries,
            last,
            lambda entry, count: entry_live(owner % SHARE, entry, count, owner, reach),
            count,
        )

    count = 0
    bounds = [0]
    for group in range(groups):
        reach = lengths_ref[group * SHARE]
        for member in range(1, SHARE):
            reach = jnp.maximum(reach, lengths_ref[group * SHARE + member])
        count = lax.fori_loop(
            0,
            jnp.minimum((reach + page_len - 1) // page_len, shared_entries),
            lambda entry, count: entry_live(-1, entry, count, group * SHARE, reach),
            count,
        )
        count = lax.fori_loop(group * SHARE, (group + 1) * SHARE, own_units, count)
        bounds.append(count)

    def fetch(unit):
        slot = unit % slots
        page = unit_ref[1, unit]
        return (
            pltpu.make_async_copy(keys_hbm.at[page], keys_ref.at[slot], key_sem.at[slot]),
            pltpu.make_async_copy(values_hbm.at[page], values_ref.at[slot], value_sem.at[slot]),
        )

    def start_fetch(unit):
        @pl.when(unit < count)
        def _():
            for copy in fetch(unit):
                copy.start()

    for ahead in range(slots - 1):
        start_fetch(ahead)

    lane = lax.broadcasted_iota(jnp.int32, (1, lanes), 1)
    lane_token = lane // (lanes // 2) * (rows // 2) + lane % (rows // 2)
    lane_traj = lane_token // new
    sub = lax.broadcasted_iota(jnp.int32, (rows, lanes), 0)
    own_row = lax.broadcasted_iota(jnp.int32, (kv_count, lanes), 0) == ctx_index
    position = lax.broadcasted_iota(jnp.int32, (page_len, lanes), 0)

    def gather_queries(group, kv):
        parts = []
        for head in range(heads):
            column = (kv * heads + head) * head_size
            if not isinstance(column, int):
                column = pl.multiple_of(column, head_size)
            value = query_ref[group * SHARE : (group + 1) * SHARE, :, pl.ds(column, head_size)]
            parts.append(value.reshape(rows, head_size))
        return jnp.concatenate(
            [part[: rows // 2] for part in parts] + [part[rows // 2 :] for part in parts], axis=0
        )

    def block(keys, values, query, live):
        scores = (
            lax.dot_general(
                keys, query, (((1,), (1,)), ((), ())), preferred_element_type=jnp.float32
            )
            * scale
        )
        scores = jnp.where(live, scores, DEAD)
        block_max = jnp.max(scores, axis=0, keepdims=True)
        expo = jnp.exp2(scores - jnp.maximum(block_max, 0.1 * DEAD))
        block_sum = jnp.sum(expo, axis=0, keepdims=True)
        block_out = lax.dot_general(
            values,
            expo.astype(jnp.bfloat16),
            (((0,), (0,)), ((), ())),
            preferred_element_type=jnp.float32,
        )
        return block_max, block_sum, block_out

    def new_block(group):
        bits = jnp.zeros((1, lanes), jnp.int32)
        for member in range(SHARE):
            seen = []
            for token in range(new):
                parent = parents_ref[token, group * SHARE + member]
                mask = jnp.int32(1 << token)
                for earlier in range(token):
                    mask = mask | jnp.where(parent == earlier, seen[earlier], 0)
                seen.append(mask)
                bits = jnp.where(lane_token == member * new + token, mask, bits)
        live = (sub // new == lane_traj) & (((bits >> (sub % new)) & 1) == 1)
        span = slice(group * SHARE, (group + 1) * SHARE)
        return block(
            new_keys_ref[span].reshape(rows, head_size),
            new_values_ref[span].reshape(rows, head_size),
            gather_queries(group, ctx_index),
            live,
        )

    def unit_step(group, unit):
        start_fetch(unit + slots - 1)
        slot = unit % slots
        member = unit_ref[0, unit]
        offset = unit_ref[2, unit]
        limit = jnp.zeros((1, lanes), jnp.int32)
        for each in range(SHARE):
            reach = jnp.where(
                (member < 0) | (member == each), lengths_ref[group * SHARE + each] - offset, 0
            )
            limit = jnp.where(lane_traj == each, reach, limit)
        live = position < limit
        for copy in fetch(unit):
            copy.wait()
        run_max = max_ref[...]
        run_sum = sum_ref[...]
        next_max = []
        next_sum = []
        for kv in range(kv_count):
            columns = slice(kv * head_size, (kv + 1) * head_size)
            block_max, block_sum, block_out = block(
                keys_ref[slot, :, columns],
                values_ref[slot, :, columns],
                group_ref[kv],
                live,
            )
            old_max = run_max[kv : kv + 1]
            new_max = jnp.maximum(old_max, block_max)
            keep = jnp.exp2(old_max - new_max)
            factor = jnp.exp2(block_max - new_max)
            next_max.append(new_max)
            next_sum.append(run_sum[kv : kv + 1] * keep + block_sum * factor)
            acc_ref[kv] = acc_ref[kv] * keep + block_out * factor
        max_ref[...] = jnp.concatenate(next_max, axis=0)
        sum_ref[...] = jnp.concatenate(next_sum, axis=0)

    def finish(group):
        total = sum_ref[...]
        some = total > 0.0
        safe = jnp.where(some, total, 1.0)
        inverse = jnp.where(some, 1.0 / safe, 0.0)
        lse = jnp.where(some, max_ref[...] + jnp.log2(safe), DEAD)
        for kv in range(kv_count):
            for half in range(2):
                row = half * groups + group
                lse_ref[kv, row : row + 1] = lse[
                    kv : kv + 1, half * (lanes // 2) : (half + 1) * (lanes // 2)
                ]
        return inverse

    def store(group, kv, value):
        for half in range(2):
            out_ref[group, kv, half] = value[
                :, half * (lanes // 2) : (half + 1) * (lanes // 2)
            ]

    out_copies = []
    for group in range(groups):
        query_copies[group].wait()
        if group == 0:
            for copy in new_copies:
                copy.wait()
        block_max, block_sum, block_out = new_block(group)
        max_ref[...] = jnp.where(own_row, block_max, DEAD)
        sum_ref[...] = jnp.where(own_row, block_sum, 0.0)
        busy = bounds[group + 1] > bounds[group]

        @pl.when(busy)
        def _():
            for kv in range(kv_count):
                group_ref[kv] = gather_queries(group, kv)
                acc_ref[kv] = jnp.zeros((head_size, lanes), jnp.float32)
            acc_ref[ctx_index] = block_out

            def step(unit, _):
                unit_step(group, unit)
                return 0

            lax.fori_loop(bounds[group], bounds[group + 1], step, 0)
            inverse = finish(group)
            for kv in range(kv_count):
                store(group, kv, (acc_ref[kv] * inverse[kv : kv + 1]).astype(jnp.bfloat16))

        @pl.when(jnp.logical_not(busy))
        def _():
            inverse = finish(group)
            own = jnp.sum(jnp.where(own_row, inverse, 0.0), axis=0, keepdims=True)
            for kv in range(kv_count):
                store(group, kv, jnp.zeros((head_size, lanes), jnp.bfloat16))
            store(group, ctx_index, (block_out * own).astype(jnp.bfloat16))

        copy = pltpu.make_async_copy(out_ref.at[group], out_hbm.at[:, :, group], out_sem.at[group])
        copy.start()
        out_copies.append(copy)
    for copy in out_copies:
        copy.wait()


def page_attention(table, lengths, parents, query, keys, values, new_keys, new_values):
    table_len, traj = table.shape
    new = parents.shape[0]
    head_size = new_keys.shape[-1]
    rows = SHARE * new
    groups = traj // SHARE
    pages, page_len, width = keys.shape
    kv_count = width // head_size
    heads = query.shape[2] // width
    lanes = rows * heads
    slots = 4
    units = traj * table_len
    smem = pl.BlockSpec(memory_space=pltpu.SMEM)
    vmem = pl.BlockSpec(memory_space=pltpu.VMEM)
    anywhere = pl.BlockSpec(memory_space=pl.ANY)
    bf16, f32, dma = jnp.bfloat16, jnp.float32, pltpu.SemaphoreType.DMA
    return pl.pallas_call(
        functools.partial(attention_kernel, table_len // 2),
        out_shape=(
            jax.ShapeDtypeStruct((kv_count, 2, groups, head_size, lanes // 2), bf16),
            jax.ShapeDtypeStruct((kv_count, 8, lanes // 2), f32),
        ),
        in_specs=[smem, smem, smem] + [anywhere] * 5,
        out_specs=(anywhere, vmem),
        scratch_shapes=[
            pltpu.VMEM(query.shape, bf16),
            pltpu.VMEM((kv_count, lanes, head_size), bf16),
            pltpu.VMEM(new_keys.shape, bf16),
            pltpu.VMEM(new_values.shape, bf16),
            pltpu.VMEM((kv_count, head_size, lanes), f32),
            pltpu.VMEM((kv_count, lanes), f32),
            pltpu.VMEM((kv_count, lanes), f32),
            pltpu.VMEM((groups, kv_count, 2, head_size, lanes // 2), bf16),
            pltpu.VMEM((slots, page_len, width), bf16),
            pltpu.VMEM((slots, page_len, width), bf16),
            pltpu.SMEM((3, units), jnp.int32),
            dma((groups,)),
            dma((2,)),
            dma((groups,)),
            dma((slots,)),
            dma((slots,)),
        ],
        cost_estimate=pl.CostEstimate(
            flops=10**10, bytes_accessed=10**7, transcendentals=10**7
        ),
        compiler_params=pltpu.CompilerParams(vmem_limit_bytes=56 * 1024 * 1024),
    )(table, lengths, parents, query, keys, values, new_keys, new_values)


def attend(queries, keys, values, new_keys, new_values, table, lengths, parents):
    traj, new, _, head_size = new_keys.shape
    return page_attention(
        table.T,
        lengths,
        parents.T,
        queries,
        keys,
        values,
        new_keys.reshape(traj, new, head_size),
        new_values.reshape(traj, new, head_size),
    )


CTX_STEPS = ((2, 1), (2, 0), (1, 1), (3, 1), (0, 1), (1, 0), (3, 0))
MESH = pl.DeviceIdType.MESH


def project_kernel(
    near,
    part_hbm,
    lse_hbm,
    weight_hbm,
    weight_below,
    weight_above,
    out_ref,
    weights,
    part_own,
    part_in,
    lse_own,
    lse_in,
    total,
    gathered,
    product,
    shard_in,
    own_sems,
    part_sems,
    lse_sems,
    ring_sems,
    gather_sems,
    shard_send,
    shard_recv,
):
    count = lax.axis_size("ctx")
    c = lax.axis_index("ctx")
    f = lax.axis_index("fsdp")
    z, r = f // near, f % near
    halves, groups, head_size, lanes = part_own.shape
    rows = gathered.shape[2]
    token_rows = rows // groups
    heads = lanes // token_rows
    shard = product.shape[4]
    piece_rows = weights.shape[1] // 2
    steps = len(CTX_STEPS)

    def ctx_step(dx, dy):
        return ((c // 2 + dx) % (count // 2)) * 2 + (c % 2 + dy) % 2

    others = [ctx_step(*step) for step in CTX_STEPS]
    locals_ = [
        (r // 2 + dy) % 2 * 2 + (r % 2 + dcore) % 2 for dy, dcore in ((0, 1), (1, 0), (1, 1))
    ]

    def at_ctx(other):
        return (other, f)

    def at_local(other):
        return (c, z * near + other)

    def at_z(step):
        return (c, ((z + count + step) % count) * near + r)

    barrier = pltpu.get_barrier_semaphore()
    peers = [at_ctx(other) for other in others] + [at_z(1), at_z(-1)]
    peers += [(other, z * near + local) for local in locals_ for other in (*others, c)]
    for peer in peers:
        pl.semaphore_signal(barrier, inc=1, device_id=peer, device_id_type=MESH)
    below, above = (z + count - 1) % count, (z + 1) % count
    own_copies = [
        pltpu.make_async_copy(source, target, own_sems.at[index])
        for index, (source, target) in enumerate(
            (
                (lse_hbm.at[c], lse_own),
                (part_hbm.at[c], part_own),
                (weight_hbm, weights.at[z]),
                (weight_below, weights.at[below]),
                (weight_above, weights.at[above]),
            )
        )
    ]
    for copy in own_copies:
        copy.start()
    pl.semaphore_wait(barrier, len(peers))

    def send(source, target, sems, index, device):
        copy = pltpu.make_async_remote_copy(
            src_ref=source,
            dst_ref=target,
            send_sem=sems.at[(0,) + index],
            recv_sem=sems.at[(1,) + index],
            device_id=device,
            device_id_type=MESH,
        )
        copy.start()
        return copy

    lse_copies = [
        send(lse_hbm.at[other], lse_in.at[index], lse_sems, (index,), at_ctx(other))
        for index, other in enumerate(others)
    ]

    def send_part(half, index):
        return send(
            part_hbm.at[others[index], half],
            part_in.at[index, half],
            part_sems,
            (index, half),
            at_ctx(others[index]),
        )

    ring = {}

    def forward(distance, part):
        for way in range(2):
            if distance == 4 and way != part:
                continue
            origin = (z + count + (1 - distance if way == 0 else distance - 1)) % count
            span = pl.ds(part * piece_rows, piece_rows)
            target = weights.at[origin, span]
            if distance == 2:
                source = (weight_below, weight_above)[way].at[span]
            else:
                source = target
            ring[distance, part, way] = send(
                source, target, ring_sems, (distance - 2, part, way), at_z(1 if way == 0 else -1)
            )

    def receive(distance, part):
        for way in range(2):
            if distance == 4 and way != part:
                continue
            ring[distance, part, way].wait_recv()
        if distance < 4:
            forward(distance + 1, part)

    part_copies = [[send_part(0, index) for index in range(steps)], []]
    forward(2, 0)
    forward(2, 1)
    for index in range(steps):
        part_copies[0][index].wait_send()
        part_copies[1].append(send_part(1, index))

    own_copies[0].wait()
    for copy in lse_copies:
        copy.wait_recv()
    each_lse = [lse_own[...]] + [lse_in[index] for index in range(steps)]
    top = functools.reduce(jnp.maximum, each_lse)
    weighing = [jnp.exp2(lse - top) for lse in each_lse]
    inverse = 1.0 / functools.reduce(jnp.add, weighing)
    weighing = [weight * inverse for weight in weighing]
    own_copies[1].wait()
    gathers = {}

    def combine(half):
        for group in range(groups):
            row = half * groups + group
            total[group] = part_own[half, group].astype(jnp.float32) * weighing[0][row : row + 1]
        for index in range(steps):
            part_copies[half][index].wait_recv()
            for group in range(groups):
                row = half * groups + group
                total[group] += (
                    part_in[index, half, group].astype(jnp.float32)
                    * weighing[index + 1][row : row + 1]
                )
        for group in range(groups):
            turned = total[group].T.astype(jnp.bfloat16)
            for head in range(heads):
                gathered[
                    half,
                    r,
                    group * token_rows : (group + 1) * token_rows,
                    head * head_size : (head + 1) * head_size,
                ] = turned[head * token_rows : (head + 1) * token_rows]
        for index in range(2):
            block = gathered.at[half, r]
            gathers[half, index] = send(
                block, block, gather_sems, (half, index), at_local(locals_[index])
            )

    def relay(half):
        gathers[half, 1].wait_recv()
        block = gathered.at[half, locals_[1]]
        gathers[half, 2] = send(block, block, gather_sems, (half, 2), at_local(locals_[0]))

    receive(2, 0)
    combine(0)
    receive(2, 1)
    relay(0)
    receive(3, 0)
    combine(1)
    relay(1)
    receive(3, 1)
    for half in range(halves):
        for index in (0, 2):
            gathers[half, index].wait_recv()
    for copy in own_copies[2:]:
        copy.wait()

    shard_copies = []

    def project(turn):
        far_turn = 3 + c % (count - 3)
        nearer = turn - (turn > far_turn).astype(jnp.int32)
        column = jnp.where(
            turn == far_turn, z + count // 2, z + count - 3 + (c + nearer) % (count - 1)
        )
        column = lax.rem(column, count)
        for half in range(halves):
            value = gathered[half].reshape(near * rows, weights.shape[1])
            result = jnp.dot(value, weights[column], preferred_element_type=jnp.float32)
            result = result.astype(jnp.bfloat16)
            for owner in range(near):
                product[column, owner, half] = result[owner * rows : (owner + 1) * rows]
        for index, owner in enumerate([*locals_[::-1], r]):
            copy = pltpu.make_async_remote_copy(
                src_ref=product.at[column, owner],
                dst_ref=shard_in.at[c, r],
                send_sem=shard_send.at[turn, index],
                recv_sem=shard_recv.at[c, r],
                device_id=(column, z * near + owner),
                device_id_type=MESH,
            )
            remote = True if index < near - 1 else column != c
            shard_copies.append((copy, remote))

            @pl.when(remote)
            def _():
                copy.start()

    for turn in range(count):
        if turn == 3:
            receive(4, 0)
            receive(4, 1)
        project(jnp.int32(turn))
    shard_in[c, r] = product[c, r]
    for source in range(near):
        for other in range(count):

            @pl.when((other != c) | (source != r))
            def _():
                pltpu.make_async_remote_copy(
                    src_ref=shard_in.at[other, source],
                    dst_ref=shard_in.at[other, source],
                    send_sem=shard_send.at[0, 0],
                    recv_sem=shard_recv.at[other, source],
                    device_id=at_z(1),
                    device_id_type=MESH,
                ).wait_recv()

        value = shard_in[0, source].astype(jnp.float32)
        for other in range(1, count):
            value = value + shard_in[other, source].astype(jnp.float32)
        value = value.astype(jnp.bfloat16)
        for half in range(halves):
            for group in range(groups):
                start = (group * halves + half) * token_rows
                out_ref[start : start + token_rows, source * shard : (source + 1) * shard] = value[
                    half, group * token_rows : (group + 1) * token_rows
                ]
    for copy, remote in shard_copies:

        @pl.when(remote)
        def _():
            copy.wait_send()

    started = lse_copies + part_copies[1]
    for copies in (ring, gathers):
        started += copies.values()
    for copy in started:
        copy.wait_send()


def project(part, lse, weight, weight_below, weight_above, near):
    count, halves, groups, head_size, lanes = part.shape
    width, shard = weight.shape
    rows = groups * lanes * head_size // width
    steps = len(CTX_STEPS)
    vmem = pl.BlockSpec(memory_space=pltpu.VMEM)
    anywhere = pl.BlockSpec(memory_space=pl.ANY)
    bf16, f32, dma = jnp.bfloat16, jnp.float32, pltpu.SemaphoreType.DMA
    return pl.pallas_call(
        functools.partial(project_kernel, near),
        out_shape=jax.ShapeDtypeStruct((halves * rows, near * shard), bf16),
        in_specs=[anywhere, anywhere, anywhere, vmem, vmem],
        out_specs=vmem,
        scratch_shapes=[
            pltpu.VMEM((count,) + weight.shape, bf16),
            pltpu.VMEM((halves, groups, head_size, lanes), bf16),
            pltpu.VMEM((steps, halves, groups, head_size, lanes), bf16),
            pltpu.VMEM(lse.shape[1:], f32),
            pltpu.VMEM((steps,) + lse.shape[1:], f32),
            pltpu.VMEM((groups, head_size, lanes), f32),
            pltpu.VMEM((halves, near, rows, width), bf16),
            pltpu.VMEM((count, near, halves, rows, shard), bf16),
            pltpu.VMEM((count, near, halves, rows, shard), bf16),
            dma((5,)),
            dma((2, steps, halves)),
            dma((2, steps)),
            dma((2, 3, 2, 2)),
            dma((2, halves, 3)),
            dma((count, near)),
            dma((count, near)),
        ],
        compiler_params=pltpu.CompilerParams(
            collective_id=0, has_side_effects=True, vmem_limit_bytes=51 * 1024 * 1024
        ),
    )(part, lse, weight, weight_below, weight_above)


def shards(
    queries, key_pages, value_pages, new_keys, new_values, page_table, lengths, parents, o_weight
):
    ctx_count = lax.axis_size("ctx")
    fsdp_count = lax.axis_size("fsdp")
    traj, new, _ = queries.shape
    near = fsdp_count // ctx_count

    def moved(step):
        pairs = [(at, (at + step * near) % fsdp_count) for at in range(fsdp_count)]
        return lax.ppermute(o_weight, "fsdp", pairs)

    weight_below, weight_above = moved(1), moved(-1)
    part, lse = attend(
        queries, key_pages, value_pages, new_keys, new_values, page_table, lengths, parents
    )
    mixed = project(part, lse, o_weight, weight_below, weight_above, near)
    return mixed.reshape(traj, new, -1)


def solution(mesh):
    placed = (
        P("fsdp", None, None),
        P("ctx", None, None),
        P("ctx", None, None),
        P("fsdp", None, "ctx", None),
        P("fsdp", None, "ctx", None),
        P("fsdp", None),
        P("fsdp"),
        P("fsdp", None),
        P("ctx", "fsdp"),
    )
    return jax.shard_map(
        shards, mesh=mesh, in_specs=placed, out_specs=P("fsdp", None, "ctx"), check_vma=False
    )
```

```python
import functools

import jax
import jax.numpy as jnp
from jax import lax
from jax.experimental import pallas as pl
from jax.experimental.pallas import tpu as pltpu
from jax.sharding import PartitionSpec as P

SHARE = 8
DEAD = -1e30
LOG2E = 1.4426950408889634


def attention_kernel(
    shared_entries,
    table_ref,
    lengths_ref,
    parents_ref,
    query_hbm,
    keys_hbm,
    values_hbm,
    new_keys_hbm,
    new_values_hbm,
    out_hbm,
    lse_ref,
    query_ref,
    group_ref,
    new_keys_ref,
    new_values_ref,
    acc_ref,
    max_ref,
    sum_ref,
    out_ref,
    keys_ref,
    values_ref,
    unit_ref,
    query_sem,
    new_sem,
    out_sem,
    key_sem,
    value_sem,
):
    table_len, traj = table_ref.shape
    new = parents_ref.shape[0]
    pages_local, page_len, width = keys_hbm.shape
    kv_count, head_size, lanes = acc_ref.shape
    rows = SHARE * new
    groups = traj // SHARE
    heads = lanes // rows
    slots = keys_ref.shape[0]
    ctx_index = lax.axis_index("ctx")
    first_page = ctx_index * pages_local
    scale = LOG2E / head_size**0.5

    query_copies = [
        pltpu.make_async_copy(
            query_hbm.at[pl.ds(group * SHARE, SHARE)],
            query_ref.at[pl.ds(group * SHARE, SHARE)],
            query_sem.at[group],
        )
        for group in range(groups)
    ]
    new_copies = [
        pltpu.make_async_copy(new_keys_hbm, new_keys_ref, new_sem.at[0]),
        pltpu.make_async_copy(new_values_hbm, new_values_ref, new_sem.at[1]),
    ]
    query_copies[0].start()
    for copy in new_copies + query_copies[1:]:
        copy.start()

    def entry_live(member, entry, count, owner, reach):
        page = table_ref[entry, owner] - first_page
        live = (page >= 0) & (page < pages_local) & (reach > entry * page_len)

        @pl.when(live)
        def _():
            unit_ref[0, count] = member
            unit_ref[1, count] = page
            unit_ref[2, count] = entry * page_len

        return count + live.astype(jnp.int32)

    def own_units(owner, count):
        reach = lengths_ref[owner]
        last = jnp.minimum((reach + page_len - 1) // page_len, table_len)
        return lax.fori_loop(
            shared_entries,
            last,
            lambda entry, count: entry_live(owner % SHARE, entry, count, owner, reach),
            count,
        )

    count = 0
    bounds = [0]
    for group in range(groups):
        reach = lengths_ref[group * SHARE]
        for member in range(1, SHARE):
            reach = jnp.maximum(reach, lengths_ref[group * SHARE + member])
        count = lax.fori_loop(
            0,
            jnp.minimum((reach + page_len - 1) // page_len, shared_entries),
            lambda entry, count: entry_live(-1, entry, count, group * SHARE, reach),
            count,
        )
        count = lax.fori_loop(group * SHARE, (group + 1) * SHARE, own_units, count)
        bounds.append(count)

    def fetch(unit):
        slot = unit % slots
        page = unit_ref[1, unit]
        return (
            pltpu.make_async_copy(keys_hbm.at[page], keys_ref.at[slot], key_sem.at[slot]),
            pltpu.make_async_copy(values_hbm.at[page], values_ref.at[slot], value_sem.at[slot]),
        )

    def start_fetch(unit):
        @pl.when(unit < count)
        def _():
            for copy in fetch(unit):
                copy.start()

    for ahead in range(slots - 1):
        start_fetch(ahead)

    lane = lax.broadcasted_iota(jnp.int32, (1, lanes), 1)
    lane_token = lane // (lanes // 2) * (rows // 2) + lane % (rows // 2)
    lane_traj = lane_token // new
    sub = lax.broadcasted_iota(jnp.int32, (rows, lanes), 0)
    own_row = lax.broadcasted_iota(jnp.int32, (kv_count, lanes), 0) == ctx_index
    position = lax.broadcasted_iota(jnp.int32, (page_len, lanes), 0)

    def gather_queries(group, kv):
        parts = []
        for head in range(heads):
            column = (kv * heads + head) * head_size
            if not isinstance(column, int):
                column = pl.multiple_of(column, head_size)
            value = query_ref[group * SHARE : (group + 1) * SHARE, :, pl.ds(column, head_size)]
            parts.append(value.reshape(rows, head_size))
        return jnp.concatenate(
            [part[: rows // 2] for part in parts] + [part[rows // 2 :] for part in parts], axis=0
        )

    def score(keys, query, live):
        scores = (
            lax.dot_general(
                keys, query, (((1,), (1,)), ((), ())), preferred_element_type=jnp.float32
            )
            * scale
        )
        return jnp.where(live, scores, DEAD)

    def weigh(scores, values):
        block_max = jnp.max(scores, axis=0, keepdims=True)
        expo = jnp.exp2(scores - jnp.maximum(block_max, 0.1 * DEAD))
        block_sum = jnp.sum(expo, axis=0, keepdims=True)
        block_out = lax.dot_general(
            values,
            expo.astype(jnp.bfloat16),
            (((0,), (0,)), ((), ())),
            preferred_element_type=jnp.float32,
        )
        return block_max, block_sum, block_out

    def block(keys, values, query, live):
        return weigh(score(keys, query, live), values)

    def new_block(group):
        bits = jnp.zeros((1, lanes), jnp.int32)
        for member in range(SHARE):
            seen = []
            for token in range(new):
                parent = parents_ref[token, group * SHARE + member]
                mask = jnp.int32(1 << token)
                for earlier in range(token):
                    mask = mask | jnp.where(parent == earlier, seen[earlier], 0)
                seen.append(mask)
                bits = jnp.where(lane_token == member * new + token, mask, bits)
        live = (sub // new == lane_traj) & (((bits >> (sub % new)) & 1) == 1)
        span = slice(group * SHARE, (group + 1) * SHARE)
        return block(
            new_keys_ref[span].reshape(rows, head_size),
            new_values_ref[span].reshape(rows, head_size),
            gather_queries(group, ctx_index),
            live,
        )

    def unit_step(group, unit):
        start_fetch(unit + slots - 1)
        slot = unit % slots
        member = unit_ref[0, unit]
        offset = unit_ref[2, unit]
        limit = jnp.zeros((1, lanes), jnp.int32)
        for each in range(SHARE):
            reach = jnp.where(
                (member < 0) | (member == each), lengths_ref[group * SHARE + each] - offset, 0
            )
            limit = jnp.where(lane_traj == each, reach, limit)
        live = position < limit
        for copy in fetch(unit):
            copy.wait()
        run_max = max_ref[...]
        run_sum = sum_ref[...]
        next_max = []
        next_sum = []
        def kv_scores(kv):
            return score(
                keys_ref[slot, :, kv * head_size : (kv + 1) * head_size], group_ref[kv], live
            )

        scores = kv_scores(0)
        for kv in range(kv_count):
            columns = slice(kv * head_size, (kv + 1) * head_size)
            ready = scores
            if kv + 1 < kv_count:
                scores = kv_scores(kv + 1)
            block_max, block_sum, block_out = weigh(ready, values_ref[slot, :, columns])
            old_max = run_max[kv : kv + 1]
            new_max = jnp.maximum(old_max, block_max)
            keep = jnp.exp2(old_max - new_max)
            factor = jnp.exp2(block_max - new_max)
            next_max.append(new_max)
            next_sum.append(run_sum[kv : kv + 1] * keep + block_sum * factor)
            acc_ref[kv] = acc_ref[kv] * keep + block_out * factor
        max_ref[...] = jnp.concatenate(next_max, axis=0)
        sum_ref[...] = jnp.concatenate(next_sum, axis=0)

    def finish(group):
        total = sum_ref[...]
        some = total > 0.0
        safe = jnp.where(some, total, 1.0)
        inverse = jnp.where(some, 1.0 / safe, 0.0)
        lse = jnp.where(some, max_ref[...] + jnp.log2(safe), DEAD)
        for kv in range(kv_count):
            for half in range(2):
                row = half * groups + group
                lse_ref[kv, row : row + 1] = lse[
                    kv : kv + 1, half * (lanes // 2) : (half + 1) * (lanes // 2)
                ]
        return inverse

    def store(group, kv, value):
        for half in range(2):
            out_ref[group, kv, half] = value[
                :, half * (lanes // 2) : (half + 1) * (lanes // 2)
            ]

    out_copies = []
    for group in range(groups):
        query_copies[group].wait()
        if group == 0:
            for copy in new_copies:
                copy.wait()
        block_max, block_sum, block_out = new_block(group)
        max_ref[...] = jnp.where(own_row, block_max, DEAD)
        sum_ref[...] = jnp.where(own_row, block_sum, 0.0)
        busy = bounds[group + 1] > bounds[group]

        @pl.when(busy)
        def _():
            for kv in range(kv_count):
                group_ref[kv] = gather_queries(group, kv)
                acc_ref[kv] = jnp.zeros((head_size, lanes), jnp.float32)
            acc_ref[ctx_index] = block_out

            def step(unit, _):
                unit_step(group, unit)
                return 0

            lax.fori_loop(bounds[group], bounds[group + 1], step, 0)
            inverse = finish(group)
            for kv in range(kv_count):
                store(group, kv, (acc_ref[kv] * inverse[kv : kv + 1]).astype(jnp.bfloat16))

        @pl.when(jnp.logical_not(busy))
        def _():
            inverse = finish(group)
            own = jnp.sum(jnp.where(own_row, inverse, 0.0), axis=0, keepdims=True)
            for kv in range(kv_count):
                store(group, kv, jnp.zeros((head_size, lanes), jnp.bfloat16))
            store(group, ctx_index, (block_out * own).astype(jnp.bfloat16))

        copy = pltpu.make_async_copy(out_ref.at[group], out_hbm.at[:, :, group], out_sem.at[group])
        copy.start()
        out_copies.append(copy)
    for copy in out_copies:
        copy.wait()


def page_attention(table, lengths, parents, query, keys, values, new_keys, new_values):
    table_len, traj = table.shape
    new = parents.shape[0]
    head_size = new_keys.shape[-1]
    rows = SHARE * new
    groups = traj // SHARE
    pages, page_len, width = keys.shape
    kv_count = width // head_size
    heads = query.shape[2] // width
    lanes = rows * heads
    slots = 4
    units = traj * table_len
    smem = pl.BlockSpec(memory_space=pltpu.SMEM)
    vmem = pl.BlockSpec(memory_space=pltpu.VMEM)
    anywhere = pl.BlockSpec(memory_space=pl.ANY)
    bf16, f32, dma = jnp.bfloat16, jnp.float32, pltpu.SemaphoreType.DMA
    return pl.pallas_call(
        functools.partial(attention_kernel, table_len // 2),
        out_shape=(
            jax.ShapeDtypeStruct((kv_count, 2, groups, head_size, lanes // 2), bf16),
            jax.ShapeDtypeStruct((kv_count, 8, lanes // 2), f32),
        ),
        in_specs=[smem, smem, smem] + [anywhere] * 5,
        out_specs=(anywhere, vmem),
        scratch_shapes=[
            pltpu.VMEM(query.shape, bf16),
            pltpu.VMEM((kv_count, lanes, head_size), bf16),
            pltpu.VMEM(new_keys.shape, bf16),
            pltpu.VMEM(new_values.shape, bf16),
            pltpu.VMEM((kv_count, head_size, lanes), f32),
            pltpu.VMEM((kv_count, lanes), f32),
            pltpu.VMEM((kv_count, lanes), f32),
            pltpu.VMEM((groups, kv_count, 2, head_size, lanes // 2), bf16),
            pltpu.VMEM((slots, page_len, width), bf16),
            pltpu.VMEM((slots, page_len, width), bf16),
            pltpu.SMEM((3, units), jnp.int32),
            dma((groups,)),
            dma((2,)),
            dma((groups,)),
            dma((slots,)),
            dma((slots,)),
        ],
        cost_estimate=pl.CostEstimate(
            flops=10**10, bytes_accessed=10**7, transcendentals=10**7
        ),
        compiler_params=pltpu.CompilerParams(vmem_limit_bytes=56 * 1024 * 1024),
    )(table, lengths, parents, query, keys, values, new_keys, new_values)


def attend(queries, keys, values, new_keys, new_values, table, lengths, parents):
    traj, new, _, head_size = new_keys.shape
    return page_attention(
        table.T,
        lengths,
        parents.T,
        queries,
        keys,
        values,
        new_keys.reshape(traj, new, head_size),
        new_values.reshape(traj, new, head_size),
    )


CTX_STEPS = ((2, 1), (2, 0), (1, 1), (3, 1), (0, 1), (1, 0), (3, 0))
MESH = pl.DeviceIdType.MESH


def project_kernel(
    near,
    part_hbm,
    lse_hbm,
    weight_hbm,
    weight_below,
    weight_above,
    out_ref,
    weights,
    part_own,
    part_in,
    lse_own,
    lse_in,
    total,
    gathered,
    product,
    shard_in,
    summed,
    final,
    own_sems,
    part_sems,
    lse_sems,
    ring_sems,
    gather_sems,
    shard_send,
    shard_recv,
    final_sems,
):
    count = lax.axis_size("ctx")
    c = lax.axis_index("ctx")
    f = lax.axis_index("fsdp")
    z, r = f // near, f % near
    halves, groups, head_size, lanes = part_own.shape
    rows = gathered.shape[2]
    token_rows = rows // groups
    heads = lanes // token_rows
    shard = product.shape[2]
    piece_rows = weights.shape[1] // 2
    steps = len(CTX_STEPS)

    def ctx_step(dx, dy):
        return ((c // 2 + dx) % (count // 2)) * 2 + (c % 2 + dy) % 2

    others = [ctx_step(*step) for step in CTX_STEPS]
    locals_ = [
        (r // 2 + dy) % 2 * 2 + (r % 2 + dcore) % 2 for dy, dcore in ((0, 1), (1, 0), (1, 1))
    ]

    def at_ctx(other):
        return (other, f)

    def at_local(other):
        return (c, z * near + other)

    def at_z(step):
        return (c, ((z + count + step) % count) * near + r)

    barrier = pltpu.get_barrier_semaphore()
    peers = [at_ctx(other) for other in others]
    peers += [at_z(1), at_z(-1)] + [at_local(other) for other in locals_]
    for peer in peers:
        pl.semaphore_signal(barrier, inc=1, device_id=peer, device_id_type=MESH)
    below, above = (z + count - 1) % count, (z + 1) % count
    own_copies = [
        pltpu.make_async_copy(source, target, own_sems.at[index])
        for index, (source, target) in enumerate(
            (
                (lse_hbm.at[c], lse_own),
                (part_hbm.at[c], part_own),
                (weight_hbm, weights.at[z]),
                (weight_below, weights.at[below]),
                (weight_above, weights.at[above]),
            )
        )
    ]
    for copy in own_copies:
        copy.start()
    pl.semaphore_wait(barrier, len(peers))

    def send(source, target, sems, index, device):
        copy = pltpu.make_async_remote_copy(
            src_ref=source,
            dst_ref=target,
            send_sem=sems.at[(0,) + index],
            recv_sem=sems.at[(1,) + index],
            device_id=device,
            device_id_type=MESH,
        )
        copy.start()
        return copy

    lse_copies = [
        send(lse_hbm.at[other], lse_in.at[index], lse_sems, (index,), at_ctx(other))
        for index, other in enumerate(others)
    ]

    def send_part(half, index):
        return send(
            part_hbm.at[others[index], half],
            part_in.at[index, half],
            part_sems,
            (index, half),
            at_ctx(others[index]),
        )

    ring = {}

    def forward(distance, part):
        for way in range(2):
            if distance == 4 and way != part:
                continue
            origin = (z + count + (1 - distance if way == 0 else distance - 1)) % count
            span = pl.ds(part * piece_rows, piece_rows)
            target = weights.at[origin, span]
            if distance == 2:
                source = (weight_below, weight_above)[way].at[span]
            else:
                source = target
            ring[distance, part, way] = send(
                source, target, ring_sems, (distance - 2, part, way), at_z(1 if way == 0 else -1)
            )

    def receive(distance, part):
        for way in range(2):
            if distance == 4 and way != part:
                continue
            ring[distance, part, way].wait_recv()
        if distance < 4:
            forward(distance + 1, part)

    part_copies = [[send_part(0, index) for index in range(steps)], []]
    forward(2, 0)
    forward(2, 1)
    for index in range(steps):
        part_copies[0][index].wait_send()
        part_copies[1].append(send_part(1, index))

    own_copies[0].wait()
    for copy in lse_copies:
        copy.wait_recv()
    each_lse = [lse_own[...]] + [lse_in[index] for index in range(steps)]
    top = functools.reduce(jnp.maximum, each_lse)
    weighing = [jnp.exp2(lse - top) for lse in each_lse]
    inverse = 1.0 / functools.reduce(jnp.add, weighing)
    weighing = [weight * inverse for weight in weighing]
    own_copies[1].wait()
    gathers = {}

    def combine(half):
        for group in range(groups):
            row = half * groups + group
            total[group] = part_own[half, group].astype(jnp.float32) * weighing[0][row : row + 1]
        for index in range(steps):
            part_copies[half][index].wait_recv()
            for group in range(groups):
                row = half * groups + group
                total[group] += (
                    part_in[index, half, group].astype(jnp.float32)
                    * weighing[index + 1][row : row + 1]
                )
        for group in range(groups):
            turned = total[group].T.astype(jnp.bfloat16)
            for head in range(heads):
                gathered[
                    half,
                    r,
                    group * token_rows : (group + 1) * token_rows,
                    head * head_size : (head + 1) * head_size,
                ] = turned[head * token_rows : (head + 1) * token_rows]
        for index in range(2):
            block = gathered.at[half, r]
            gathers[half, index] = send(
                block, block, gather_sems, (half, index), at_local(locals_[index])
            )

    def relay(half):
        gathers[half, 1].wait_recv()
        block = gathered.at[half, locals_[1]]
        gathers[half, 2] = send(block, block, gather_sems, (half, 2), at_local(locals_[0]))

    receive(2, 0)
    combine(0)
    receive(2, 1)
    relay(0)
    receive(3, 0)
    combine(1)
    relay(1)
    receive(3, 1)
    for half in range(halves):
        for index in (0, 2):
            gathers[half, index].wait_recv()
    for copy in own_copies[2:]:
        copy.wait()

    order = [dx * 2 + dy for dx, dy in (*CTX_STEPS, (0, 0))]
    far = (z + count // 2) % count
    far_step = (far // 2 - c // 2 + count // 2) % (count // 2) * 2 + (far % 2 + c % 2) % 2
    shard_copies = []

    def project(turn):
        step = order[turn]
        for early in range(3):
            late = early + 3
            if turn == early:
                step = jnp.where(far_step == order[early], order[late], order[early])
            if turn == late:
                step = jnp.where(far_step == order[early], order[early], order[late])
        column = ctx_step(step // 2, step % 2)
        for half in range(halves):
            value = gathered[half].reshape(near * rows, weights.shape[1])
            result = jnp.dot(value, weights[column], preferred_element_type=jnp.float32)
            product[column, half * near * rows : (half + 1) * near * rows] = result.astype(
                jnp.bfloat16
            )
        copy = pltpu.make_async_remote_copy(
            src_ref=product.at[column],
            dst_ref=shard_in.at[c],
            send_sem=shard_send.at[turn],
            recv_sem=shard_recv.at[c],
            device_id=at_ctx(column),
            device_id_type=MESH,
        )
        shard_copies.append((copy, column))

        @pl.when(column != c)
        def _():
            copy.start()

    for turn in range(count):
        if turn == 3:
            receive(4, 0)
            receive(4, 1)
        project(turn)
    shard_in[c] = product[c]
    for other in range(count):

        @pl.when(other != c)
        def _():
            pltpu.make_async_remote_copy(
                src_ref=shard_in.at[other],
                dst_ref=shard_in.at[other],
                send_sem=shard_send.at[0],
                recv_sem=shard_recv.at[other],
                device_id=at_z(1),
                device_id_type=MESH,
            ).wait_recv()

    final_copies = []
    for index, owner in enumerate([*locals_[::-1], r]):
        for half in range(halves):
            base = pl.multiple_of((half * near + owner) * rows, rows)
            span = pl.ds(base, rows)
            value = shard_in[0, span].astype(jnp.float32)
            for other in range(1, count):
                value = value + shard_in[other, span].astype(jnp.float32)
            summed[owner, half] = value.astype(jnp.bfloat16)
        if index < near - 1:
            final_copies.append(
                send(summed.at[owner], final.at[r], final_sems, (index,), at_local(owner))
            )
    final[r] = summed[r]
    for copy in final_copies:
        copy.wait_recv()
    for source in range(near):
        for half in range(halves):
            for group in range(groups):
                start = (group * halves + half) * token_rows
                out_ref[start : start + token_rows, source * shard : (source + 1) * shard] = final[
                    source, half, group * token_rows : (group + 1) * token_rows
                ]
    for copy, column in shard_copies:

        @pl.when(column != c)
        def _():
            copy.wait_send()

    started = lse_copies + part_copies[1] + final_copies
    for copies in (ring, gathers):
        started += copies.values()
    for copy in started:
        copy.wait_send()


def project(part, lse, weight, weight_below, weight_above, near):
    count, halves, groups, head_size, lanes = part.shape
    width, shard = weight.shape
    rows = groups * lanes * head_size // width
    steps = len(CTX_STEPS)
    vmem = pl.BlockSpec(memory_space=pltpu.VMEM)
    anywhere = pl.BlockSpec(memory_space=pl.ANY)
    bf16, f32, dma = jnp.bfloat16, jnp.float32, pltpu.SemaphoreType.DMA
    return pl.pallas_call(
        functools.partial(project_kernel, near),
        out_shape=jax.ShapeDtypeStruct((halves * rows, near * shard), bf16),
        in_specs=[anywhere, anywhere, anywhere, vmem, vmem],
        out_specs=vmem,
        scratch_shapes=[
            pltpu.VMEM((count,) + weight.shape, bf16),
            pltpu.VMEM((halves, groups, head_size, lanes), bf16),
            pltpu.VMEM((steps, halves, groups, head_size, lanes), bf16),
            pltpu.VMEM(lse.shape[1:], f32),
            pltpu.VMEM((steps,) + lse.shape[1:], f32),
            pltpu.VMEM((groups, head_size, lanes), f32),
            pltpu.VMEM((halves, near, rows, width), bf16),
            pltpu.VMEM((count, near * halves * rows, shard), bf16),
            pltpu.VMEM((count, near * halves * rows, shard), bf16),
            pltpu.VMEM((near, halves, rows, shard), bf16),
            pltpu.VMEM((near, halves, rows, shard), bf16),
            dma((5,)),
            dma((2, steps, halves)),
            dma((2, steps)),
            dma((2, 3, 2, 2)),
            dma((2, halves, 3)),
            dma((count,)),
            dma((count,)),
            dma((2, 3)),
        ],
        compiler_params=pltpu.CompilerParams(
            collective_id=0, has_side_effects=True, vmem_limit_bytes=51 * 1024 * 1024
        ),
    )(part, lse, weight, weight_below, weight_above)


def shards(
    queries, key_pages, value_pages, new_keys, new_values, page_table, lengths, parents, o_weight
):
    ctx_count = lax.axis_size("ctx")
    fsdp_count = lax.axis_size("fsdp")
    traj, new, _ = queries.shape
    near = fsdp_count // ctx_count

    def moved(step):
        pairs = [(at, (at + step * near) % fsdp_count) for at in range(fsdp_count)]
        return lax.ppermute(o_weight, "fsdp", pairs)

    weight_below, weight_above = moved(1), moved(-1)
    part, lse = attend(
        queries, key_pages, value_pages, new_keys, new_values, page_table, lengths, parents
    )
    mixed = project(part, lse, o_weight, weight_below, weight_above, near)
    return mixed.reshape(traj, new, -1)


def solution(mesh):
    placed = (
        P("fsdp", None, None),
        P("ctx", None, None),
        P("ctx", None, None),
        P("fsdp", None, "ctx", None),
        P("fsdp", None, "ctx", None),
        P("fsdp", None),
        P("fsdp"),
        P("fsdp", None),
        P("ctx", "fsdp"),
    )
    return jax.shard_map(
        shards, mesh=mesh, in_specs=placed, out_specs=P("fsdp", None, "ctx"), check_vma=False
    )
```

```python
import functools

import jax
import jax.numpy as jnp
from jax import lax
from jax.experimental import pallas as pl
from jax.experimental.pallas import tpu as pltpu
from jax.sharding import PartitionSpec as P

SHARE = 8
DEAD = -1e30
LOG2E = 1.4426950408889634
LSE_ROWS = 8
LSE_ROOM = 1024


def attention_kernel(
    shared_entries,
    table_ref,
    lengths_ref,
    parents_ref,
    query_hbm,
    keys_hbm,
    values_hbm,
    new_keys_hbm,
    new_values_hbm,
    out_hbm,
    lse_hbm,
    query_ref,
    group_ref,
    new_keys_ref,
    new_values_ref,
    acc_ref,
    max_ref,
    sum_ref,
    out_ref,
    lse_ref,
    keys_ref,
    values_ref,
    unit_ref,
    query_sem,
    new_sem,
    out_sem,
    lse_sem,
    key_sem,
    value_sem,
):
    table_len, traj = table_ref.shape
    new = parents_ref.shape[0]
    pages_local, page_len, width = keys_hbm.shape
    kv_count, head_size, lanes = acc_ref.shape
    rows = SHARE * new
    groups = traj // SHARE
    heads = lanes // rows
    slots = keys_ref.shape[0]
    ctx_index = lax.axis_index("ctx")
    first_page = ctx_index * pages_local
    scale = LOG2E / head_size**0.5

    query_copies = [
        pltpu.make_async_copy(
            query_hbm.at[pl.ds(group * SHARE, SHARE)],
            query_ref.at[pl.ds(group * SHARE, SHARE)],
            query_sem.at[group],
        )
        for group in range(groups)
    ]
    new_copies = [
        pltpu.make_async_copy(new_keys_hbm, new_keys_ref, new_sem.at[0]),
        pltpu.make_async_copy(new_values_hbm, new_values_ref, new_sem.at[1]),
    ]
    query_copies[0].start()
    for copy in new_copies + query_copies[1:]:
        copy.start()

    def entry_live(member, entry, count, owner, reach):
        page = table_ref[entry, owner] - first_page
        live = (page >= 0) & (page < pages_local) & (reach > entry * page_len)

        @pl.when(live)
        def _():
            unit_ref[0, count] = member
            unit_ref[1, count] = page
            unit_ref[2, count] = entry * page_len

        return count + live.astype(jnp.int32)

    def own_units(owner, count):
        reach = lengths_ref[owner]
        last = jnp.minimum((reach + page_len - 1) // page_len, table_len)
        return lax.fori_loop(
            shared_entries,
            last,
            lambda entry, count: entry_live(owner % SHARE, entry, count, owner, reach),
            count,
        )

    count = 0
    bounds = [0]
    for group in range(groups):
        reach = lengths_ref[group * SHARE]
        for member in range(1, SHARE):
            reach = jnp.maximum(reach, lengths_ref[group * SHARE + member])
        count = lax.fori_loop(
            0,
            jnp.minimum((reach + page_len - 1) // page_len, shared_entries),
            lambda entry, count: entry_live(-1, entry, count, group * SHARE, reach),
            count,
        )
        count = lax.fori_loop(group * SHARE, (group + 1) * SHARE, own_units, count)
        bounds.append(count)

    def fetch(unit):
        slot = unit % slots
        page = unit_ref[1, unit]
        return (
            pltpu.make_async_copy(keys_hbm.at[page], keys_ref.at[slot], key_sem.at[slot]),
            pltpu.make_async_copy(values_hbm.at[page], values_ref.at[slot], value_sem.at[slot]),
        )

    def start_fetch(unit):
        @pl.when(unit < count)
        def _():
            for copy in fetch(unit):
                copy.start()

    for ahead in range(slots - 1):
        start_fetch(ahead)

    lane = lax.broadcasted_iota(jnp.int32, (1, lanes), 1)
    lane_token = lane // (lanes // 2) * (rows // 2) + lane % (rows // 2)
    lane_traj = lane_token // new
    sub = lax.broadcasted_iota(jnp.int32, (rows, lanes), 0)
    own_row = lax.broadcasted_iota(jnp.int32, (kv_count, lanes), 0) == ctx_index
    position = lax.broadcasted_iota(jnp.int32, (page_len, lanes), 0)

    def gather_queries(group, kv):
        parts = []
        for head in range(heads):
            column = (kv * heads + head) * head_size
            if not isinstance(column, int):
                column = pl.multiple_of(column, head_size)
            value = query_ref[group * SHARE : (group + 1) * SHARE, :, pl.ds(column, head_size)]
            parts.append(value.reshape(rows, head_size))
        return jnp.concatenate(
            [part[: rows // 2] for part in parts] + [part[rows // 2 :] for part in parts], axis=0
        )

    def score(keys, query, live):
        scores = (
            lax.dot_general(
                keys, query, (((1,), (1,)), ((), ())), preferred_element_type=jnp.float32
            )
            * scale
        )
        return jnp.where(live, scores, DEAD)

    def weigh(scores, values):
        block_max = jnp.max(scores, axis=0, keepdims=True)
        expo = jnp.exp2(scores - jnp.maximum(block_max, 0.1 * DEAD))
        block_sum = jnp.sum(expo, axis=0, keepdims=True)
        block_out = lax.dot_general(
            values,
            expo.astype(jnp.bfloat16),
            (((0,), (0,)), ((), ())),
            preferred_element_type=jnp.float32,
        )
        return block_max, block_sum, block_out

    def block(keys, values, query, live):
        return weigh(score(keys, query, live), values)

    def new_block(group):
        bits = jnp.zeros((1, lanes), jnp.int32)
        for member in range(SHARE):
            seen = []
            for token in range(new):
                parent = parents_ref[token, group * SHARE + member]
                mask = jnp.int32(1 << token)
                for earlier in range(token):
                    mask = mask | jnp.where(parent == earlier, seen[earlier], 0)
                seen.append(mask)
                bits = jnp.where(lane_token == member * new + token, mask, bits)
        live = (sub // new == lane_traj) & (((bits >> (sub % new)) & 1) == 1)
        span = slice(group * SHARE, (group + 1) * SHARE)
        return block(
            new_keys_ref[span].reshape(rows, head_size),
            new_values_ref[span].reshape(rows, head_size),
            gather_queries(group, ctx_index),
            live,
        )

    def unit_step(group, unit):
        start_fetch(unit + slots - 1)
        slot = unit % slots
        member = unit_ref[0, unit]
        offset = unit_ref[2, unit]
        limit = jnp.zeros((1, lanes), jnp.int32)
        for each in range(SHARE):
            reach = jnp.where(
                (member < 0) | (member == each), lengths_ref[group * SHARE + each] - offset, 0
            )
            limit = jnp.where(lane_traj == each, reach, limit)
        live = position < limit
        for copy in fetch(unit):
            copy.wait()
        run_max = max_ref[...]
        run_sum = sum_ref[...]
        next_max = []
        next_sum = []
        def kv_scores(kv):
            return score(
                keys_ref[slot, :, kv * head_size : (kv + 1) * head_size], group_ref[kv], live
            )

        scores = kv_scores(0)
        for kv in range(kv_count):
            columns = slice(kv * head_size, (kv + 1) * head_size)
            ready = scores
            if kv + 1 < kv_count:
                scores = kv_scores(kv + 1)
            block_max, block_sum, block_out = weigh(ready, values_ref[slot, :, columns])
            old_max = run_max[kv : kv + 1]
            new_max = jnp.maximum(old_max, block_max)
            keep = jnp.exp2(old_max - new_max)
            factor = jnp.exp2(block_max - new_max)
            next_max.append(new_max)
            next_sum.append(run_sum[kv : kv + 1] * keep + block_sum * factor)
            acc_ref[kv] = acc_ref[kv] * keep + block_out * factor
        max_ref[...] = jnp.concatenate(next_max, axis=0)
        sum_ref[...] = jnp.concatenate(next_sum, axis=0)

    def finish(group):
        total = sum_ref[...]
        some = total > 0.0
        safe = jnp.where(some, total, 1.0)
        inverse = jnp.where(some, 1.0 / safe, 0.0)
        lse = jnp.where(some, max_ref[...] + jnp.log2(safe), DEAD)
        for kv in range(kv_count):
            for half in range(2):
                row = half * groups + group
                lse_ref[kv, row : row + 1] = lse[
                    kv : kv + 1, half * (lanes // 2) : (half + 1) * (lanes // 2)
                ]
        return inverse

    def store(group, kv, value):
        for half in range(2):
            out_ref[group, kv, half] = value[
                :, half * (lanes // 2) : (half + 1) * (lanes // 2)
            ]

    lse_ref[...] = jnp.zeros(lse_ref.shape, jnp.float32)
    out_copies = []
    for group in range(groups):
        query_copies[group].wait()
        if group == 0:
            for copy in new_copies:
                copy.wait()
        block_max, block_sum, block_out = new_block(group)
        max_ref[...] = jnp.where(own_row, block_max, DEAD)
        sum_ref[...] = jnp.where(own_row, block_sum, 0.0)
        busy = bounds[group + 1] > bounds[group]

        @pl.when(busy)
        def _():
            for kv in range(kv_count):
                group_ref[kv] = gather_queries(group, kv)
                acc_ref[kv] = jnp.zeros((head_size, lanes), jnp.float32)
            acc_ref[ctx_index] = block_out

            def step(unit, _):
                unit_step(group, unit)
                return 0

            lax.fori_loop(bounds[group], bounds[group + 1], step, 0)
            inverse = finish(group)
            for kv in range(kv_count):
                store(group, kv, (acc_ref[kv] * inverse[kv : kv + 1]).astype(jnp.bfloat16))

        @pl.when(jnp.logical_not(busy))
        def _():
            inverse = finish(group)
            own = jnp.sum(jnp.where(own_row, inverse, 0.0), axis=0, keepdims=True)
            for kv in range(kv_count):
                store(group, kv, jnp.zeros((head_size, lanes), jnp.bfloat16))
            store(group, ctx_index, (block_out * own).astype(jnp.bfloat16))

        copy = pltpu.make_async_copy(out_ref.at[group], out_hbm.at[:, :, group], out_sem.at[group])
        copy.start()
        out_copies.append(copy)
    copy = pltpu.make_async_copy(lse_ref, lse_hbm.at[:, pl.ds(0, lse_ref.shape[1])], lse_sem)
    copy.start()
    out_copies.append(copy)
    for copy in out_copies:
        copy.wait()


def page_attention(table, lengths, parents, query, keys, values, new_keys, new_values):
    table_len, traj = table.shape
    new = parents.shape[0]
    head_size = new_keys.shape[-1]
    rows = SHARE * new
    groups = traj // SHARE
    pages, page_len, width = keys.shape
    kv_count = width // head_size
    heads = query.shape[2] // width
    lanes = rows * heads
    slots = 4
    units = traj * table_len
    smem = pl.BlockSpec(memory_space=pltpu.SMEM)
    vmem = pl.BlockSpec(memory_space=pltpu.VMEM)
    anywhere = pl.BlockSpec(memory_space=pl.ANY)
    bf16, f32, dma = jnp.bfloat16, jnp.float32, pltpu.SemaphoreType.DMA
    return pl.pallas_call(
        functools.partial(attention_kernel, table_len // 2),
        out_shape=(
            jax.ShapeDtypeStruct((kv_count, 2, groups, head_size, lanes // 2), bf16),
            jax.ShapeDtypeStruct((kv_count, LSE_ROOM, lanes // 2), f32),
        ),
        in_specs=[smem, smem, smem] + [anywhere] * 5,
        out_specs=(anywhere, anywhere),
        scratch_shapes=[
            pltpu.VMEM(query.shape, bf16),
            pltpu.VMEM((kv_count, lanes, head_size), bf16),
            pltpu.VMEM(new_keys.shape, bf16),
            pltpu.VMEM(new_values.shape, bf16),
            pltpu.VMEM((kv_count, head_size, lanes), f32),
            pltpu.VMEM((kv_count, lanes), f32),
            pltpu.VMEM((kv_count, lanes), f32),
            pltpu.VMEM((groups, kv_count, 2, head_size, lanes // 2), bf16),
            pltpu.VMEM((kv_count, LSE_ROWS, lanes // 2), f32),
            pltpu.VMEM((slots, page_len, width), bf16),
            pltpu.VMEM((slots, page_len, width), bf16),
            pltpu.SMEM((3, units), jnp.int32),
            dma((groups,)),
            dma((2,)),
            dma((groups,)),
            dma,
            dma((slots,)),
            dma((slots,)),
        ],
        cost_estimate=pl.CostEstimate(
            flops=10**10, bytes_accessed=10**7, transcendentals=10**7
        ),
        compiler_params=pltpu.CompilerParams(vmem_limit_bytes=56 * 1024 * 1024),
    )(table, lengths, parents, query, keys, values, new_keys, new_values)


def attend(queries, keys, values, new_keys, new_values, table, lengths, parents):
    traj, new, _, head_size = new_keys.shape
    return page_attention(
        table.T,
        lengths,
        parents.T,
        queries,
        keys,
        values,
        new_keys.reshape(traj, new, head_size),
        new_values.reshape(traj, new, head_size),
    )


CTX_STEPS = ((2, 1), (2, 0), (1, 1), (3, 1), (0, 1), (1, 0), (3, 0))
MESH = pl.DeviceIdType.MESH


def project_kernel(
    near,
    part_hbm,
    lse_hbm,
    weight_hbm,
    weight_below,
    weight_above,
    out_ref,
    weights,
    part_own,
    part_in,
    lse_own,
    lse_in,
    total,
    gathered,
    product,
    shard_in,
    sums,
    summed,
    final,
    own_sems,
    part_sems,
    lse_sems,
    ring_sems,
    gather_sems,
    shard_send,
    shard_recv,
    final_sems,
):
    count = lax.axis_size("ctx")
    c = lax.axis_index("ctx")
    f = lax.axis_index("fsdp")
    z, r = f // near, f % near
    halves, groups, head_size, lanes = part_own.shape
    rows = gathered.shape[2]
    token_rows = rows // groups
    heads = lanes // token_rows
    shard = product.shape[2]
    piece_rows = weights.shape[1] // 2
    steps = len(CTX_STEPS)

    def ctx_step(dx, dy):
        return ((c // 2 + dx) % (count // 2)) * 2 + (c % 2 + dy) % 2

    others = [ctx_step(*step) for step in CTX_STEPS]
    locals_ = [
        (r // 2 + dy) % 2 * 2 + (r % 2 + dcore) % 2 for dy, dcore in ((0, 1), (1, 0), (1, 1))
    ]

    def at_ctx(other):
        return (other, f)

    def at_local(other):
        return (c, z * near + other)

    def at_z(step):
        return (c, ((z + count + step) % count) * near + r)

    barrier = pltpu.get_barrier_semaphore()
    peers = [at_ctx(other) for other in others]
    peers += [at_z(1), at_z(-1)] + [at_local(other) for other in locals_]
    for peer in peers:
        pl.semaphore_signal(barrier, inc=1, device_id=peer, device_id_type=MESH)
    below, above = (z + count - 1) % count, (z + 1) % count
    own_copies = [
        pltpu.make_async_copy(source, target, own_sems.at[index])
        for index, (source, target) in enumerate(
            (
                (lse_hbm.at[c, pl.ds(0, LSE_ROWS)], lse_own),
                (part_hbm.at[c], part_own),
                (weight_hbm, weights.at[z]),
                (weight_below, weights.at[below]),
                (weight_above, weights.at[above]),
            )
        )
    ]
    for copy in own_copies:
        copy.start()
    pl.semaphore_wait(barrier, len(peers))

    def send(source, target, sems, index, device):
        copy = pltpu.make_async_remote_copy(
            src_ref=source,
            dst_ref=target,
            send_sem=sems.at[(0,) + index],
            recv_sem=sems.at[(1,) + index],
            device_id=device,
            device_id_type=MESH,
        )
        copy.start()
        return copy

    lse_copies = [
        send(
            lse_hbm.at[other, pl.ds(0, LSE_ROWS)],
            lse_in.at[index],
            lse_sems,
            (index,),
            at_ctx(other),
        )
        for index, other in enumerate(others)
    ]

    def send_part(half, index):
        return send(
            part_hbm.at[others[index], half],
            part_in.at[index, half],
            part_sems,
            (index, half),
            at_ctx(others[index]),
        )

    ring = {}

    def forward(distance, part):
        for way in range(2):
            if distance == 4 and way != part:
                continue
            origin = (z + count + (1 - distance if way == 0 else distance - 1)) % count
            span = pl.ds(part * piece_rows, piece_rows)
            target = weights.at[origin, span]
            if distance == 2:
                source = (weight_below, weight_above)[way].at[span]
            else:
                source = target
            ring[distance, part, way] = send(
                source, target, ring_sems, (distance - 2, part, way), at_z(1 if way == 0 else -1)
            )

    def receive(distance, part):
        for way in range(2):
            if distance == 4 and way != part:
                continue
            ring[distance, part, way].wait_recv()
        if distance < 4:
            forward(distance + 1, part)

    part_copies = [[send_part(0, index) for index in range(steps)], []]
    forward(2, 0)
    forward(2, 1)
    for index in range(steps):
        part_copies[0][index].wait_send()
        part_copies[1].append(send_part(1, index))

    own_copies[0].wait()
    for copy in lse_copies:
        copy.wait_recv()
    each_lse = [lse_own[...]] + [lse_in[index] for index in range(steps)]
    top = functools.reduce(jnp.maximum, each_lse)
    weighing = [jnp.exp2(lse - top) for lse in each_lse]
    inverse = 1.0 / functools.reduce(jnp.add, weighing)
    weighing = [weight * inverse for weight in weighing]
    own_copies[1].wait()
    gathers = {}

    def combine(half):
        for group in range(groups):
            row = half * groups + group
            total[group] = part_own[half, group].astype(jnp.float32) * weighing[0][row : row + 1]
        for index in range(steps):
            part_copies[half][index].wait_recv()
            for group in range(groups):
                row = half * groups + group
                total[group] += (
                    part_in[index, half, group].astype(jnp.float32)
                    * weighing[index + 1][row : row + 1]
                )
        for group in range(groups):
            turned = total[group].T.astype(jnp.bfloat16)
            for head in range(heads):
                gathered[
                    half,
                    r,
                    group * token_rows : (group + 1) * token_rows,
                    head * head_size : (head + 1) * head_size,
                ] = turned[head * token_rows : (head + 1) * token_rows]
        for index in range(2):
            block = gathered.at[half, r]
            gathers[half, index] = send(
                block, block, gather_sems, (half, index), at_local(locals_[index])
            )

    def relay(half):
        gathers[half, 1].wait_recv()
        block = gathered.at[half, locals_[1]]
        gathers[half, 2] = send(block, block, gather_sems, (half, 2), at_local(locals_[0]))

    receive(2, 0)
    combine(0)
    receive(2, 1)
    relay(0)
    receive(3, 0)
    combine(1)
    relay(1)
    receive(3, 1)
    for half in range(halves):
        for index in (0, 2):
            gathers[half, index].wait_recv()
    for copy in own_copies[2:]:
        copy.wait()

    order = [dx * 2 + dy for dx, dy in (*CTX_STEPS, (0, 0))]
    far = (z + count // 2) % count
    far_step = (far // 2 - c // 2 + count // 2) % (count // 2) * 2 + (far % 2 + c % 2) % 2
    shard_copies = []

    def project(turn):
        step = order[turn]
        for early in range(3):
            late = early + 3
            if turn == early:
                step = jnp.where(far_step == order[early], order[late], order[early])
            if turn == late:
                step = jnp.where(far_step == order[early], order[early], order[late])
        column = ctx_step(step // 2, step % 2)
        for half in range(halves):
            value = gathered[half].reshape(near * rows, weights.shape[1])
            result = jnp.dot(value, weights[column], preferred_element_type=jnp.float32)
            product[column, half * near * rows : (half + 1) * near * rows] = result.astype(
                jnp.bfloat16
            )
        copy = pltpu.make_async_remote_copy(
            src_ref=product.at[column],
            dst_ref=shard_in.at[c],
            send_sem=shard_send.at[turn],
            recv_sem=shard_recv.at[c],
            device_id=at_ctx(column),
            device_id_type=MESH,
        )
        shard_copies.append((copy, column))

        @pl.when(column != c)
        def _():
            copy.start()

    for turn in range(count):
        if turn == 3:
            receive(4, 0)
            receive(4, 1)
        project(turn)
    sums[...] = product[c].astype(jnp.float32)
    for dx, dy in CTX_STEPS:
        other = ctx_step(count // 2 - dx, dy)
        pltpu.make_async_remote_copy(
            src_ref=shard_in.at[other],
            dst_ref=shard_in.at[other],
            send_sem=shard_send.at[0],
            recv_sem=shard_recv.at[other],
            device_id=at_z(1),
            device_id_type=MESH,
        ).wait_recv()
        sums[...] += shard_in[other].astype(jnp.float32)
    final_copies = []
    for index, owner in enumerate([*locals_[::-1], r]):
        for half in range(halves):
            span = pl.ds(pl.multiple_of((half * near + owner) * rows, rows), rows)
            summed[owner, half] = sums[span].astype(jnp.bfloat16)
        if index < near - 1:
            final_copies.append(
                send(summed.at[owner], final.at[r], final_sems, (index,), at_local(owner))
            )
    final[r] = summed[r]
    for copy in final_copies:
        copy.wait_recv()
    for source in range(near):
        for half in range(halves):
            for group in range(groups):
                start = (group * halves + half) * token_rows
                out_ref[start : start + token_rows, source * shard : (source + 1) * shard] = final[
                    source, half, group * token_rows : (group + 1) * token_rows
                ]
    for copy, column in shard_copies:

        @pl.when(column != c)
        def _():
            copy.wait_send()

    started = lse_copies + part_copies[1] + final_copies
    for copies in (ring, gathers):
        started += copies.values()
    for copy in started:
        copy.wait_send()


def project(part, lse, weight, weight_below, weight_above, near):
    count, halves, groups, head_size, lanes = part.shape
    width, shard = weight.shape
    rows = groups * lanes * head_size // width
    steps = len(CTX_STEPS)
    vmem = pl.BlockSpec(memory_space=pltpu.VMEM)
    anywhere = pl.BlockSpec(memory_space=pl.ANY)
    bf16, f32, dma = jnp.bfloat16, jnp.float32, pltpu.SemaphoreType.DMA
    return pl.pallas_call(
        functools.partial(project_kernel, near),
        out_shape=jax.ShapeDtypeStruct((halves * rows, near * shard), bf16),
        in_specs=[anywhere, anywhere, anywhere, vmem, vmem],
        out_specs=vmem,
        scratch_shapes=[
            pltpu.VMEM((count,) + weight.shape, bf16),
            pltpu.VMEM((halves, groups, head_size, lanes), bf16),
            pltpu.VMEM((steps, halves, groups, head_size, lanes), bf16),
            pltpu.VMEM((LSE_ROWS, lanes), f32),
            pltpu.VMEM((steps, LSE_ROWS, lanes), f32),
            pltpu.VMEM((groups, head_size, lanes), f32),
            pltpu.VMEM((halves, near, rows, width), bf16),
            pltpu.VMEM((count, near * halves * rows, shard), bf16),
            pltpu.VMEM((count, near * halves * rows, shard), bf16),
            pltpu.VMEM((near * halves * rows, shard), f32),
            pltpu.VMEM((near, halves, rows, shard), bf16),
            pltpu.VMEM((near, halves, rows, shard), bf16),
            dma((5,)),
            dma((2, steps, halves)),
            dma((2, steps)),
            dma((2, 3, 2, 2)),
            dma((2, halves, 3)),
            dma((count,)),
            dma((count,)),
            dma((2, 3)),
        ],
        compiler_params=pltpu.CompilerParams(
            collective_id=0, has_side_effects=True, vmem_limit_bytes=51 * 1024 * 1024
        ),
    )(part, lse, weight, weight_below, weight_above)


def shards(
    queries, key_pages, value_pages, new_keys, new_values, page_table, lengths, parents, o_weight
):
    ctx_count = lax.axis_size("ctx")
    fsdp_count = lax.axis_size("fsdp")
    traj, new, _ = queries.shape
    near = fsdp_count // ctx_count

    def moved(step):
        pairs = [(at, (at + step * near) % fsdp_count) for at in range(fsdp_count)]
        return lax.ppermute(o_weight, "fsdp", pairs)

    weight_below, weight_above = moved(1), moved(-1)
    part, lse = attend(
        queries, key_pages, value_pages, new_keys, new_values, page_table, lengths, parents
    )
    mixed = project(part, lse, o_weight, weight_below, weight_above, near)
    return mixed.reshape(traj, new, -1)


def solution(mesh):
    placed = (
        P("fsdp", None, None),
        P("ctx", None, None),
        P("ctx", None, None),
        P("fsdp", None, "ctx", None),
        P("fsdp", None, "ctx", None),
        P("fsdp", None),
        P("fsdp"),
        P("fsdp", None),
        P("ctx", "fsdp"),
    )
    return jax.shard_map(
        shards, mesh=mesh, in_specs=placed, out_specs=P("fsdp", None, "ctx"), check_vma=False
    )
```

```python
import functools

import jax
import jax.numpy as jnp
from jax import lax
from jax.experimental import pallas as pl
from jax.experimental.pallas import tpu as pltpu
from jax.sharding import PartitionSpec as P

SHARE = 8
DEAD = -1e30
LOG2E = 1.4426950408889634
LSE_ROWS = 8
LSE_ROOM = 1024


def attention_kernel(
    shared_entries,
    table_ref,
    lengths_ref,
    parents_ref,
    query_hbm,
    keys_hbm,
    values_hbm,
    new_keys_hbm,
    new_values_hbm,
    out_hbm,
    lse_hbm,
    query_ref,
    group_ref,
    new_keys_ref,
    new_values_ref,
    acc_ref,
    max_ref,
    sum_ref,
    out_ref,
    lse_ref,
    keys_ref,
    values_ref,
    unit_ref,
    query_sem,
    new_sem,
    out_sem,
    lse_sem,
    key_sem,
    value_sem,
):
    table_len, traj = table_ref.shape
    new = parents_ref.shape[0]
    pages_local, page_len, width = keys_hbm.shape
    kv_count, head_size, lanes = acc_ref.shape
    rows = SHARE * new
    groups = traj // SHARE
    heads = lanes // rows
    slots = keys_ref.shape[0]
    ctx_index = lax.axis_index("ctx")
    first_page = ctx_index * pages_local
    scale = LOG2E / head_size**0.5

    query_copies = [
        pltpu.make_async_copy(
            query_hbm.at[pl.ds(group * SHARE, SHARE)],
            query_ref.at[pl.ds(group * SHARE, SHARE)],
            query_sem.at[group],
        )
        for group in range(groups)
    ]
    new_copies = [
        pltpu.make_async_copy(new_keys_hbm, new_keys_ref, new_sem.at[0]),
        pltpu.make_async_copy(new_values_hbm, new_values_ref, new_sem.at[1]),
    ]
    query_copies[0].start()
    for copy in new_copies + query_copies[1:]:
        copy.start()

    def entry_live(member, entry, count, owner, reach):
        page = table_ref[entry, owner] - first_page
        live = (page >= 0) & (page < pages_local) & (reach > entry * page_len)

        @pl.when(live)
        def _():
            unit_ref[0, count] = member
            unit_ref[1, count] = page
            unit_ref[2, count] = entry * page_len

        return count + live.astype(jnp.int32)

    def own_units(owner, count):
        reach = lengths_ref[owner]
        last = jnp.minimum((reach + page_len - 1) // page_len, table_len)
        return lax.fori_loop(
            shared_entries,
            last,
            lambda entry, count: entry_live(owner % SHARE, entry, count, owner, reach),
            count,
        )

    count = 0
    bounds = [0]
    for group in range(groups):
        reach = lengths_ref[group * SHARE]
        for member in range(1, SHARE):
            reach = jnp.maximum(reach, lengths_ref[group * SHARE + member])
        count = lax.fori_loop(
            0,
            jnp.minimum((reach + page_len - 1) // page_len, shared_entries),
            lambda entry, count: entry_live(-1, entry, count, group * SHARE, reach),
            count,
        )
        count = lax.fori_loop(group * SHARE, (group + 1) * SHARE, own_units, count)
        bounds.append(count)

    def fetch(unit):
        slot = unit % slots
        page = unit_ref[1, unit]
        return (
            pltpu.make_async_copy(keys_hbm.at[page], keys_ref.at[slot], key_sem.at[slot]),
            pltpu.make_async_copy(values_hbm.at[page], values_ref.at[slot], value_sem.at[slot]),
        )

    def start_fetch(unit):
        @pl.when(unit < count)
        def _():
            for copy in fetch(unit):
                copy.start()

    for ahead in range(slots - 1):
        start_fetch(ahead)

    lane = lax.broadcasted_iota(jnp.int32, (1, lanes), 1)
    lane_token = lane // (lanes // 2) * (rows // 2) + lane % (rows // 2)
    lane_traj = lane_token // new
    sub = lax.broadcasted_iota(jnp.int32, (rows, lanes), 0)
    own_row = lax.broadcasted_iota(jnp.int32, (kv_count, lanes), 0) == ctx_index
    position = lax.broadcasted_iota(jnp.int32, (page_len, lanes), 0)

    def gather_queries(group, kv):
        parts = []
        for head in range(heads):
            column = (kv * heads + head) * head_size
            if not isinstance(column, int):
                column = pl.multiple_of(column, head_size)
            value = query_ref[group * SHARE : (group + 1) * SHARE, :, pl.ds(column, head_size)]
            parts.append(value.reshape(rows, head_size))
        return jnp.concatenate(
            [part[: rows // 2] for part in parts] + [part[rows // 2 :] for part in parts], axis=0
        )

    def score(keys, query, live):
        scores = (
            lax.dot_general(
                keys, query, (((1,), (1,)), ((), ())), preferred_element_type=jnp.float32
            )
            * scale
        )
        return jnp.where(live, scores, DEAD)

    def weigh(scores, values):
        block_max = jnp.max(scores, axis=0, keepdims=True)
        expo = jnp.exp2(scores - jnp.maximum(block_max, 0.1 * DEAD))
        block_sum = jnp.sum(expo, axis=0, keepdims=True)
        block_out = lax.dot_general(
            values,
            expo.astype(jnp.bfloat16),
            (((0,), (0,)), ((), ())),
            preferred_element_type=jnp.float32,
        )
        return block_max, block_sum, block_out

    def block(keys, values, query, live):
        return weigh(score(keys, query, live), values)

    def new_block(group):
        bits = jnp.zeros((1, lanes), jnp.int32)
        for member in range(SHARE):
            seen = []
            for token in range(new):
                parent = parents_ref[token, group * SHARE + member]
                mask = jnp.int32(1 << token)
                for earlier in range(token):
                    mask = mask | jnp.where(parent == earlier, seen[earlier], 0)
                seen.append(mask)
                bits = jnp.where(lane_token == member * new + token, mask, bits)
        live = (sub // new == lane_traj) & (((bits >> (sub % new)) & 1) == 1)
        span = slice(group * SHARE, (group + 1) * SHARE)
        return block(
            new_keys_ref[span].reshape(rows, head_size),
            new_values_ref[span].reshape(rows, head_size),
            gather_queries(group, ctx_index),
            live,
        )

    def unit_step(group, unit):
        start_fetch(unit + slots - 1)
        slot = unit % slots
        member = unit_ref[0, unit]
        offset = unit_ref[2, unit]
        limit = jnp.zeros((1, lanes), jnp.int32)
        for each in range(SHARE):
            reach = jnp.where(
                (member < 0) | (member == each), lengths_ref[group * SHARE + each] - offset, 0
            )
            limit = jnp.where(lane_traj == each, reach, limit)
        live = position < limit
        for copy in fetch(unit):
            copy.wait()
        run_max = max_ref[...]
        run_sum = sum_ref[...]
        next_max = []
        next_sum = []
        def kv_scores(kv):
            return score(
                keys_ref[slot, :, kv * head_size : (kv + 1) * head_size], group_ref[kv], live
            )

        scores = kv_scores(0)
        for kv in range(kv_count):
            columns = slice(kv * head_size, (kv + 1) * head_size)
            ready = scores
            if kv + 1 < kv_count:
                scores = kv_scores(kv + 1)
            block_max, block_sum, block_out = weigh(ready, values_ref[slot, :, columns])
            old_max = run_max[kv : kv + 1]
            new_max = jnp.maximum(old_max, block_max)
            keep = jnp.exp2(old_max - new_max)
            factor = jnp.exp2(block_max - new_max)
            next_max.append(new_max)
            next_sum.append(run_sum[kv : kv + 1] * keep + block_sum * factor)
            acc_ref[kv] = acc_ref[kv] * keep + block_out * factor
        max_ref[...] = jnp.concatenate(next_max, axis=0)
        sum_ref[...] = jnp.concatenate(next_sum, axis=0)

    def finish(group):
        total = sum_ref[...]
        some = total > 0.0
        safe = jnp.where(some, total, 1.0)
        inverse = jnp.where(some, 1.0 / safe, 0.0)
        lse = jnp.where(some, max_ref[...] + jnp.log2(safe), DEAD)
        for kv in range(kv_count):
            for half in range(2):
                row = half * groups + group
                lse_ref[kv, row : row + 1] = lse[
                    kv : kv + 1, half * (lanes // 2) : (half + 1) * (lanes // 2)
                ]
        return inverse

    def store(group, kv, value):
        for half in range(2):
            out_ref[group, kv, half] = value[
                :, half * (lanes // 2) : (half + 1) * (lanes // 2)
            ]

    lse_ref[...] = jnp.zeros(lse_ref.shape, jnp.float32)
    out_copies = []
    for group in range(groups):
        query_copies[group].wait()
        if group == 0:
            for copy in new_copies:
                copy.wait()
        block_max, block_sum, block_out = new_block(group)
        max_ref[...] = jnp.where(own_row, block_max, DEAD)
        sum_ref[...] = jnp.where(own_row, block_sum, 0.0)
        busy = bounds[group + 1] > bounds[group]

        @pl.when(busy)
        def _():
            for kv in range(kv_count):
                group_ref[kv] = gather_queries(group, kv)
                acc_ref[kv] = jnp.zeros((head_size, lanes), jnp.float32)
            acc_ref[ctx_index] = block_out

            def step(unit, _):
                unit_step(group, unit)
                return 0

            lax.fori_loop(bounds[group], bounds[group + 1], step, 0)
            inverse = finish(group)
            for kv in range(kv_count):
                store(group, kv, (acc_ref[kv] * inverse[kv : kv + 1]).astype(jnp.bfloat16))

        @pl.when(jnp.logical_not(busy))
        def _():
            inverse = finish(group)
            own = jnp.sum(jnp.where(own_row, inverse, 0.0), axis=0, keepdims=True)
            for kv in range(kv_count):
                store(group, kv, jnp.zeros((head_size, lanes), jnp.bfloat16))
            store(group, ctx_index, (block_out * own).astype(jnp.bfloat16))

        copy = pltpu.make_async_copy(out_ref.at[group], out_hbm.at[:, :, group], out_sem.at[group])
        copy.start()
        out_copies.append(copy)
    copy = pltpu.make_async_copy(lse_ref, lse_hbm.at[:, pl.ds(0, lse_ref.shape[1])], lse_sem)
    copy.start()
    out_copies.append(copy)
    for copy in out_copies:
        copy.wait()


def page_attention(table, lengths, parents, query, keys, values, new_keys, new_values):
    table_len, traj = table.shape
    new = parents.shape[0]
    head_size = new_keys.shape[-1]
    rows = SHARE * new
    groups = traj // SHARE
    pages, page_len, width = keys.shape
    kv_count = width // head_size
    heads = query.shape[2] // width
    lanes = rows * heads
    slots = 4
    units = traj * table_len
    smem = pl.BlockSpec(memory_space=pltpu.SMEM)
    vmem = pl.BlockSpec(memory_space=pltpu.VMEM)
    anywhere = pl.BlockSpec(memory_space=pl.ANY)
    bf16, f32, dma = jnp.bfloat16, jnp.float32, pltpu.SemaphoreType.DMA
    return pl.pallas_call(
        functools.partial(attention_kernel, table_len // 2),
        out_shape=(
            jax.ShapeDtypeStruct((kv_count, 2, groups, head_size, lanes // 2), bf16),
            jax.ShapeDtypeStruct((kv_count, LSE_ROOM, lanes // 2), f32),
        ),
        in_specs=[smem, smem, smem] + [anywhere] * 5,
        out_specs=(anywhere, anywhere),
        scratch_shapes=[
            pltpu.VMEM(query.shape, bf16),
            pltpu.VMEM((kv_count, lanes, head_size), bf16),
            pltpu.VMEM(new_keys.shape, bf16),
            pltpu.VMEM(new_values.shape, bf16),
            pltpu.VMEM((kv_count, head_size, lanes), f32),
            pltpu.VMEM((kv_count, lanes), f32),
            pltpu.VMEM((kv_count, lanes), f32),
            pltpu.VMEM((groups, kv_count, 2, head_size, lanes // 2), bf16),
            pltpu.VMEM((kv_count, LSE_ROWS, lanes // 2), f32),
            pltpu.VMEM((slots, page_len, width), bf16),
            pltpu.VMEM((slots, page_len, width), bf16),
            pltpu.SMEM((3, units), jnp.int32),
            dma((groups,)),
            dma((2,)),
            dma((groups,)),
            dma,
            dma((slots,)),
            dma((slots,)),
        ],
        cost_estimate=pl.CostEstimate(
            flops=10**10, bytes_accessed=10**7, transcendentals=10**7
        ),
        compiler_params=pltpu.CompilerParams(vmem_limit_bytes=56 * 1024 * 1024),
    )(table, lengths, parents, query, keys, values, new_keys, new_values)


def attend(queries, keys, values, new_keys, new_values, table, lengths, parents):
    traj, new, _, head_size = new_keys.shape
    return page_attention(
        table.T,
        lengths,
        parents.T,
        queries,
        keys,
        values,
        new_keys.reshape(traj, new, head_size),
        new_values.reshape(traj, new, head_size),
    )


CTX_STEPS = ((2, 1), (2, 0), (1, 1), (3, 1), (0, 1), (1, 0), (3, 0))
MESH = pl.DeviceIdType.MESH


def project_kernel(
    near,
    part_hbm,
    lse_hbm,
    weight_hbm,
    weight_below,
    weight_above,
    out_ref,
    weights,
    part_own,
    part_in,
    lse_own,
    lse_in,
    total,
    gathered,
    product,
    shard_in,
    sums,
    summed,
    final,
    own_sems,
    part_sems,
    lse_sems,
    ring_sems,
    gather_sems,
    shard_send,
    shard_recv,
    final_sems,
):
    count = lax.axis_size("ctx")
    c = lax.axis_index("ctx")
    f = lax.axis_index("fsdp")
    z, r = f // near, f % near
    halves, groups, head_size, lanes = part_own.shape
    rows = gathered.shape[2]
    token_rows = rows // groups
    heads = lanes // token_rows
    shard = product.shape[2]
    piece_rows = weights.shape[1] // 2
    steps = len(CTX_STEPS)

    def ctx_step(dx, dy):
        return ((c // 2 + dx) % (count // 2)) * 2 + (c % 2 + dy) % 2

    others = [ctx_step(*step) for step in CTX_STEPS]
    locals_ = [
        (r // 2 + dy) % 2 * 2 + (r % 2 + dcore) % 2 for dy, dcore in ((0, 1), (1, 0), (1, 1))
    ]

    def at_ctx(other):
        return (other, f)

    def at_local(other):
        return (c, z * near + other)

    def at_z(step):
        return (c, ((z + count + step) % count) * near + r)

    barrier = pltpu.get_barrier_semaphore()
    peers = [at_ctx(other) for other in others]
    peers += [at_z(1), at_z(-1)] + [at_local(other) for other in locals_]
    for peer in peers:
        pl.semaphore_signal(barrier, inc=1, device_id=peer, device_id_type=MESH)
    below, above = (z + count - 1) % count, (z + 1) % count
    own_copies = [
        pltpu.make_async_copy(source, target, own_sems.at[index])
        for index, (source, target) in enumerate(
            (
                (lse_hbm.at[c, pl.ds(0, LSE_ROWS)], lse_own),
                (part_hbm.at[c], part_own),
                (weight_hbm, weights.at[z]),
                (weight_below, weights.at[below]),
                (weight_above, weights.at[above]),
            )
        )
    ]
    for copy in own_copies:
        copy.start()
    pl.semaphore_wait(barrier, len(peers))

    def send(source, target, sems, index, device):
        copy = pltpu.make_async_remote_copy(
            src_ref=source,
            dst_ref=target,
            send_sem=sems.at[(0,) + index],
            recv_sem=sems.at[(1,) + index],
            device_id=device,
            device_id_type=MESH,
        )
        copy.start()
        return copy

    lse_copies = [
        send(
            lse_hbm.at[other, pl.ds(0, LSE_ROWS)],
            lse_in.at[index],
            lse_sems,
            (index,),
            at_ctx(other),
        )
        for index, other in enumerate(others)
    ]

    def send_part(half, index):
        return send(
            part_hbm.at[others[index], half],
            part_in.at[index, half],
            part_sems,
            (index, half),
            at_ctx(others[index]),
        )

    ring = {}

    def forward(distance, part):
        for way in range(2):
            if distance == 4 and way != part:
                continue
            origin = (z + count + (1 - distance if way == 0 else distance - 1)) % count
            span = pl.ds(part * piece_rows, piece_rows)
            target = weights.at[origin, span]
            if distance == 2:
                source = (weight_below, weight_above)[way].at[span]
            else:
                source = target
            ring[distance, part, way] = send(
                source, target, ring_sems, (distance - 2, part, way), at_z(1 if way == 0 else -1)
            )

    def receive(distance, part):
        for way in range(2):
            if distance == 4 and way != part:
                continue
            ring[distance, part, way].wait_recv()
        if distance < 4:
            forward(distance + 1, part)

    part_copies = [[send_part(0, index) for index in range(steps)], []]
    forward(2, 0)
    forward(2, 1)
    for index in range(steps):
        part_copies[0][index].wait_send()
        part_copies[1].append(send_part(1, index))

    own_copies[0].wait()
    for copy in lse_copies:
        copy.wait_recv()
    each_lse = [lse_own[...]] + [lse_in[index] for index in range(steps)]
    top = functools.reduce(jnp.maximum, each_lse)
    weighing = [jnp.exp2(lse - top) for lse in each_lse]
    inverse = 1.0 / functools.reduce(jnp.add, weighing)
    weighing = [weight * inverse for weight in weighing]
    own_copies[1].wait()
    gathers = {}

    def combine(half):
        for group in range(groups):
            row = half * groups + group
            total[group] = part_own[half, group].astype(jnp.float32) * weighing[0][row : row + 1]
        for index in range(steps):
            part_copies[half][index].wait_recv()
            for group in range(groups):
                row = half * groups + group
                total[group] += (
                    part_in[index, half, group].astype(jnp.float32)
                    * weighing[index + 1][row : row + 1]
                )
        for group in range(groups):
            turned = total[group].T.astype(jnp.bfloat16)
            for head in range(heads):
                gathered[
                    half,
                    r,
                    group * token_rows : (group + 1) * token_rows,
                    head * head_size : (head + 1) * head_size,
                ] = turned[head * token_rows : (head + 1) * token_rows]
        for index in range(2):
            block = gathered.at[half, r]
            gathers[half, index] = send(
                block, block, gather_sems, (half, index), at_local(locals_[index])
            )

    def relay(half):
        gathers[half, 1].wait_recv()
        block = gathered.at[half, locals_[1]]
        gathers[half, 2] = send(block, block, gather_sems, (half, 2), at_local(locals_[0]))

    receive(2, 0)
    receive(2, 1)
    combine(0)
    receive(3, 0)
    relay(0)
    combine(1)
    relay(1)
    receive(3, 1)
    for half in range(halves):
        for index in (0, 2):
            gathers[half, index].wait_recv()
    for copy in own_copies[2:]:
        copy.wait()

    order = [dx * 2 + dy for dx, dy in (*CTX_STEPS, (0, 0))]
    far = (z + count // 2) % count
    far_step = (far // 2 - c // 2 + count // 2) % (count // 2) * 2 + (far % 2 + c % 2) % 2
    shard_copies = []

    def project(turn):
        step = order[turn]
        for early in range(3):
            late = early + 3
            if turn == early:
                step = jnp.where(far_step == order[early], order[late], order[early])
            if turn == late:
                step = jnp.where(far_step == order[early], order[early], order[late])
        column = ctx_step(step // 2, step % 2)
        for half in range(halves):
            value = gathered[half].reshape(near * rows, weights.shape[1])
            result = jnp.dot(value, weights[column], preferred_element_type=jnp.float32)
            product[column, half * near * rows : (half + 1) * near * rows] = result.astype(
                jnp.bfloat16
            )
        copy = pltpu.make_async_remote_copy(
            src_ref=product.at[column],
            dst_ref=shard_in.at[c],
            send_sem=shard_send.at[turn],
            recv_sem=shard_recv.at[c],
            device_id=at_ctx(column),
            device_id_type=MESH,
        )
        shard_copies.append((copy, column))

        @pl.when(column != c)
        def _():
            copy.start()

    for turn in range(count):
        if turn == 3:
            receive(4, 0)
            receive(4, 1)
        project(turn)
    sums[...] = product[c].astype(jnp.float32)
    for dx, dy in CTX_STEPS:
        other = ctx_step(count // 2 - dx, dy)
        pltpu.make_async_remote_copy(
            src_ref=shard_in.at[other],
            dst_ref=shard_in.at[other],
            send_sem=shard_send.at[0],
            recv_sem=shard_recv.at[other],
            device_id=at_z(1),
            device_id_type=MESH,
        ).wait_recv()
        sums[...] += shard_in[other].astype(jnp.float32)
    final_copies = []
    for index, owner in enumerate([*locals_[::-1], r]):
        for half in range(halves):
            span = pl.ds(pl.multiple_of((half * near + owner) * rows, rows), rows)
            summed[owner, half] = sums[span].astype(jnp.bfloat16)
        if index < near - 1:
            final_copies.append(
                send(summed.at[owner], final.at[r], final_sems, (index,), at_local(owner))
            )
    final[r] = summed[r]
    for copy in final_copies:
        copy.wait_recv()
    for source in range(near):
        for half in range(halves):
            for group in range(groups):
                start = (group * halves + half) * token_rows
                out_ref[start : start + token_rows, source * shard : (source + 1) * shard] = final[
                    source, half, group * token_rows : (group + 1) * token_rows
                ]
    for copy, column in shard_copies:

        @pl.when(column != c)
        def _():
            copy.wait_send()

    started = lse_copies + part_copies[1] + final_copies
    for copies in (ring, gathers):
        started += copies.values()
    for copy in started:
        copy.wait_send()


def project(part, lse, weight, weight_below, weight_above, near):
    count, halves, groups, head_size, lanes = part.shape
    width, shard = weight.shape
    rows = groups * lanes * head_size // width
    steps = len(CTX_STEPS)
    vmem = pl.BlockSpec(memory_space=pltpu.VMEM)
    anywhere = pl.BlockSpec(memory_space=pl.ANY)
    bf16, f32, dma = jnp.bfloat16, jnp.float32, pltpu.SemaphoreType.DMA
    return pl.pallas_call(
        functools.partial(project_kernel, near),
        out_shape=jax.ShapeDtypeStruct((halves * rows, near * shard), bf16),
        in_specs=[anywhere, anywhere, anywhere, vmem, vmem],
        out_specs=vmem,
        scratch_shapes=[
            pltpu.VMEM((count,) + weight.shape, bf16),
            pltpu.VMEM((halves, groups, head_size, lanes), bf16),
            pltpu.VMEM((steps, halves, groups, head_size, lanes), bf16),
            pltpu.VMEM((LSE_ROWS, lanes), f32),
            pltpu.VMEM((steps, LSE_ROWS, lanes), f32),
            pltpu.VMEM((groups, head_size, lanes), f32),
            pltpu.VMEM((halves, near, rows, width), bf16),
            pltpu.VMEM((count, near * halves * rows, shard), bf16),
            pltpu.VMEM((count, near * halves * rows, shard), bf16),
            pltpu.VMEM((near * halves * rows, shard), f32),
            pltpu.VMEM((near, halves, rows, shard), bf16),
            pltpu.VMEM((near, halves, rows, shard), bf16),
            dma((5,)),
            dma((2, steps, halves)),
            dma((2, steps)),
            dma((2, 3, 2, 2)),
            dma((2, halves, 3)),
            dma((count,)),
            dma((count,)),
            dma((2, 3)),
        ],
        compiler_params=pltpu.CompilerParams(
            collective_id=0, has_side_effects=True, vmem_limit_bytes=51 * 1024 * 1024
        ),
    )(part, lse, weight, weight_below, weight_above)


def shards(
    queries, key_pages, value_pages, new_keys, new_values, page_table, lengths, parents, o_weight
):
    ctx_count = lax.axis_size("ctx")
    fsdp_count = lax.axis_size("fsdp")
    traj, new, _ = queries.shape
    near = fsdp_count // ctx_count

    def moved(step):
        pairs = [(at, (at + step * near) % fsdp_count) for at in range(fsdp_count)]
        return lax.ppermute(o_weight, "fsdp", pairs)

    weight_below, weight_above = moved(1), moved(-1)
    part, lse = attend(
        queries, key_pages, value_pages, new_keys, new_values, page_table, lengths, parents
    )
    mixed = project(part, lse, o_weight, weight_below, weight_above, near)
    return mixed.reshape(traj, new, -1)


def solution(mesh):
    placed = (
        P("fsdp", None, None),
        P("ctx", None, None),
        P("ctx", None, None),
        P("fsdp", None, "ctx", None),
        P("fsdp", None, "ctx", None),
        P("fsdp", None),
        P("fsdp"),
        P("fsdp", None),
        P("ctx", "fsdp"),
    )
    return jax.shard_map(
        shards, mesh=mesh, in_specs=placed, out_specs=P("fsdp", None, "ctx"), check_vma=False
    )
```

```python
import functools

import jax
import jax.numpy as jnp
from jax import lax
from jax.experimental import pallas as pl
from jax.experimental.pallas import tpu as pltpu
from jax.sharding import PartitionSpec as P

SHARE = 8
DEAD = -1e30
LOG2E = 1.4426950408889634
LSE_ROWS = 8
LSE_ROOM = 1024


def attention_kernel(
    shared_entries,
    table_ref,
    lengths_ref,
    parents_ref,
    query_hbm,
    keys_hbm,
    values_hbm,
    new_keys_hbm,
    new_values_hbm,
    out_hbm,
    lse_hbm,
    query_ref,
    group_ref,
    new_keys_ref,
    new_values_ref,
    acc_ref,
    max_ref,
    sum_ref,
    out_ref,
    lse_ref,
    keys_ref,
    values_ref,
    unit_ref,
    query_sem,
    new_sem,
    out_sem,
    lse_sem,
    key_sem,
    value_sem,
):
    table_len, traj = table_ref.shape
    new = parents_ref.shape[0]
    pages_local, page_len, width = keys_hbm.shape
    kv_count, head_size, lanes = acc_ref.shape
    rows = SHARE * new
    groups = traj // SHARE
    heads = lanes // rows
    slots = keys_ref.shape[0]
    ctx_index = lax.axis_index("ctx")
    first_page = ctx_index * pages_local
    scale = LOG2E / head_size**0.5

    query_copies = [
        pltpu.make_async_copy(
            query_hbm.at[pl.ds(group * SHARE, SHARE)],
            query_ref.at[pl.ds(group * SHARE, SHARE)],
            query_sem.at[group],
        )
        for group in range(groups)
    ]
    new_copies = [
        pltpu.make_async_copy(new_keys_hbm, new_keys_ref, new_sem.at[0]),
        pltpu.make_async_copy(new_values_hbm, new_values_ref, new_sem.at[1]),
    ]
    query_copies[0].start()
    for copy in new_copies + query_copies[1:]:
        copy.start()

    def entry_live(member, entry, count, owner, reach):
        page = table_ref[entry, owner] - first_page
        live = (page >= 0) & (page < pages_local) & (reach > entry * page_len)

        @pl.when(live)
        def _():
            unit_ref[0, count] = member
            unit_ref[1, count] = page
            unit_ref[2, count] = entry * page_len

        return count + live.astype(jnp.int32)

    def own_units(owner, count):
        reach = lengths_ref[owner]
        last = jnp.minimum((reach + page_len - 1) // page_len, table_len)
        return lax.fori_loop(
            shared_entries,
            last,
            lambda entry, count: entry_live(owner % SHARE, entry, count, owner, reach),
            count,
        )

    count = 0
    bounds = [0]
    for group in range(groups):
        reach = lengths_ref[group * SHARE]
        for member in range(1, SHARE):
            reach = jnp.maximum(reach, lengths_ref[group * SHARE + member])
        count = lax.fori_loop(
            0,
            jnp.minimum((reach + page_len - 1) // page_len, shared_entries),
            lambda entry, count: entry_live(-1, entry, count, group * SHARE, reach),
            count,
        )
        count = lax.fori_loop(group * SHARE, (group + 1) * SHARE, own_units, count)
        bounds.append(count)

    def fetch(unit):
        slot = unit % slots
        page = unit_ref[1, unit]
        return (
            pltpu.make_async_copy(keys_hbm.at[page], keys_ref.at[slot], key_sem.at[slot]),
            pltpu.make_async_copy(values_hbm.at[page], values_ref.at[slot], value_sem.at[slot]),
        )

    def start_fetch(unit):
        @pl.when(unit < count)
        def _():
            for copy in fetch(unit):
                copy.start()

    for ahead in range(slots - 1):
        start_fetch(ahead)

    lane = lax.broadcasted_iota(jnp.int32, (1, lanes), 1)
    lane_token = lane // (lanes // 2) * (rows // 2) + lane % (rows // 2)
    lane_traj = lane_token // new
    sub = lax.broadcasted_iota(jnp.int32, (rows, lanes), 0)
    own_row = lax.broadcasted_iota(jnp.int32, (kv_count, lanes), 0) == ctx_index
    position = lax.broadcasted_iota(jnp.int32, (page_len, lanes), 0)

    def gather_queries(group, kv):
        parts = []
        for head in range(heads):
            column = (kv * heads + head) * head_size
            if not isinstance(column, int):
                column = pl.multiple_of(column, head_size)
            value = query_ref[group * SHARE : (group + 1) * SHARE, :, pl.ds(column, head_size)]
            parts.append(value.reshape(rows, head_size))
        return jnp.concatenate(
            [part[: rows // 2] for part in parts] + [part[rows // 2 :] for part in parts], axis=0
        )

    def score(keys, query, live):
        scores = (
            lax.dot_general(
                keys, query, (((1,), (1,)), ((), ())), preferred_element_type=jnp.float32
            )
            * scale
        )
        return jnp.where(live, scores, DEAD)

    def weigh(scores, values):
        block_max = jnp.max(scores, axis=0, keepdims=True)
        expo = jnp.exp2(scores - jnp.maximum(block_max, 0.1 * DEAD))
        block_sum = jnp.sum(expo, axis=0, keepdims=True)
        block_out = lax.dot_general(
            values,
            expo.astype(jnp.bfloat16),
            (((0,), (0,)), ((), ())),
            preferred_element_type=jnp.float32,
        )
        return block_max, block_sum, block_out

    def block(keys, values, query, live):
        return weigh(score(keys, query, live), values)

    def new_block(group):
        bits = jnp.zeros((1, lanes), jnp.int32)
        for member in range(SHARE):
            seen = []
            for token in range(new):
                parent = parents_ref[token, group * SHARE + member]
                mask = jnp.int32(1 << token)
                for earlier in range(token):
                    mask = mask | jnp.where(parent == earlier, seen[earlier], 0)
                seen.append(mask)
                bits = jnp.where(lane_token == member * new + token, mask, bits)
        live = (sub // new == lane_traj) & (((bits >> (sub % new)) & 1) == 1)
        span = slice(group * SHARE, (group + 1) * SHARE)
        return block(
            new_keys_ref[span].reshape(rows, head_size),
            new_values_ref[span].reshape(rows, head_size),
            gather_queries(group, ctx_index),
            live,
        )

    def unit_step(group, unit):
        start_fetch(unit + slots - 1)
        slot = unit % slots
        member = unit_ref[0, unit]
        offset = unit_ref[2, unit]
        limit = jnp.zeros((1, lanes), jnp.int32)
        for each in range(SHARE):
            reach = jnp.where(
                (member < 0) | (member == each), lengths_ref[group * SHARE + each] - offset, 0
            )
            limit = jnp.where(lane_traj == each, reach, limit)
        live = position < limit
        for copy in fetch(unit):
            copy.wait()
        run_max = max_ref[...]
        run_sum = sum_ref[...]
        next_max = []
        next_sum = []
        def kv_scores(kv):
            return score(
                keys_ref[slot, :, kv * head_size : (kv + 1) * head_size], group_ref[kv], live
            )

        scores = kv_scores(0)
        for kv in range(kv_count):
            columns = slice(kv * head_size, (kv + 1) * head_size)
            ready = scores
            if kv + 1 < kv_count:
                scores = kv_scores(kv + 1)
            block_max, block_sum, block_out = weigh(ready, values_ref[slot, :, columns])
            old_max = run_max[kv : kv + 1]
            new_max = jnp.maximum(old_max, block_max)
            keep = jnp.exp2(old_max - new_max)
            factor = jnp.exp2(block_max - new_max)
            next_max.append(new_max)
            next_sum.append(run_sum[kv : kv + 1] * keep + block_sum * factor)
            acc_ref[kv] = acc_ref[kv] * keep + block_out * factor
        max_ref[...] = jnp.concatenate(next_max, axis=0)
        sum_ref[...] = jnp.concatenate(next_sum, axis=0)

    def finish(group):
        total = sum_ref[...]
        some = total > 0.0
        safe = jnp.where(some, total, 1.0)
        inverse = jnp.where(some, 1.0 / safe, 0.0)
        lse = jnp.where(some, max_ref[...] + jnp.log2(safe), DEAD)
        for kv in range(kv_count):
            for half in range(2):
                row = half * groups + group
                lse_ref[kv, row : row + 1] = lse[
                    kv : kv + 1, half * (lanes // 2) : (half + 1) * (lanes // 2)
                ]
        return inverse

    def store(group, kv, value):
        for half in range(2):
            out_ref[group, kv, half] = value[
                :, half * (lanes // 2) : (half + 1) * (lanes // 2)
            ]

    lse_ref[...] = jnp.zeros(lse_ref.shape, jnp.float32)
    out_copies = []
    for group in range(groups):
        query_copies[group].wait()
        if group == 0:
            for copy in new_copies:
                copy.wait()
        block_max, block_sum, block_out = new_block(group)
        max_ref[...] = jnp.where(own_row, block_max, DEAD)
        sum_ref[...] = jnp.where(own_row, block_sum, 0.0)
        busy = bounds[group + 1] > bounds[group]

        @pl.when(busy)
        def _():
            for kv in range(kv_count):
                group_ref[kv] = gather_queries(group, kv)
                acc_ref[kv] = jnp.zeros((head_size, lanes), jnp.float32)
            acc_ref[ctx_index] = block_out

            def step(unit, _):
                unit_step(group, unit)
                return 0

            lax.fori_loop(bounds[group], bounds[group + 1], step, 0)
            inverse = finish(group)
            for kv in range(kv_count):
                store(group, kv, (acc_ref[kv] * inverse[kv : kv + 1]).astype(jnp.bfloat16))

        @pl.when(jnp.logical_not(busy))
        def _():
            inverse = finish(group)
            own = jnp.sum(jnp.where(own_row, inverse, 0.0), axis=0, keepdims=True)
            for kv in range(kv_count):
                store(group, kv, jnp.zeros((head_size, lanes), jnp.bfloat16))
            store(group, ctx_index, (block_out * own).astype(jnp.bfloat16))

        copy = pltpu.make_async_copy(out_ref.at[group], out_hbm.at[:, :, group], out_sem.at[group])
        copy.start()
        out_copies.append(copy)
    copy = pltpu.make_async_copy(lse_ref, lse_hbm.at[:, pl.ds(0, lse_ref.shape[1])], lse_sem)
    copy.start()
    out_copies.append(copy)
    for copy in out_copies:
        copy.wait()


def page_attention(table, lengths, parents, query, keys, values, new_keys, new_values):
    table_len, traj = table.shape
    new = parents.shape[0]
    head_size = new_keys.shape[-1]
    rows = SHARE * new
    groups = traj // SHARE
    pages, page_len, width = keys.shape
    kv_count = width // head_size
    heads = query.shape[2] // width
    lanes = rows * heads
    slots = 4
    units = traj * table_len
    smem = pl.BlockSpec(memory_space=pltpu.SMEM)
    vmem = pl.BlockSpec(memory_space=pltpu.VMEM)
    anywhere = pl.BlockSpec(memory_space=pl.ANY)
    bf16, f32, dma = jnp.bfloat16, jnp.float32, pltpu.SemaphoreType.DMA
    return pl.pallas_call(
        functools.partial(attention_kernel, table_len // 2),
        out_shape=(
            jax.ShapeDtypeStruct((kv_count, 2, groups, head_size, lanes // 2), bf16),
            jax.ShapeDtypeStruct((kv_count, LSE_ROOM, lanes // 2), f32),
        ),
        in_specs=[smem, smem, smem] + [anywhere] * 5,
        out_specs=(anywhere, anywhere),
        scratch_shapes=[
            pltpu.VMEM(query.shape, bf16),
            pltpu.VMEM((kv_count, lanes, head_size), bf16),
            pltpu.VMEM(new_keys.shape, bf16),
            pltpu.VMEM(new_values.shape, bf16),
            pltpu.VMEM((kv_count, head_size, lanes), f32),
            pltpu.VMEM((kv_count, lanes), f32),
            pltpu.VMEM((kv_count, lanes), f32),
            pltpu.VMEM((groups, kv_count, 2, head_size, lanes // 2), bf16),
            pltpu.VMEM((kv_count, LSE_ROWS, lanes // 2), f32),
            pltpu.VMEM((slots, page_len, width), bf16),
            pltpu.VMEM((slots, page_len, width), bf16),
            pltpu.SMEM((3, units), jnp.int32),
            dma((groups,)),
            dma((2,)),
            dma((groups,)),
            dma,
            dma((slots,)),
            dma((slots,)),
        ],
        cost_estimate=pl.CostEstimate(
            flops=10**10, bytes_accessed=10**7, transcendentals=10**7
        ),
        compiler_params=pltpu.CompilerParams(vmem_limit_bytes=56 * 1024 * 1024),
    )(table, lengths, parents, query, keys, values, new_keys, new_values)


def attend(queries, keys, values, new_keys, new_values, table, lengths, parents):
    traj, new, _, head_size = new_keys.shape
    return page_attention(
        table.T,
        lengths,
        parents.T,
        queries,
        keys,
        values,
        new_keys.reshape(traj, new, head_size),
        new_values.reshape(traj, new, head_size),
    )


CTX_STEPS = ((2, 1), (2, 0), (1, 1), (3, 1), (0, 1), (1, 0), (3, 0))
MESH = pl.DeviceIdType.MESH


def project_kernel(
    near,
    part_hbm,
    lse_hbm,
    weight_hbm,
    weight_below,
    weight_above,
    out_ref,
    weights,
    part_own,
    part_in,
    lse_own,
    lse_in,
    total,
    gathered,
    product,
    shard_in,
    sums,
    summed,
    final,
    own_sems,
    part_sems,
    lse_sems,
    ring_sems,
    gather_sems,
    shard_send,
    shard_recv,
    final_sems,
):
    count = lax.axis_size("ctx")
    c = lax.axis_index("ctx")
    f = lax.axis_index("fsdp")
    z, r = f // near, f % near
    halves, groups, head_size, lanes = part_own.shape
    rows = gathered.shape[2]
    token_rows = rows // groups
    heads = lanes // token_rows
    shard = product.shape[2]
    piece_rows = weights.shape[1] // 2
    steps = len(CTX_STEPS)

    def ctx_step(dx, dy):
        return ((c // 2 + dx) % (count // 2)) * 2 + (c % 2 + dy) % 2

    others = [ctx_step(*step) for step in CTX_STEPS]
    locals_ = [
        (r // 2 + dy) % 2 * 2 + (r % 2 + dcore) % 2 for dy, dcore in ((0, 1), (1, 0), (1, 1))
    ]

    def at_ctx(other):
        return (other, f)

    def at_local(other):
        return (c, z * near + other)

    def at_z(step):
        return (c, ((z + count + step) % count) * near + r)

    barrier = pltpu.get_barrier_semaphore()
    peers = [at_ctx(other) for other in others]
    peers += [at_z(1), at_z(-1)] + [at_local(other) for other in locals_]
    for peer in peers:
        pl.semaphore_signal(barrier, inc=1, device_id=peer, device_id_type=MESH)
    below, above = (z + count - 1) % count, (z + 1) % count
    own_copies = [
        pltpu.make_async_copy(source, target, own_sems.at[index])
        for index, (source, target) in enumerate(
            (
                (lse_hbm.at[c, pl.ds(0, LSE_ROWS)], lse_own),
                (part_hbm.at[c], part_own),
                (weight_hbm, weights.at[z]),
                (weight_below, weights.at[below]),
                (weight_above, weights.at[above]),
            )
        )
    ]
    for copy in own_copies:
        copy.start()
    pl.semaphore_wait(barrier, len(peers))

    def send(source, target, sems, index, device):
        copy = pltpu.make_async_remote_copy(
            src_ref=source,
            dst_ref=target,
            send_sem=sems.at[(0,) + index],
            recv_sem=sems.at[(1,) + index],
            device_id=device,
            device_id_type=MESH,
        )
        copy.start()
        return copy

    lse_copies = [
        send(
            lse_hbm.at[other, pl.ds(0, LSE_ROWS)],
            lse_in.at[index],
            lse_sems,
            (index,),
            at_ctx(other),
        )
        for index, other in enumerate(others)
    ]

    def send_part(half, index):
        return send(
            part_hbm.at[others[index], half],
            part_in.at[index, half],
            part_sems,
            (index, half),
            at_ctx(others[index]),
        )

    ring = {}

    def forward(distance, part):
        for way in range(2):
            if distance == 4 and way != part:
                continue
            origin = (z + count + (1 - distance if way == 0 else distance - 1)) % count
            span = pl.ds(part * piece_rows, piece_rows)
            target = weights.at[origin, span]
            if distance == 2:
                source = (weight_below, weight_above)[way].at[span]
            else:
                source = target
            ring[distance, part, way] = send(
                source, target, ring_sems, (distance - 2, part, way), at_z(1 if way == 0 else -1)
            )

    def receive(distance, part):
        for way in range(2):
            if distance == 4 and way != part:
                continue
            ring[distance, part, way].wait_recv()
        if distance < 4:
            forward(distance + 1, part)

    part_copies = [[send_part(0, index) for index in range(steps)], []]
    forward(2, 0)
    forward(2, 1)
    for index in range(steps):
        part_copies[0][index].wait_send()
        part_copies[1].append(send_part(1, index))

    own_copies[0].wait()
    for copy in lse_copies:
        copy.wait_recv()
    each_lse = [lse_own[...]] + [lse_in[index] for index in range(steps)]
    top = functools.reduce(jnp.maximum, each_lse)
    weighing = [jnp.exp2(lse - top) for lse in each_lse]
    inverse = 1.0 / functools.reduce(jnp.add, weighing)
    weighing = [weight * inverse for weight in weighing]
    own_copies[1].wait()
    gathers = {}

    def combine(half):
        for group in range(groups):
            row = half * groups + group
            total[group] = part_own[half, group].astype(jnp.float32) * weighing[0][row : row + 1]
        for index in range(steps):
            part_copies[half][index].wait_recv()
            for group in range(groups):
                row = half * groups + group
                total[group] += (
                    part_in[index, half, group].astype(jnp.float32)
                    * weighing[index + 1][row : row + 1]
                )
        for group in range(groups):
            turned = total[group].T.astype(jnp.bfloat16)
            for head in range(heads):
                gathered[
                    half,
                    r,
                    group * token_rows : (group + 1) * token_rows,
                    head * head_size : (head + 1) * head_size,
                ] = turned[head * token_rows : (head + 1) * token_rows]
        for index in range(2):
            block = gathered.at[half, r]
            gathers[half, index] = send(
                block, block, gather_sems, (half, index), at_local(locals_[index])
            )

    def relay(half):
        gathers[half, 1].wait_recv()
        block = gathered.at[half, locals_[1]]
        gathers[half, 2] = send(block, block, gather_sems, (half, 2), at_local(locals_[0]))

    receive(2, 0)
    receive(2, 1)
    combine(0)
    receive(3, 0)
    relay(0)
    combine(1)
    relay(1)
    receive(3, 1)
    for half in range(halves):
        for index in (0, 2):
            gathers[half, index].wait_recv()
    for copy in own_copies[2:]:
        copy.wait()

    order = [dx * 2 + dy for dx, dy in (*CTX_STEPS, (0, 0))]
    far = (z + count // 2) % count
    far_step = (far // 2 - c // 2 + count // 2) % (count // 2) * 2 + (far % 2 + c % 2) % 2
    shard_copies = []

    def project(turn):
        step = order[turn]
        for early in range(3):
            late = early + 3
            if turn == early:
                step = jnp.where(far_step == order[early], order[late], order[early])
            if turn == late:
                step = jnp.where(far_step == order[early], order[early], order[late])
        column = ctx_step(step // 2, step % 2)
        for half in range(halves):
            value = gathered[half].reshape(near * rows, weights.shape[1])
            result = jnp.dot(value, weights[column], preferred_element_type=jnp.float32)
            product[column, half * near * rows : (half + 1) * near * rows] = result.astype(
                jnp.bfloat16
            )
        copy = pltpu.make_async_remote_copy(
            src_ref=product.at[column],
            dst_ref=shard_in.at[c],
            send_sem=shard_send.at[turn],
            recv_sem=shard_recv.at[c],
            device_id=at_ctx(column),
            device_id_type=MESH,
        )
        shard_copies.append((copy, column))

        @pl.when(column != c)
        def _():
            copy.start()

    for turn in range(count):
        if turn == 3:
            receive(4, 0)
            receive(4, 1)
        project(turn)
    sums[...] = product[c].astype(jnp.float32)
    for dx, dy in CTX_STEPS:
        other = ctx_step(count // 2 - dx, dy)
        pltpu.make_async_remote_copy(
            src_ref=shard_in.at[other],
            dst_ref=shard_in.at[other],
            send_sem=shard_send.at[0],
            recv_sem=shard_recv.at[other],
            device_id=at_z(1),
            device_id_type=MESH,
        ).wait_recv()
        sums[...] += shard_in[other].astype(jnp.float32)
    final_copies = []
    for index, owner in enumerate([*locals_[::-1], r]):
        for half in range(halves):
            span = pl.ds(pl.multiple_of((half * near + owner) * rows, rows), rows)
            summed[owner, half] = sums[span].astype(jnp.bfloat16)
        if index < near - 1:
            final_copies.append(
                send(summed.at[owner], final.at[r], final_sems, (index,), at_local(owner))
            )
    final[r] = summed[r]
    for copy in final_copies:
        copy.wait_recv()
    for source in range(near):
        for half in range(halves):
            for group in range(groups):
                new = out_ref.shape[1]
                size = token_rows // new
                start = (group * halves + half) * size
                value = final[source, half, group * token_rows : (group + 1) * token_rows]
                out_ref[start : start + size, :, source * shard : (source + 1) * shard] = (
                    value.reshape(size, new, shard)
                )
    for copy, column in shard_copies:

        @pl.when(column != c)
        def _():
            copy.wait_send()

    started = lse_copies + part_copies[1] + final_copies
    for copies in (ring, gathers):
        started += copies.values()
    for copy in started:
        copy.wait_send()


def project(part, lse, weight, weight_below, weight_above, near, new):
    count, halves, groups, head_size, lanes = part.shape
    width, shard = weight.shape
    rows = groups * lanes * head_size // width
    steps = len(CTX_STEPS)
    vmem = pl.BlockSpec(memory_space=pltpu.VMEM)
    anywhere = pl.BlockSpec(memory_space=pl.ANY)
    bf16, f32, dma = jnp.bfloat16, jnp.float32, pltpu.SemaphoreType.DMA
    return pl.pallas_call(
        functools.partial(project_kernel, near),
        out_shape=jax.ShapeDtypeStruct((halves * rows // new, new, near * shard), bf16),
        in_specs=[anywhere, anywhere, anywhere, vmem, vmem],
        out_specs=vmem,
        scratch_shapes=[
            pltpu.VMEM((count,) + weight.shape, bf16),
            pltpu.VMEM((halves, groups, head_size, lanes), bf16),
            pltpu.VMEM((steps, halves, groups, head_size, lanes), bf16),
            pltpu.VMEM((LSE_ROWS, lanes), f32),
            pltpu.VMEM((steps, LSE_ROWS, lanes), f32),
            pltpu.VMEM((groups, head_size, lanes), f32),
            pltpu.VMEM((halves, near, rows, width), bf16),
            pltpu.VMEM((count, near * halves * rows, shard), bf16),
            pltpu.VMEM((count, near * halves * rows, shard), bf16),
            pltpu.VMEM((near * halves * rows, shard), f32),
            pltpu.VMEM((near, halves, rows, shard), bf16),
            pltpu.VMEM((near, halves, rows, shard), bf16),
            dma((5,)),
            dma((2, steps, halves)),
            dma((2, steps)),
            dma((2, 3, 2, 2)),
            dma((2, halves, 3)),
            dma((count,)),
            dma((count,)),
            dma((2, 3)),
        ],
        compiler_params=pltpu.CompilerParams(
            collective_id=0, has_side_effects=True, vmem_limit_bytes=51 * 1024 * 1024
        ),
    )(part, lse, weight, weight_below, weight_above)


def shards(
    queries, key_pages, value_pages, new_keys, new_values, page_table, lengths, parents, o_weight
):
    ctx_count = lax.axis_size("ctx")
    fsdp_count = lax.axis_size("fsdp")
    new = queries.shape[1]
    near = fsdp_count // ctx_count

    def moved(step):
        pairs = [(at, (at + step * near) % fsdp_count) for at in range(fsdp_count)]
        return lax.ppermute(o_weight, "fsdp", pairs)

    weight_below, weight_above = moved(1), moved(-1)
    part, lse = attend(
        queries, key_pages, value_pages, new_keys, new_values, page_table, lengths, parents
    )
    return project(part, lse, o_weight, weight_below, weight_above, near, new)


def solution(mesh):
    placed = (
        P("fsdp", None, None),
        P("ctx", None, None),
        P("ctx", None, None),
        P("fsdp", None, "ctx", None),
        P("fsdp", None, "ctx", None),
        P("fsdp", None),
        P("fsdp"),
        P("fsdp", None),
        P("ctx", "fsdp"),
    )
    return jax.shard_map(
        shards, mesh=mesh, in_specs=placed, out_specs=P("fsdp", None, "ctx"), check_vma=False
    )
```

```python
import functools

import jax
import jax.numpy as jnp
from jax import lax
from jax.experimental import pallas as pl
from jax.experimental.pallas import tpu as pltpu
from jax.sharding import PartitionSpec as P

SHARE = 8
DEAD = -1e30
LOG2E = 1.4426950408889634
LSE_ROWS = 8
LSE_ROOM = 1024


def attention_kernel(
    shared_entries,
    table_ref,
    lengths_ref,
    parents_ref,
    query_hbm,
    keys_hbm,
    values_hbm,
    new_keys_hbm,
    new_values_hbm,
    out_hbm,
    lse_hbm,
    query_ref,
    group_ref,
    new_keys_ref,
    new_values_ref,
    acc_ref,
    max_ref,
    sum_ref,
    out_ref,
    lse_ref,
    keys_ref,
    values_ref,
    unit_ref,
    query_sem,
    new_sem,
    out_sem,
    lse_sem,
    key_sem,
    value_sem,
):
    table_len, traj = table_ref.shape
    new = parents_ref.shape[0]
    pages_local, page_len, width = keys_hbm.shape
    kv_count, head_size, lanes = acc_ref.shape
    rows = SHARE * new
    groups = traj // SHARE
    heads = lanes // rows
    slots = keys_ref.shape[0]
    ctx_index = lax.axis_index("ctx")
    first_page = ctx_index * pages_local
    scale = LOG2E / head_size**0.5

    query_copies = [
        pltpu.make_async_copy(
            query_hbm.at[pl.ds(group * SHARE, SHARE)],
            query_ref.at[pl.ds(group * SHARE, SHARE)],
            query_sem.at[group],
        )
        for group in range(groups)
    ]
    new_copies = [
        pltpu.make_async_copy(new_keys_hbm, new_keys_ref, new_sem.at[0]),
        pltpu.make_async_copy(new_values_hbm, new_values_ref, new_sem.at[1]),
    ]
    query_copies[0].start()
    for copy in new_copies + query_copies[1:]:
        copy.start()

    def entry_live(member, entry, count, owner, reach):
        page = table_ref[entry, owner] - first_page
        live = (page >= 0) & (page < pages_local) & (reach > entry * page_len)

        @pl.when(live)
        def _():
            unit_ref[0, count] = member
            unit_ref[1, count] = page
            unit_ref[2, count] = entry * page_len

        return count + live.astype(jnp.int32)

    def own_units(owner, count):
        reach = lengths_ref[owner]
        last = jnp.minimum((reach + page_len - 1) // page_len, table_len)
        return lax.fori_loop(
            shared_entries,
            last,
            lambda entry, count: entry_live(owner % SHARE, entry, count, owner, reach),
            count,
        )

    count = 0
    bounds = [0]
    for group in range(groups):
        reach = lengths_ref[group * SHARE]
        for member in range(1, SHARE):
            reach = jnp.maximum(reach, lengths_ref[group * SHARE + member])
        count = lax.fori_loop(
            0,
            jnp.minimum((reach + page_len - 1) // page_len, shared_entries),
            lambda entry, count: entry_live(-1, entry, count, group * SHARE, reach),
            count,
        )
        count = lax.fori_loop(group * SHARE, (group + 1) * SHARE, own_units, count)
        bounds.append(count)

    def fetch(unit):
        slot = unit % slots
        page = unit_ref[1, unit]
        return (
            pltpu.make_async_copy(keys_hbm.at[page], keys_ref.at[slot], key_sem.at[slot]),
            pltpu.make_async_copy(values_hbm.at[page], values_ref.at[slot], value_sem.at[slot]),
        )

    def start_fetch(unit):
        @pl.when(unit < count)
        def _():
            for copy in fetch(unit):
                copy.start()

    for ahead in range(slots - 1):
        start_fetch(ahead)

    lane = lax.broadcasted_iota(jnp.int32, (1, lanes), 1)
    lane_token = lane // (lanes // 2) * (rows // 2) + lane % (rows // 2)
    lane_traj = lane_token // new
    sub = lax.broadcasted_iota(jnp.int32, (rows, lanes), 0)
    own_row = lax.broadcasted_iota(jnp.int32, (kv_count, lanes), 0) == ctx_index
    position = lax.broadcasted_iota(jnp.int32, (page_len, lanes), 0)

    def gather_queries(group, kv):
        parts = []
        for head in range(heads):
            column = (kv * heads + head) * head_size
            if not isinstance(column, int):
                column = pl.multiple_of(column, head_size)
            value = query_ref[group * SHARE : (group + 1) * SHARE, :, pl.ds(column, head_size)]
            parts.append(value.reshape(rows, head_size))
        return jnp.concatenate(
            [part[: rows // 2] for part in parts] + [part[rows // 2 :] for part in parts], axis=0
        )

    def score(keys, query, live):
        scores = (
            lax.dot_general(
                keys, query, (((1,), (1,)), ((), ())), preferred_element_type=jnp.float32
            )
            * scale
        )
        return jnp.where(live, scores, DEAD)

    def weigh(scores, values):
        block_max = jnp.max(scores, axis=0, keepdims=True)
        expo = jnp.exp2(scores - jnp.maximum(block_max, 0.1 * DEAD))
        block_sum = jnp.sum(expo, axis=0, keepdims=True)
        block_out = lax.dot_general(
            values,
            expo.astype(jnp.bfloat16),
            (((0,), (0,)), ((), ())),
            preferred_element_type=jnp.float32,
        )
        return block_max, block_sum, block_out

    def block(keys, values, query, live):
        return weigh(score(keys, query, live), values)

    def new_block(group):
        bits = jnp.zeros((1, lanes), jnp.int32)
        for member in range(SHARE):
            seen = []
            for token in range(new):
                parent = parents_ref[token, group * SHARE + member]
                mask = jnp.int32(1 << token)
                for earlier in range(token):
                    mask = mask | jnp.where(parent == earlier, seen[earlier], 0)
                seen.append(mask)
                bits = jnp.where(lane_token == member * new + token, mask, bits)
        live = (sub // new == lane_traj) & (((bits >> (sub % new)) & 1) == 1)
        span = slice(group * SHARE, (group + 1) * SHARE)
        return block(
            new_keys_ref[span].reshape(rows, head_size),
            new_values_ref[span].reshape(rows, head_size),
            gather_queries(group, ctx_index),
            live,
        )

    def unit_step(group, unit):
        start_fetch(unit + slots - 1)
        slot = unit % slots
        member = unit_ref[0, unit]
        offset = unit_ref[2, unit]
        limit = jnp.zeros((1, lanes), jnp.int32)
        for each in range(SHARE):
            reach = jnp.where(
                (member < 0) | (member == each), lengths_ref[group * SHARE + each] - offset, 0
            )
            limit = jnp.where(lane_traj == each, reach, limit)
        live = position < limit
        for copy in fetch(unit):
            copy.wait()
        run_max = max_ref[...]
        run_sum = sum_ref[...]
        next_max = []
        next_sum = []
        def kv_scores(kv):
            return score(
                keys_ref[slot, :, kv * head_size : (kv + 1) * head_size], group_ref[kv], live
            )

        scores = kv_scores(0)
        for kv in range(kv_count):
            columns = slice(kv * head_size, (kv + 1) * head_size)
            ready = scores
            if kv + 1 < kv_count:
                scores = kv_scores(kv + 1)
            block_max, block_sum, block_out = weigh(ready, values_ref[slot, :, columns])
            old_max = run_max[kv : kv + 1]
            new_max = jnp.maximum(old_max, block_max)
            keep = jnp.exp2(old_max - new_max)
            factor = jnp.exp2(block_max - new_max)
            next_max.append(new_max)
            next_sum.append(run_sum[kv : kv + 1] * keep + block_sum * factor)
            acc_ref[kv] = acc_ref[kv] * keep + block_out * factor
        max_ref[...] = jnp.concatenate(next_max, axis=0)
        sum_ref[...] = jnp.concatenate(next_sum, axis=0)

    def finish(group):
        total = sum_ref[...]
        some = total > 0.0
        safe = jnp.where(some, total, 1.0)
        inverse = jnp.where(some, 1.0 / safe, 0.0)
        lse = jnp.where(some, max_ref[...] + jnp.log2(safe), DEAD)
        for kv in range(kv_count):
            for half in range(2):
                row = half * groups + group
                lse_ref[kv, row : row + 1] = lse[
                    kv : kv + 1, half * (lanes // 2) : (half + 1) * (lanes // 2)
                ]
        return inverse

    def store(group, kv, value):
        for half in range(2):
            out_ref[group, kv, half] = value[
                :, half * (lanes // 2) : (half + 1) * (lanes // 2)
            ]

    lse_ref[...] = jnp.zeros(lse_ref.shape, jnp.float32)
    out_copies = []
    for group in range(groups):
        query_copies[group].wait()
        if group == 0:
            for copy in new_copies:
                copy.wait()
        block_max, block_sum, block_out = new_block(group)
        max_ref[...] = jnp.where(own_row, block_max, DEAD)
        sum_ref[...] = jnp.where(own_row, block_sum, 0.0)
        busy = bounds[group + 1] > bounds[group]

        @pl.when(busy)
        def _():
            for kv in range(kv_count):
                group_ref[kv] = gather_queries(group, kv)
                acc_ref[kv] = jnp.zeros((head_size, lanes), jnp.float32)
            acc_ref[ctx_index] = block_out

            def step(unit, _):
                unit_step(group, unit)
                return 0

            lax.fori_loop(bounds[group], bounds[group + 1], step, 0)
            inverse = finish(group)
            for kv in range(kv_count):
                store(group, kv, (acc_ref[kv] * inverse[kv : kv + 1]).astype(jnp.bfloat16))

        @pl.when(jnp.logical_not(busy))
        def _():
            inverse = finish(group)
            own = jnp.sum(jnp.where(own_row, inverse, 0.0), axis=0, keepdims=True)
            for kv in range(kv_count):
                store(group, kv, jnp.zeros((head_size, lanes), jnp.bfloat16))
            store(group, ctx_index, (block_out * own).astype(jnp.bfloat16))

        copy = pltpu.make_async_copy(out_ref.at[group], out_hbm.at[:, :, group], out_sem.at[group])
        copy.start()
        out_copies.append(copy)
    copy = pltpu.make_async_copy(lse_ref, lse_hbm.at[:, pl.ds(0, lse_ref.shape[1])], lse_sem)
    copy.start()
    out_copies.append(copy)
    for copy in out_copies:
        copy.wait()


def page_attention(table, lengths, parents, query, keys, values, new_keys, new_values):
    table_len, traj = table.shape
    new = parents.shape[0]
    head_size = new_keys.shape[-1]
    rows = SHARE * new
    groups = traj // SHARE
    pages, page_len, width = keys.shape
    kv_count = width // head_size
    heads = query.shape[2] // width
    lanes = rows * heads
    slots = 4
    units = traj * table_len
    smem = pl.BlockSpec(memory_space=pltpu.SMEM)
    vmem = pl.BlockSpec(memory_space=pltpu.VMEM)
    anywhere = pl.BlockSpec(memory_space=pl.ANY)
    bf16, f32, dma = jnp.bfloat16, jnp.float32, pltpu.SemaphoreType.DMA
    return pl.pallas_call(
        functools.partial(attention_kernel, table_len // 2),
        out_shape=(
            jax.ShapeDtypeStruct((kv_count, 2, groups, head_size, lanes // 2), bf16),
            jax.ShapeDtypeStruct((kv_count, LSE_ROOM, lanes // 2), f32),
        ),
        in_specs=[smem, smem, smem] + [anywhere] * 5,
        out_specs=(anywhere, anywhere),
        scratch_shapes=[
            pltpu.VMEM(query.shape, bf16),
            pltpu.VMEM((kv_count, lanes, head_size), bf16),
            pltpu.VMEM(new_keys.shape, bf16),
            pltpu.VMEM(new_values.shape, bf16),
            pltpu.VMEM((kv_count, head_size, lanes), f32),
            pltpu.VMEM((kv_count, lanes), f32),
            pltpu.VMEM((kv_count, lanes), f32),
            pltpu.VMEM((groups, kv_count, 2, head_size, lanes // 2), bf16),
            pltpu.VMEM((kv_count, LSE_ROWS, lanes // 2), f32),
            pltpu.VMEM((slots, page_len, width), bf16),
            pltpu.VMEM((slots, page_len, width), bf16),
            pltpu.SMEM((3, units), jnp.int32),
            dma((groups,)),
            dma((2,)),
            dma((groups,)),
            dma,
            dma((slots,)),
            dma((slots,)),
        ],
        cost_estimate=pl.CostEstimate(
            flops=10**10, bytes_accessed=10**7, transcendentals=10**7
        ),
        compiler_params=pltpu.CompilerParams(vmem_limit_bytes=56 * 1024 * 1024),
    )(table, lengths, parents, query, keys, values, new_keys, new_values)


def attend(queries, keys, values, new_keys, new_values, table, lengths, parents):
    traj, new, _, head_size = new_keys.shape
    return page_attention(
        table.T,
        lengths,
        parents.T,
        queries,
        keys,
        values,
        new_keys.reshape(traj, new, head_size),
        new_values.reshape(traj, new, head_size),
    )


CTX_STEPS = ((2, 1), (2, 0), (1, 1), (3, 1), (0, 1), (1, 0), (3, 0))
MESH = pl.DeviceIdType.MESH


def project_kernel(
    near,
    part_hbm,
    lse_hbm,
    weight_hbm,
    weight_below,
    weight_above,
    out_ref,
    weights,
    part_own,
    part_in,
    lse_own,
    lse_in,
    total,
    gathered,
    product,
    shard_in,
    sums,
    summed,
    final,
    own_sems,
    part_sems,
    lse_sems,
    ring_sems,
    gather_sems,
    shard_send,
    shard_recv,
    final_sems,
):
    count = lax.axis_size("ctx")
    c = lax.axis_index("ctx")
    f = lax.axis_index("fsdp")
    z, r = f // near, f % near
    halves, groups, head_size, lanes = part_own.shape
    rows = gathered.shape[2]
    token_rows = rows // groups
    heads = lanes // token_rows
    shard = product.shape[2]
    piece_rows = weights.shape[1] // 2
    steps = len(CTX_STEPS)

    def ctx_step(dx, dy):
        return ((c // 2 + dx) % (count // 2)) * 2 + (c % 2 + dy) % 2

    others = [ctx_step(*step) for step in CTX_STEPS]
    locals_ = [
        (r // 2 + dy) % 2 * 2 + (r % 2 + dcore) % 2 for dy, dcore in ((0, 1), (1, 0), (1, 1))
    ]

    def at_ctx(other):
        return (other, f)

    def at_local(other):
        return (c, z * near + other)

    def at_z(step):
        return (c, ((z + count + step) % count) * near + r)

    barrier = pltpu.get_barrier_semaphore()
    peers = [at_ctx(other) for other in others]
    peers += [at_z(1), at_z(-1)] + [at_local(other) for other in locals_]
    for peer in peers:
        pl.semaphore_signal(barrier, inc=1, device_id=peer, device_id_type=MESH)
    below, above = (z + count - 1) % count, (z + 1) % count
    own_copies = [
        pltpu.make_async_copy(source, target, own_sems.at[index])
        for index, (source, target) in enumerate(
            (
                (lse_hbm.at[c, pl.ds(0, LSE_ROWS)], lse_own),
                (part_hbm.at[c], part_own),
                (weight_hbm, weights.at[z]),
                (weight_below, weights.at[below]),
                (weight_above, weights.at[above]),
            )
        )
    ]
    for copy in own_copies:
        copy.start()
    pl.semaphore_wait(barrier, len(peers))

    def send(source, target, sems, index, device):
        copy = pltpu.make_async_remote_copy(
            src_ref=source,
            dst_ref=target,
            send_sem=sems.at[(0,) + index],
            recv_sem=sems.at[(1,) + index],
            device_id=device,
            device_id_type=MESH,
        )
        copy.start()
        return copy

    lse_copies = [
        send(
            lse_hbm.at[other, pl.ds(0, LSE_ROWS)],
            lse_in.at[index],
            lse_sems,
            (index,),
            at_ctx(other),
        )
        for index, other in enumerate(others)
    ]

    def send_part(half, index):
        return send(
            part_hbm.at[others[index], half],
            part_in.at[index, half],
            part_sems,
            (index, half),
            at_ctx(others[index]),
        )

    ring = {}

    def forward(distance, part):
        for way in range(2):
            if distance == 4 and way != part:
                continue
            origin = (z + count + (1 - distance if way == 0 else distance - 1)) % count
            span = pl.ds(part * piece_rows, piece_rows)
            target = weights.at[origin, span]
            if distance == 2:
                source = (weight_below, weight_above)[way].at[span]
            else:
                source = target
            ring[distance, part, way] = send(
                source, target, ring_sems, (distance - 2, part, way), at_z(1 if way == 0 else -1)
            )

    def receive(distance, part):
        for way in range(2):
            if distance == 4 and way != part:
                continue
            ring[distance, part, way].wait_recv()
        if distance < 4:
            forward(distance + 1, part)

    part_copies = [[send_part(0, index) for index in range(steps)], []]
    forward(2, 0)
    forward(2, 1)
    for index in range(steps):
        part_copies[0][index].wait_send()
        part_copies[1].append(send_part(1, index))

    own_copies[0].wait()
    for copy in lse_copies:
        copy.wait_recv()
    each_lse = [lse_own[...]] + [lse_in[index] for index in range(steps)]
    top = functools.reduce(jnp.maximum, each_lse)
    weighing = [jnp.exp2(lse - top) for lse in each_lse]
    inverse = 1.0 / functools.reduce(jnp.add, weighing)
    weighing = [weight * inverse for weight in weighing]
    own_copies[1].wait()
    gathers = {}

    def combine(half):
        for group in range(groups):
            row = half * groups + group
            total[group] = part_own[half, group].astype(jnp.float32) * weighing[0][row : row + 1]
        for index in range(steps):
            part_copies[half][index].wait_recv()
            for group in range(groups):
                row = half * groups + group
                total[group] += (
                    part_in[index, half, group].astype(jnp.float32)
                    * weighing[index + 1][row : row + 1]
                )
        for group in range(groups):
            turned = total[group].T.astype(jnp.bfloat16)
            for head in range(heads):
                gathered[
                    half,
                    r,
                    group * token_rows : (group + 1) * token_rows,
                    head * head_size : (head + 1) * head_size,
                ] = turned[head * token_rows : (head + 1) * token_rows]
        for index in range(2):
            block = gathered.at[half, r]
            gathers[half, index] = send(
                block, block, gather_sems, (half, index), at_local(locals_[index])
            )

    def relay(half):
        gathers[half, 1].wait_recv()
        block = gathered.at[half, locals_[1]]
        gathers[half, 2] = send(block, block, gather_sems, (half, 2), at_local(locals_[0]))

    receive(2, 0)
    receive(2, 1)
    combine(0)
    receive(3, 0)
    relay(0)
    combine(1)
    relay(1)
    receive(3, 1)
    for half in range(halves):
        for index in (0, 2):
            gathers[half, index].wait_recv()
    for copy in own_copies[2:]:
        copy.wait()

    order = [dx * 2 + dy for dx, dy in (*CTX_STEPS, (0, 0))]
    far = (z + count // 2) % count
    far_step = (far // 2 - c // 2 + count // 2) % (count // 2) * 2 + (far % 2 + c % 2) % 2
    shard_copies = []

    def project(turn):
        step = order[turn]
        for early, late in ((0, 4), (1, 5), (2, 6), (3, 5)):
            if turn == early:
                step = jnp.where(far_step == order[early], order[late], step)
            if turn == late:
                step = jnp.where(far_step == order[early], order[early], step)
        column = ctx_step(step // 2, step % 2)
        for half in range(halves):
            value = gathered[half].reshape(near * rows, weights.shape[1])
            result = jnp.dot(value, weights[column], preferred_element_type=jnp.float32)
            product[column, half * near * rows : (half + 1) * near * rows] = result.astype(
                jnp.bfloat16
            )
        copy = pltpu.make_async_remote_copy(
            src_ref=product.at[column],
            dst_ref=shard_in.at[c],
            send_sem=shard_send.at[turn],
            recv_sem=shard_recv.at[c],
            device_id=at_ctx(column),
            device_id_type=MESH,
        )
        shard_copies.append((copy, column))

        @pl.when(column != c)
        def _():
            copy.start()

    for turn in range(count):
        if turn == 4:
            receive(4, 0)
            receive(4, 1)
        project(turn)
    sums[...] = product[c].astype(jnp.float32)
    for dx, dy in CTX_STEPS:
        other = ctx_step(count // 2 - dx, dy)
        pltpu.make_async_remote_copy(
            src_ref=shard_in.at[other],
            dst_ref=shard_in.at[other],
            send_sem=shard_send.at[0],
            recv_sem=shard_recv.at[other],
            device_id=at_z(1),
            device_id_type=MESH,
        ).wait_recv()
        sums[...] += shard_in[other].astype(jnp.float32)
    final_copies = []
    for index, owner in enumerate([*locals_[::-1], r]):
        for half in range(halves):
            span = pl.ds(pl.multiple_of((half * near + owner) * rows, rows), rows)
            summed[owner, half] = sums[span].astype(jnp.bfloat16)
        if index < near - 1:
            final_copies.append(
                send(summed.at[owner], final.at[r], final_sems, (index,), at_local(owner))
            )
    final[r] = summed[r]
    for copy in final_copies:
        copy.wait_recv()
    for source in range(near):
        for half in range(halves):
            for group in range(groups):
                new = out_ref.shape[1]
                size = token_rows // new
                start = (group * halves + half) * size
                value = final[source, half, group * token_rows : (group + 1) * token_rows]
                out_ref[start : start + size, :, source * shard : (source + 1) * shard] = (
                    value.reshape(size, new, shard)
                )
    for copy, column in shard_copies:

        @pl.when(column != c)
        def _():
            copy.wait_send()

    started = lse_copies + part_copies[1] + final_copies
    for copies in (ring, gathers):
        started += copies.values()
    for copy in started:
        copy.wait_send()


def project(part, lse, weight, weight_below, weight_above, near, new):
    count, halves, groups, head_size, lanes = part.shape
    width, shard = weight.shape
    rows = groups * lanes * head_size // width
    steps = len(CTX_STEPS)
    vmem = pl.BlockSpec(memory_space=pltpu.VMEM)
    anywhere = pl.BlockSpec(memory_space=pl.ANY)
    bf16, f32, dma = jnp.bfloat16, jnp.float32, pltpu.SemaphoreType.DMA
    return pl.pallas_call(
        functools.partial(project_kernel, near),
        out_shape=jax.ShapeDtypeStruct((halves * rows // new, new, near * shard), bf16),
        in_specs=[anywhere, anywhere, anywhere, vmem, vmem],
        out_specs=vmem,
        scratch_shapes=[
            pltpu.VMEM((count,) + weight.shape, bf16),
            pltpu.VMEM((halves, groups, head_size, lanes), bf16),
            pltpu.VMEM((steps, halves, groups, head_size, lanes), bf16),
            pltpu.VMEM((LSE_ROWS, lanes), f32),
            pltpu.VMEM((steps, LSE_ROWS, lanes), f32),
            pltpu.VMEM((groups, head_size, lanes), f32),
            pltpu.VMEM((halves, near, rows, width), bf16),
            pltpu.VMEM((count, near * halves * rows, shard), bf16),
            pltpu.VMEM((count, near * halves * rows, shard), bf16),
            pltpu.VMEM((near * halves * rows, shard), f32),
            pltpu.VMEM((near, halves, rows, shard), bf16),
            pltpu.VMEM((near, halves, rows, shard), bf16),
            dma((5,)),
            dma((2, steps, halves)),
            dma((2, steps)),
            dma((2, 3, 2, 2)),
            dma((2, halves, 3)),
            dma((count,)),
            dma((count,)),
            dma((2, 3)),
        ],
        compiler_params=pltpu.CompilerParams(
            collective_id=0, has_side_effects=True, vmem_limit_bytes=51 * 1024 * 1024
        ),
    )(part, lse, weight, weight_below, weight_above)


def shards(
    queries, key_pages, value_pages, new_keys, new_values, page_table, lengths, parents, o_weight
):
    ctx_count = lax.axis_size("ctx")
    fsdp_count = lax.axis_size("fsdp")
    new = queries.shape[1]
    near = fsdp_count // ctx_count

    def moved(step):
        pairs = [(at, (at + step * near) % fsdp_count) for at in range(fsdp_count)]
        return lax.ppermute(o_weight, "fsdp", pairs)

    weight_below, weight_above = moved(1), moved(-1)
    part, lse = attend(
        queries, key_pages, value_pages, new_keys, new_values, page_table, lengths, parents
    )
    return project(part, lse, o_weight, weight_below, weight_above, near, new)


def solution(mesh):
    placed = (
        P("fsdp", None, None),
        P("ctx", None, None),
        P("ctx", None, None),
        P("fsdp", None, "ctx", None),
        P("fsdp", None, "ctx", None),
        P("fsdp", None),
        P("fsdp"),
        P("fsdp", None),
        P("ctx", "fsdp"),
    )
    return jax.shard_map(
        shards, mesh=mesh, in_specs=placed, out_specs=P("fsdp", None, "ctx"), check_vma=False
    )
```
